256 devices in a mesh: dp: 64 (over z, y, core), seq: 4 (over x).
Axes of the slice: x: 4, y: 4, z: 8, core: 2. Of those that a mesh axis runs over, the one named last changes fastest.
Arguments:
- queries: bfloat16 [64, 512, 1024], P('dp', 'seq'), may hold values from -6 to 6
- key_rows: bfloat16 [64, 512, 1024], P('dp', 'seq'), may hold values from -6 to 6
- value_rows: bfloat16 [64, 512, 1024], P('dp', 'seq'), may hold values from -6 to 6
- inputs: bfloat16 [64, 512, 1024], P('dp', 'seq'), may hold values from -6 to 6
- w_gate: float32 [1024, 32], replicated, may hold values from -0.1875 to 0.1875
- poly_coef: float32 [1024], replicated, may hold values from -0.6 to 0.6
- decay_rate: float32 [16], replicated, may hold values from 0.0003 to 0.05
- cotangent: bfloat16 [64, 512, 1024], P('dp', 'seq'), may hold values from -6 to 6
Outputs:
- grad_queries: bfloat16 [64, 512, 1024], P('dp', 'seq')
- grad_keys: bfloat16 [64, 512, 1024], P('dp', 'seq')
- grad_values: bfloat16 [64, 512, 1024], P('dp', 'seq')
- grad_inputs: bfloat16 [64, 512, 1024], P('dp', 'seq')
- grad_gate: float32 [1024, 32], replicated
- grad_coef: float32 [1024], replicated
- grad_rate: float32 [16], replicated
The draws below stay inside these ranges and needn't reach their ends.
All inputs are finite; a program needn't handle non-finite values.
Results may differ from the reference program's by a relative error of at most 0.02.
Values may be sent and summed in bfloat16 or wider, within the bound.
A program may use at most 64 MiB of HBM per device.

```python
import math
import jax
import jax.numpy as jnp
from jax import lax

D = 1024
H = 16
DH = 64
WINDOW = 64
WIDTH = 1024
SEQS = 64
LENGTH = 512


def block_levels(key, shape, pieces, smallest, high):
    loudness = 1.0
    for position, shards_of in pieces:
        steps = jax.random.uniform(jax.random.fold_in(jax.random.fold_in(key, 6), position), (shards_of,), jnp.float32, smallest / len(pieces), high / len(pieces))
        loudness = loudness * jnp.repeat(jnp.exp(steps), shape[position] // shards_of).reshape((-1,) + (1,) * (len(shape) - 1 - position))
    return loudness


def centred(key, extent, deviation, most, pieces=(), dtype=jnp.bfloat16):
    entries = deviation * jax.random.normal(key, extent, jnp.float32)
    if pieces:
        entries = entries * block_levels(key, extent, pieces, -0.22, 0.18)
    return jnp.clip(entries, -most, most).astype(dtype)


def setup_inputs(seed: int = 0) -> dict:
    key_list = jax.random.split(jax.random.key(seed), 9)
    return {
        "queries": centred(key_list[0], (SEQS, LENGTH, WIDTH), 1.0, 6.0, ((0, 64), (1, 4))),
        "key_rows": centred(key_list[1], (SEQS, LENGTH, WIDTH), 1.0, 6.0, ((0, 64), (1, 4))),
        "value_rows": centred(key_list[2], (SEQS, LENGTH, WIDTH), 1.0, 6.0, ((0, 64), (1, 4))),
        "inputs": centred(key_list[3], (SEQS, LENGTH, D), 1.0, 6.0, ((0, 64), (1, 4))),
        "w_gate": centred(key_list[4], (D, 2 * H), D ** -0.5, 0.1875, (), jnp.float32),
        "poly_coef": jnp.clip(jax.random.uniform(key_list[5], (WIDTH,), jnp.float32, -0.6, 0.6), -0.6, 0.6),
        "decay_rate": jnp.clip(jnp.exp(jax.random.uniform(key_list[6], (H,), jnp.float32, math.log(0.0003), math.log(0.05))), 0.0003, 0.05),
        "cotangent": centred(key_list[7], (SEQS, LENGTH, WIDTH), 1.0, 6.0, ((0, 64), (1, 4))),
    }


highest = lax.Precision.HIGHEST

def features(raw, poly_coef):
    as_float = raw.astype(jnp.float32)
    return 0.125 * (as_float + poly_coef * as_float * as_float)

def block_step(memory, block_in):
    q_block, key_pairs, value_pairs, decay_log = block_in
    window = q_block.shape[0]
    head_count = decay_log.shape[1]
    head_dim = q_block.shape[1] // head_count
    log_decay = jnp.cumsum(decay_log, axis=0)
    row_ids = lax.broadcasted_iota(jnp.int32, (window, window), 0)
    col_ids = lax.broadcasted_iota(jnp.int32, (window, window), 1)
    causal = col_ids <= row_ids
    gap_log = jnp.where(causal[:, :, None], log_decay[:, None, :] - log_decay[None, :, :], 0.0)
    decay_mat = jnp.where(causal[:, :, None], jnp.exp(gap_log), 0.0)
    step_ids = lax.broadcasted_iota(jnp.int32, (window, 2 * window), 0)
    slot_ids = lax.broadcasted_iota(jnp.int32, (window, 2 * window), 1)
    offset = step_ids - slot_ids + window
    window_mask = ((offset >= 0) & (offset < window)).astype(jnp.float32)
    kernel = jnp.einsum('tsh,si->hti', decay_mat, window_mask, precision=highest)
    q_heads = q_block.reshape(window, head_count, head_dim).astype(jnp.float32)
    key_heads = key_pairs.reshape(2 * window, head_count, head_dim)
    value_heads = value_pairs.reshape(2 * window, head_count, head_dim).astype(jnp.float32)
    scores = jnp.einsum('thd,ihd->hti', q_heads, key_heads.astype(jnp.float32), precision=highest)
    weights = (scores * kernel).astype(jnp.bfloat16)
    inside = jnp.einsum('hti,ihd->thd', weights.astype(jnp.float32), value_heads, precision=highest)
    carried_out = jnp.einsum('thd,hde->the', q_heads, memory, precision=highest) * jnp.exp(log_decay)[:, :, None]
    last_row = kernel[:, window - 1, :]
    carried = (key_heads.astype(jnp.float32) * jnp.transpose(last_row)[:, :, None]).astype(jnp.bfloat16)
    update = jnp.einsum('ihd,ihe->hde', carried.astype(jnp.float32), value_heads, precision=highest)
    memory_next = jnp.exp(log_decay[window - 1])[:, None, None] * memory + update
    return (memory_next, (inside + carried_out).reshape(window, head_count * head_dim))

def local_forward(queries, key_rows, value_rows, inputs, w_gate, poly_coef, decay_rate, key_rim, value_rim, input_rim, memory):
    length = queries.shape[0]
    window = key_rim.shape[0]
    head_count = decay_rate.shape[0]
    width_all = queries.shape[1]
    head_dim = width_all // head_count
    blocks = length // window
    all_inputs = jnp.concatenate([input_rim, inputs], axis=0)
    logits = jnp.dot(all_inputs.astype(jnp.float32), w_gate, precision=highest)
    decay_log = -decay_rate * jax.nn.softplus(logits[window:, :head_count])
    gamma = jax.nn.sigmoid(logits[:, head_count:]) / window
    all_keys = jnp.concatenate([key_rim, key_rows], axis=0)
    all_values = jnp.concatenate([value_rim, value_rows], axis=0)
    weighted = (features(all_keys, poly_coef).reshape(-1, head_count, head_dim) * gamma[:, :, None]).astype(jnp.bfloat16).reshape(-1, width_all)
    query_feat = features(queries, poly_coef).astype(jnp.bfloat16)
    key_pairs = jnp.concatenate([weighted[:length].reshape(blocks, window, width_all), weighted[window:].reshape(blocks, window, width_all)], axis=1)
    value_pairs = jnp.concatenate([all_values[:length].reshape(blocks, window, width_all), all_values[window:].reshape(blocks, window, width_all)], axis=1)
    memory_end, outputs = lax.scan(block_step, memory, (query_feat.reshape(blocks, window, width_all), key_pairs, value_pairs, decay_log.reshape(blocks, window, head_count)))
    return (outputs.reshape(length, width_all), memory_end, lax.optimization_barrier(jnp.sum(decay_log, axis=0)))

def reference(queries, key_rows, value_rows, inputs, w_gate, poly_coef, decay_rate, cotangent):

    def one_sequence(items):
        q_seq, k_seq, v_seq, x_seq, g_seq = items
        width_all = q_seq.shape[1]
        key_rim = jnp.zeros((WINDOW, width_all), jnp.bfloat16)
        value_rim = jnp.zeros((WINDOW, width_all), jnp.bfloat16)
        input_rim = jnp.zeros((WINDOW, D), jnp.bfloat16)
        memory = jnp.zeros((H, DH, DH), jnp.float32)
        primal, pullback = jax.vjp(local_forward, q_seq, k_seq, v_seq, x_seq, w_gate, poly_coef, decay_rate, key_rim, value_rim, input_rim, memory)
        grads = pullback((g_seq.astype(jnp.float32), jnp.zeros_like(primal[1]), jnp.zeros_like(primal[2])))
        return (grads[0], grads[1], grads[2], grads[3], grads[4], grads[5], grads[6])
    results = lax.map(one_sequence, (queries, key_rows, value_rows, inputs, cotangent))
    return (results[0], results[1], results[2], results[3], lax.optimization_barrier(jnp.sum(results[4], axis=0)), lax.optimization_barrier(jnp.sum(results[5], axis=0)), lax.optimization_barrier(jnp.sum(results[6], axis=0)))
```

```python
import functools

import jax
import jax.numpy as jnp
from jax import lax
from jax.experimental import pallas as pl
from jax.experimental.pallas import tpu as pltpu
from jax.sharding import PartitionSpec as P

BLOCK = 64
LANES = 128
WIDTH = 1024
PAIRS = WIDTH // LANES
HEADS = 16
F32 = jnp.float32
BF16 = jnp.bfloat16
MESH = pl.DeviceIdType.MESH


def nn(a, b):
    return lax.dot_general(a, b, (((1,), (0,)), ((), ())), preferred_element_type=F32)


def nt(a, b):
    return lax.dot_general(a, b, (((1,), (1,)), ((), ())), preferred_element_type=F32)


def tn(a, b):
    return lax.dot_general(a, b, (((0,), (0,)), ((), ())), preferred_element_type=F32)


def pieces(a, count):
    parts = []
    for _ in range(count):
        part = a.astype(BF16)
        parts.append(part)
        a = a - part.astype(F32)
    return parts


def flag(condition):
    return jnp.where(condition, 1.0, 0.0).astype(BF16)


def iota(shape, dimension):
    return lax.broadcasted_iota(jnp.int32, shape, dimension)


Q_UP, G_UP, L_UP, S_UP, SS2_UP, SS3_UP, TOT1, TOT2, TOT3 = range(9)
P_DN, R_DN, T2_DN, T3_DN, DQ_DN, DA_DN = range(9, 15)
MESSAGES = 15


def main_kernel(
    q_ref, k_ref, v_ref, x_ref, w_ref, coef_ref, rate_ref, g_ref,
    dq_ref, dk_ref, dv_ref, dx_ref, part_ref,
    qn, gn, lbuf, tot, tot_in, s1_out, ss_out, s1_in, ss_in, p_out, r_out, t_out, p_in, r_in, t_in,
    dqn_out, dqn_in, dan_out, dan_in,
    lrow, lx, gamma_x, blast_x, qf, wk, gq, s0c, u0c, c1c, m_in, m_mid, n_mid, n_end, z_end,
    dqf, dwk, dvf, gmat, xmat,
    send_sem, recv_sem,
):
    place = lax.axis_index("seq")
    last = 3

    def copy(source, target, message, to):
        return pltpu.make_async_remote_copy(
            src_ref=source,
            dst_ref=target,
            send_sem=send_sem.at[message],
            recv_sem=recv_sem.at[message],
            device_id={"seq": to},
            device_id_type=MESH,
        )

    up1, up2, up3 = place - 1, place - 2, place - 3
    dn1, dn2, dn3 = place + 1, place + 2, place + 3
    around = [lax.rem(place + 4 - hop, 4) for hop in (1, 2, 3)]
    copies = {
        Q_UP: (copy(q_ref.at[pl.ds(0, BLOCK)], qn, Q_UP, up1), 1),
        G_UP: (copy(g_ref.at[pl.ds(0, BLOCK)], gn, G_UP, up1), 1),
        L_UP: (copy(lbuf.at[pl.ds(0, BLOCK)], lbuf.at[pl.ds(2 * BLOCK, BLOCK)], L_UP, up1), 1),
        S_UP: (copy(s1_out, s1_in, S_UP, up1), 1),
        SS2_UP: (copy(ss_out, ss_in.at[0], SS2_UP, up2), 2),
        SS3_UP: (copy(ss_out, ss_in.at[1], SS3_UP, up3), 3),
        TOT1: (copy(tot, tot_in.at[0], TOT1, around[0]), 0),
        TOT2: (copy(tot, tot_in.at[1], TOT2, around[1]), 0),
        TOT3: (copy(tot, tot_in.at[2], TOT3, around[2]), 0),
        P_DN: (copy(p_out, p_in, P_DN, dn1), -1),
        R_DN: (copy(r_out, r_in, R_DN, dn1), -1),
        T2_DN: (copy(t_out, t_in.at[0], T2_DN, dn2), -2),
        T3_DN: (copy(t_out, t_in.at[1], T3_DN, dn3), -3),
        DQ_DN: (copy(dqn_out, dqn_in, DQ_DN, dn1), -1),
        DA_DN: (copy(dan_out, dan_in, DA_DN, dn1), -1),
    }

    def guarded(steps, action):
        if steps == 0:
            action()
        elif steps > 0:
            pl.when(place >= steps)(action)
        else:
            pl.when(place <= last + steps)(action)

    def send(message):
        description, steps = copies[message]
        guarded(steps, description.start)

    def sent(message):
        description, steps = copies[message]
        guarded(steps, description.wait_send)

    def received(message):
        description, steps = copies[message]
        guarded(-steps, description.wait_recv)

    barrier = pltpu.get_barrier_semaphore()
    for hop in (1, 2, 3):
        pl.semaphore_signal(
            barrier, inc=1, device_id={"seq": lax.rem(place + hop, 4)}, device_id_type=MESH
        )

    @pl.when(place == last)
    def _():
        qn[...] = jnp.zeros_like(qn)
        gn[...] = jnp.zeros_like(gn)
        lbuf[pl.ds(2 * BLOCK, BLOCK), :] = jnp.zeros((BLOCK, LANES), F32)
        s1_in[...] = jnp.zeros_like(s1_in)

    for hop in (2, 3):
        @pl.when(place > last - hop)
        def _():
            ss_in[hop - 2] = jnp.zeros(ss_in.shape[1:], BF16)

        @pl.when(place < hop)
        def _():
            t_in[hop - 2] = jnp.zeros(t_in.shape[1:], BF16)

    @pl.when(place == 0)
    def _():
        p_in[...] = jnp.zeros_like(p_in)
        r_in[...] = jnp.zeros_like(r_in)
        dqn_in[...] = jnp.zeros_like(dqn_in)
        dan_in[...] = jnp.zeros_like(dan_in)

    w_hi, w_lo = pieces(
        jnp.concatenate([w_ref[...], jnp.zeros((LANES - 2 * HEADS, WIDTH), F32)], axis=0), 2
    )
    pl.semaphore_wait(barrier, 3)
    send(Q_UP)
    send(G_UP)
    x = x_ref[...]
    logits = nt(x, w_hi) + nt(x, w_lo)
    small = jnp.exp(-jnp.abs(logits))
    soft = jnp.maximum(logits, 0.0) + jnp.log1p(small)
    sig = jnp.where(logits >= 0.0, 1.0, small) / (1.0 + small)
    rate = jnp.concatenate([rate_ref[...], jnp.zeros((1, LANES - HEADS), F32)], axis=1)
    decay = -rate * soft
    gamma = sig * (1.0 / BLOCK)
    row, col = iota((LANES, LANES), 0), iota((LANES, LANES), 1)
    same = (row // BLOCK) == (col // BLOCK)
    tri = flag(same & (col <= row))
    log_own = sum(nn(tri, part) for part in pieces(decay, 3))
    lbuf[pl.ds(0, LANES), :] = log_own
    tot[...] = jnp.zeros_like(tot)
    tot[0:1, :] = log_own[BLOCK - 1 : BLOCK]
    tot[1:2, :] = log_own[LANES - 1 :]
    send(L_UP)
    for message in (TOT1, TOT2, TOT3):
        send(message)

    head_row = iota((LANES, WIDTH), 0)
    head_lane = iota((LANES, WIDTH), 1) // BLOCK
    spread = flag(head_row == head_lane)
    spread_gate = flag(head_row == head_lane + HEADS)
    left = iota((BLOCK, LANES), 1) < BLOCK
    left1 = iota((1, LANES), 1) < BLOCK

    def expand(a, count):
        return sum(nn(part, spread) for part in pieces(a, count))

    def block_rows(logs, block, offset):
        pick = flag(row == (col % BLOCK) + offset)
        turned = sum(tn(part, pick) for part in pieces(logs, 3))
        for pair in range(PAIRS):
            lrow[block : block + 1, pl.ds(pair * LANES, LANES)] = jnp.where(
                left1, turned[2 * pair : 2 * pair + 1], turned[2 * pair + 1 : 2 * pair + 2]
            )

    block_rows(log_own, 0, 0)
    block_rows(log_own, 1, BLOCK)
    lx[pl.ds(0, LANES), :] = expand(log_own, 3)
    gamma_x[...] = sum(nn(part, spread_gate) for part in pieces(gamma, 2))

    srow, scol = iota((BLOCK, BLOCK), 0), iota((BLOCK, BLOCK), 1)
    cur_t = flag(scol >= srow)
    prev_t = flag(scol < srow)
    tail0 = jnp.exp(log_own[BLOCK - 1 : BLOCK] - log_own[:BLOCK])
    tail1 = jnp.exp(log_own[LANES - 1 :] - log_own[BLOCK:])

    def ending(mask, tail):
        return expand(sum(nn(mask, part) for part in pieces(tail, 2)), 2)

    blast_x[pl.ds(0, BLOCK), :] = ending(cur_t, tail0)
    blast_x[pl.ds(BLOCK, BLOCK), :] = ending(prev_t, tail1)
    blast_x[pl.ds(2 * BLOCK, BLOCK), :] = ending(cur_t, tail1)

    def lanes_of(pair):
        return pl.ds(pl.multiple_of(pair * LANES, LANES), LANES)

    def phi(raw, coef):
        value = raw.astype(F32)
        return 0.125 * (value + coef * value * value)

    def compact(full):
        return jnp.where(left, full[:BLOCK], full[BLOCK:])

    def diagonal(value):
        none = jnp.zeros_like(value)
        return jnp.concatenate([jnp.where(left, value, none), jnp.where(left, none, value)], axis=0)

    def weighted(a, weights):
        return (a.astype(F32) * weights).astype(BF16)

    def own_step(pair, carry):
        at = lanes_of(pair)
        coef = coef_ref[:, at]
        q_feat = phi(q_ref[:, at], coef).astype(BF16)
        qf[pl.ds(0, LANES), at] = q_feat
        keys = (phi(k_ref[:, at], coef) * gamma_x[:, at]).astype(BF16)
        wk[:, at] = keys
        logs = lx[pl.ds(0, LANES), at]
        scaled = weighted(g_ref[:, at], jnp.exp(logs))
        gq[:, at] = scaled
        s0 = compact(tn(q_feat[:BLOCK], scaled[:BLOCK]))
        s1 = compact(tn(q_feat[BLOCK:], scaled[BLOCK:]))
        fall0 = jnp.exp(logs[BLOCK - 1 : BLOCK])
        fall1 = jnp.exp(logs[LANES - 1 :])
        s1_out[:, at] = s1.astype(BF16)
        ss_out[:, at] = (s0 + fall0 * s1).astype(BF16)
        values = v_ref[:, at]
        weights = blast_x[pl.ds(0, 3 * BLOCK), at]
        carried0 = weighted(keys[:BLOCK], weights[:BLOCK])
        carried1 = weighted(keys, weights[BLOCK:])
        u0 = compact(tn(carried0, values[:BLOCK]))
        c1 = compact(tn(carried1, values))
        u0c[:, at] = u0
        c1c[:, at] = fall1 * u0 + c1
        s0c[:, at] = s1
        p_out[:, at] = (fall1 * u0 + c1).astype(BF16)
        return carry

    lax.fori_loop(0, PAIRS, own_step, 0)
    send(S_UP)
    send(SS2_UP)
    send(SS3_UP)
    send(P_DN)

    received(L_UP)
    received(Q_UP)
    received(G_UP)
    log_next = lbuf[pl.ds(2 * BLOCK, BLOCK), :]
    log_pair = lbuf[pl.ds(BLOCK, LANES), :]
    block_rows(log_pair, 2, BLOCK)
    lx[pl.ds(LANES, BLOCK), :] = expand(log_next, 3)
    tail2 = jnp.exp(log_next[BLOCK - 1 :] - log_next)
    blast_x[pl.ds(3 * BLOCK, BLOCK), :] = ending(prev_t, tail2)

    def next_step(pair, carry):
        at = lanes_of(pair)
        coef = coef_ref[:, at]
        qf[pl.ds(LANES, BLOCK), at] = phi(qn[:, at], coef).astype(BF16)
        fall2 = jnp.exp(lx[3 * BLOCK - 1 : 3 * BLOCK, at])
        carried = weighted(wk[pl.ds(BLOCK, BLOCK), at], blast_x[pl.ds(3 * BLOCK, BLOCK), at])
        r = compact(tn(carried, v_ref[pl.ds(BLOCK, BLOCK), at]))
        r_out[:, at] = r.astype(BF16)
        t_out[:, at] = (fall2 * c1c[:, at] + r).astype(BF16)
        return carry

    lax.fori_loop(0, PAIRS, next_step, 0)
    send(R_DN)
    send(T2_DN)
    send(T3_DN)

    step = col % BLOCK
    cur_mask = flag(same & (row % BLOCK >= step))
    prev_mask = flag(same & (row % BLOCK < step))
    both_mask = jnp.concatenate([cur_mask, prev_mask], axis=1)
    causal = (iota((3 * BLOCK, LANES), 1) % BLOCK) <= (iota((3 * BLOCK, LANES), 0) % BLOCK)

    def window_step(pair, carry):
        at = lanes_of(pair)
        keys, values = wk[:, at], v_ref[:, at]
        queries = qf[:, at]
        grads = jnp.concatenate([g_ref[:, at], gn[:, at]], axis=0)
        logs = lx[:, at]
        rows = jnp.concatenate(
            [jnp.broadcast_to(lrow[b : b + 1, at], (BLOCK, LANES)) for b in range(3)], axis=0
        )
        decays = jnp.where(causal, jnp.exp(jnp.where(causal, logs - rows, 0.0)), 0.0)
        decays_low = decays.astype(BF16)
        first = nn(decays_low[:BLOCK], cur_mask)
        middle = nn(decays_low[BLOCK:LANES], both_mask)
        final = nn(decays_low[LANES:], prev_mask)
        kernels = (
            jnp.concatenate([first, middle[:, LANES:]], axis=0),
            jnp.concatenate([middle[:, :LANES], final], axis=0),
        )
        d_kernels = []
        d_queries = []
        for block in range(2):
            part = slice(block * BLOCK, (block + 1) * BLOCK)
            span = slice(block * BLOCK, block * BLOCK + LANES)
            keys_bd, values_bd = diagonal(keys[part]), diagonal(values[part])
            scores = nt(queries[span], keys_bd)
            d_weights = nt(grads[span], values_bd).astype(BF16).astype(F32)
            weights = (scores * kernels[block]).astype(BF16)
            d_scores = (d_weights * kernels[block]).astype(BF16)
            d_kernels.append((d_weights * scores).astype(BF16))
            d_queries.append(nn(d_scores, keys_bd))
            dvf[pl.ds(block * BLOCK, BLOCK), at] = compact(tn(weights, grads[span]))
            dwk[pl.ds(block * BLOCK, BLOCK), at] = compact(tn(d_scores, queries[span]))
        dqf[pl.ds(0, BLOCK), at] = d_queries[0][:BLOCK]
        dqf[pl.ds(BLOCK, BLOCK), at] = d_queries[0][BLOCK:] + d_queries[1][:BLOCK]
        dqn_out[:, at] = d_queries[1][BLOCK:].astype(BF16)
        d_decays = jnp.concatenate(
            [
                nt(d_kernels[0][:BLOCK], cur_mask),
                nt(jnp.concatenate([d_kernels[1][:BLOCK], d_kernels[0][BLOCK:]], axis=1), both_mask),
                nt(d_kernels[1][BLOCK:], prev_mask),
            ],
            axis=0,
        )
        gmat[:, at] = (d_decays * decays).astype(BF16)
        return carry

    lax.fori_loop(0, PAIRS, window_step, 0)
    send(DQ_DN)

    for message in (TOT1, TOT2, TOT3, S_UP, SS2_UP, SS3_UP, P_DN, R_DN, T2_DN, T3_DN):
        received(message)
    falls = [expand(tot_in[slot], 3) for slot in range(3)]
    back2 = expand(tot_in[1], 3)
    next1_fall1 = jnp.exp(falls[0][1:2])
    next2_all = jnp.exp(falls[1][0:1] + falls[1][1:2])
    prev1_fall1 = jnp.exp(falls[2][1:2])
    prev1_all = jnp.exp(falls[2][0:1] + falls[2][1:2])
    prev2_fall1 = jnp.exp(back2[1:2])
    own0 = jnp.exp(lx[BLOCK - 1 : BLOCK, :])
    own1 = jnp.exp(lx[LANES - 1 : LANES, :])
    next0 = jnp.exp(lx[3 * BLOCK - 1 :, :])

    memory = (
        p_in[...].astype(F32)
        + prev1_fall1 * t_in[0].astype(F32)
        + (prev2_fall1 * prev1_all) * t_in[1].astype(F32)
    )
    middle_memory = own0 * memory + r_in[...].astype(F32) + u0c[...]
    m_in[...] = memory.astype(BF16)
    m_mid[...] = middle_memory.astype(BF16)
    z = s1_in[...].astype(F32) + next1_fall1 * (
        ss_in[0].astype(F32) + next2_all * ss_in[1].astype(F32)
    )
    z_end[...] = z.astype(BF16)

    def next_adjoint(pair, carry):
        at = lanes_of(pair)
        scaled = weighted(gn[:, at], jnp.exp(lx[pl.ds(LANES, BLOCK), at]))
        c1c[:, at] = compact(tn(qf[pl.ds(LANES, BLOCK), at], scaled))
        return carry

    lax.fori_loop(0, PAIRS, next_adjoint, 0)
    end_grad = next0 * z + c1c[...]
    mid_grad = own1 * end_grad + s0c[...]
    n_end[...] = end_grad.astype(BF16)
    n_mid[...] = mid_grad.astype(BF16)
    fall_grad = jnp.concatenate(
        [
            own0 * jnp.sum(memory * mid_grad, axis=0, keepdims=True),
            own1 * jnp.sum(middle_memory * end_grad, axis=0, keepdims=True),
            jnp.zeros((6, WIDTH), F32),
        ],
        axis=0,
    )
    fall_grad = sum(nt(part, spread) for part in pieces(fall_grad, 2))

    def memory_step(pair, carry):
        at = lanes_of(pair)
        keys, values, scaled = wk[:, at], v_ref[:, at], gq[:, at]
        memory0, memory1 = diagonal(m_in[:, at]), diagonal(m_mid[:, at])
        dq_carried = jnp.concatenate(
            [nt(scaled[:BLOCK], memory0), nt(scaled[BLOCK:], memory1)], axis=0
        )
        dqf[:, at] = dqf[:, at] + dq_carried
        xmat[pl.ds(4 * BLOCK, LANES), at] = (
            dq_carried * qf[pl.ds(0, LANES), at].astype(F32)
        ).astype(BF16)
        grads = [diagonal(ref[:, at]) for ref in (n_mid, n_end, z_end)]
        for block in range(2):
            part = slice(block * BLOCK, (block + 1) * BLOCK)
            both = jnp.concatenate(grads[block : block + 2], axis=0)
            d_carried = nt(values[part], both).astype(BF16).astype(F32)
            own_keys = keys[part].astype(F32)
            d_keys = dwk[pl.ds(block * BLOCK, BLOCK), at]
            carried = []
            for role in range(2):
                index = 2 * block + role
                weights = blast_x[pl.ds(index * BLOCK, BLOCK), at]
                d_role = d_carried[:, role * LANES : (role + 1) * LANES]
                carried.append((own_keys * weights).astype(BF16))
                d_keys = d_keys + d_role * weights
                xmat[pl.ds(index * BLOCK, BLOCK), at] = (d_role * own_keys).astype(BF16)
            dwk[pl.ds(block * BLOCK, BLOCK), at] = d_keys
            dv_ref[pl.ds(block * BLOCK, BLOCK), at] = (
                dvf[pl.ds(block * BLOCK, BLOCK), at] + nn(jnp.concatenate(carried, axis=1), both)
            ).astype(BF16)
        coef = coef_ref[:, at]
        raw = k_ref[:, at].astype(F32)
        d_keys = dwk[:, at]
        d_feat = d_keys * gamma_x[:, at]
        square = 0.125 * raw * raw
        xmat[pl.ds(6 * BLOCK, LANES), at] = (d_keys * (0.125 * raw + coef * square)).astype(BF16)
        dk_ref[:, at] = (d_feat * (0.125 + (0.25 * coef) * raw)).astype(BF16)
        part_ref[32:33, at] = jnp.sum(d_feat * square, axis=0, keepdims=True)
        return carry

    lax.fori_loop(0, PAIRS, memory_step, 0)

    summed = nt(xmat[...], spread)
    lower = flag(scol < srow)
    upper_in = flag(scol >= srow)
    at_or_before = flag(scol <= srow)
    after = flag(scol > srow)

    def twice(mask, a):
        return sum(nn(mask, part) for part in pieces(a, 2))

    def decay_grad(block):
        later = nn(upper_in, gmat[pl.ds(block * BLOCK, BLOCK), :])
        lanes = iota((BLOCK, WIDTH), 1) % BLOCK
        kept = jnp.where(lanes < iota((BLOCK, WIDTH), 0), later, 0.0)
        return sum(nt(part, spread) for part in pieces(kept, 2))

    def tail_grad(block, tail):
        total = 0.0
        if block < 2:
            begin = 0 if block == 0 else 2 * BLOCK
            total = total + twice(at_or_before, summed[begin : begin + BLOCK])
        if block > 0:
            begin = BLOCK if block == 1 else 3 * BLOCK
            total = total + twice(after, summed[begin : begin + BLOCK])
        return twice(lower, total * tail)

    dan_out[...] = decay_grad(2) + tail_grad(2, tail2)
    send(DA_DN)
    d_decay = []
    for block, tail in ((0, tail0), (1, tail1)):
        carried = summed[4 * BLOCK + block * BLOCK : 5 * BLOCK + block * BLOCK]
        d_decay.append(
            decay_grad(block)
            + tail_grad(block, tail)
            + twice(upper_in, carried)
            + fall_grad[block : block + 1]
        )
    received(DA_DN)
    received(DQ_DN)
    d_decay[0] = d_decay[0] + dan_in[...]
    d_decay = jnp.concatenate(d_decay, axis=0)
    gate_row, gate_col = iota((LANES, LANES), 0), iota((LANES, LANES), 1)
    shift = flag(gate_col == gate_row + HEADS)
    d_gamma = sum(nn(part, shift) for part in pieces(summed[6 * BLOCK :], 2))
    is_decay = iota((LANES, LANES), 1) < HEADS
    d_logits = jnp.where(is_decay, -rate * sig * d_decay, d_gamma * gamma * (1.0 - sig))
    rates = jnp.sum(jnp.where(is_decay, -soft * d_decay, 0.0), axis=0, keepdims=True)
    d_hi, d_lo = pieces(d_logits, 2)
    dx_ref[...] = (nn(d_hi, w_hi) + (nn(d_hi, w_lo) + nn(d_lo, w_hi))).astype(BF16)
    gate = tn(d_hi, x) + tn(d_lo, x)
    part_ref[0:32, :] = gate[:32]
    part_ref[33:40, :] = jnp.zeros((7, WIDTH), F32)
    part_ref[33:34, 0:LANES] = rates

    def query_step(pair, carry):
        at = lanes_of(pair)
        coef = coef_ref[:, at]
        raw = q_ref[:, at].astype(F32)
        d_feat = dqf[:, at] + jnp.concatenate(
            [dqn_in[:, at].astype(F32), jnp.zeros((BLOCK, LANES), F32)], axis=0
        )
        dq_ref[:, at] = (d_feat * (0.125 + (0.25 * coef) * raw)).astype(BF16)
        part_ref[32:33, at] = part_ref[32:33, at] + jnp.sum(
            d_feat * (0.125 * raw * raw), axis=0, keepdims=True
        )
        return carry

    lax.fori_loop(0, PAIRS, query_step, 0)
    for message in range(MESSAGES):
        sent(message)


def main_call(queries, keys, values, inputs, gate, coef, rate, cotangent):
    rows = queries.shape[0]
    vmem = pl.BlockSpec(memory_space=pltpu.VMEM)
    block = (BLOCK, WIDTH)
    out = jax.ShapeDtypeStruct((rows, WIDTH), BF16)
    scratch = [
        (block, BF16), (block, BF16), ((3 * BLOCK, LANES), F32), ((8, LANES), F32), ((3, 8, LANES), F32),
        (block, BF16), (block, BF16), (block, BF16), ((2,) + block, BF16),
        (block, BF16), (block, BF16), (block, BF16), (block, BF16), (block, BF16), ((2,) + block, BF16),
        (block, BF16), (block, BF16), ((BLOCK, LANES), F32), ((BLOCK, LANES), F32),
        ((8, WIDTH), F32), ((3 * BLOCK, WIDTH), F32), ((LANES, WIDTH), F32), ((4 * BLOCK, WIDTH), F32),
        ((3 * BLOCK, WIDTH), BF16), ((LANES, WIDTH), BF16), ((LANES, WIDTH), BF16),
        (block, F32), (block, F32), (block, F32),
        (block, BF16), (block, BF16), (block, BF16), (block, BF16), (block, BF16),
        ((LANES, WIDTH), F32), ((LANES, WIDTH), F32), ((LANES, WIDTH), F32),
        ((3 * BLOCK, WIDTH), BF16), ((8 * BLOCK, WIDTH), BF16),
    ]
    return pl.pallas_call(
        main_kernel,
        out_shape=[out, out, out, out, jax.ShapeDtypeStruct((40, WIDTH), F32)],
        in_specs=[vmem] * 8,
        out_specs=[vmem] * 5,
        scratch_shapes=[pltpu.VMEM(shape, dtype) for shape, dtype in scratch]
        + [pltpu.SemaphoreType.DMA((MESSAGES,)), pltpu.SemaphoreType.DMA((MESSAGES,))],
        compiler_params=pltpu.CompilerParams(
            collective_id=0, has_side_effects=True, vmem_limit_bytes=48 * 2**20
        ),
        name="window_backward",
    )(queries, keys, values, inputs, gate, coef, rate, cotangent)


def reduce_kernel(z_size, y_size, part_ref, out_ref, mine, first, second, third, done, acc, send_sem, recv_sem):
    dp, xpos = lax.axis_index("dp"), lax.axis_index("seq")
    z, y, core = dp // (y_size * 2), (dp // 2) % y_size, dp % 2
    eight = xpos * 2 + core

    def octet(hop):
        other = lax.rem(eight + hop, 8)
        return {"dp": (z * y_size + y) * 2 + other % 2, "seq": other // 2}

    def along_y(hop):
        return {"dp": (z * y_size + lax.rem(y + hop, y_size)) * 2 + core, "seq": xpos}

    def along_z(hop):
        return {"dp": (lax.rem(z + hop, z_size) * y_size + y) * 2 + core, "seq": xpos}

    groups = [(octet, 8), (along_y, y_size), (along_z, z_size)]
    barrier = pltpu.get_barrier_semaphore()
    partners = 0
    for where, size in groups:
        for hop in range(1, size):
            pl.semaphore_signal(barrier, inc=1, device_id=where(hop), device_id_type=MESH)
            partners += 1
    for chunk in range(8):
        mine[chunk] = part_ref[:, chunk * LANES : (chunk + 1) * LANES].astype(BF16)
    pl.semaphore_wait(barrier, partners)

    def exchange(base, size, where, source, target):
        made = []
        for hop in range(1, size):
            made.append(
                pltpu.make_async_remote_copy(
                    src_ref=source(hop),
                    dst_ref=target(hop),
                    send_sem=send_sem.at[base + hop],
                    recv_sem=recv_sem.at[base + hop],
                    device_id=where(hop),
                    device_id_type=MESH,
                )
            )
        for made_copy in made:
            made_copy.start()
        return made

    copies = exchange(
        0, 8, octet, lambda hop: mine.at[lax.rem(eight + hop, 8)], lambda hop: first.at[eight]
    )
    first[eight] = mine[eight]
    for made in copies:
        made.wait_recv()
    total = first[0].astype(F32)
    for index in range(1, 8):
        total = total + first[index].astype(F32)
    second[y] = total.astype(BF16)
    more = exchange(8, y_size, along_y, lambda hop: second.at[y], lambda hop: second.at[y])
    for made in more:
        made.wait_recv()
    copies += more
    total = second[0].astype(F32)
    for index in range(1, y_size):
        total = total + second[index].astype(F32)
    third[z] = total.astype(BF16)
    more = exchange(8 + y_size, z_size, along_z, lambda hop: third.at[z], lambda hop: third.at[z])
    for made in more:
        made.wait_recv()
    copies += more
    total = third[0].astype(F32)
    for index in range(1, z_size):
        total = total + third[index].astype(F32)
    done[eight] = total.astype(BF16)
    more = exchange(
        8 + y_size + z_size, 8, octet, lambda hop: done.at[eight], lambda hop: done.at[eight]
    )
    for made in more:
        made.wait_recv()
    copies += more
    for chunk in range(8):
        out_ref[:, chunk * LANES : (chunk + 1) * LANES] = done[chunk].astype(F32)
    for made in copies:
        made.wait_send()


def reduce_call(part, z_size, y_size):
    vmem = pl.BlockSpec(memory_space=pltpu.VMEM)
    chunk = (part.shape[0], LANES)
    count = 16 + y_size + z_size
    return pl.pallas_call(
        functools.partial(reduce_kernel, z_size, y_size),
        out_shape=jax.ShapeDtypeStruct(part.shape, F32),
        in_specs=[vmem],
        out_specs=vmem,
        scratch_shapes=[
            pltpu.VMEM((8,) + chunk, BF16),
            pltpu.VMEM((8,) + chunk, BF16),
            pltpu.VMEM((y_size,) + chunk, BF16),
            pltpu.VMEM((z_size,) + chunk, BF16),
            pltpu.VMEM((8,) + chunk, BF16),
            pltpu.VMEM(chunk, F32),
            pltpu.SemaphoreType.DMA((count,)),
            pltpu.SemaphoreType.DMA((count,)),
        ],
        compiler_params=pltpu.CompilerParams(
            collective_id=1, has_side_effects=True, vmem_limit_bytes=16 * 2**20
        ),
        name="sum_parameters",
    )(part)


def on_device(z_size, y_size, queries, keys, values, inputs, gate, coef, rate, cotangent):
    dq, dk, dv, dx, part = main_call(
        queries[0], keys[0], values[0], inputs[0], gate.T, coef[None], rate[None], cotangent[0]
    )
    if z_size:
        total = reduce_call(part, z_size, y_size)
    else:
        total = lax.psum(part, ("dp", "seq"))
    return (
        dq[None], dk[None], dv[None], dx[None],
        total[:32].T, total[32], total[33, :HEADS],
    )


def solution(mesh):
    rows = P("dp", "seq", None)
    sizes = (8, 4) if mesh.shape["dp"] == 64 else (0, 0)
    return jax.shard_map(
        functools.partial(on_device, *sizes),
        mesh=mesh,
        in_specs=(rows, rows, rows, rows, P(), P(), P(), rows),
        out_specs=(rows, rows, rows, rows, P(), P(), P()),
        check_vma=False,
    )
```

```python
import functools

import jax
import jax.numpy as jnp
from jax import lax
from jax.experimental import pallas as pl
from jax.experimental.pallas import tpu as pltpu
from jax.sharding import PartitionSpec as P

BLOCK = 64
LANES = 128
WIDTH = 1024
PAIRS = WIDTH // LANES
HEADS = 16
F32 = jnp.float32
BF16 = jnp.bfloat16
MESH = pl.DeviceIdType.MESH


def nn(a, b):
    return lax.dot_general(a, b, (((1,), (0,)), ((), ())), preferred_element_type=F32)


def nt(a, b):
    return lax.dot_general(a, b, (((1,), (1,)), ((), ())), preferred_element_type=F32)


def tn(a, b):
    return lax.dot_general(a, b, (((0,), (0,)), ((), ())), preferred_element_type=F32)


def pieces(a, count):
    parts = []
    for _ in range(count):
        part = a.astype(BF16)
        parts.append(part)
        a = a - part.astype(F32)
    return parts


def flag(condition):
    return jnp.where(condition, 1.0, 0.0).astype(BF16)


def iota(shape, dimension):
    return lax.broadcasted_iota(jnp.int32, shape, dimension)


Q_UP, G_UP, L_UP, S_UP, SS2_UP, SS3_UP, TOT1, TOT2, TOT3 = range(9)
P_DN, R_DN, T2_DN, T3_DN, DQ_DN, DA_DN = range(9, 15)
MESSAGES = 15
LOADS = 8
TALL = 48


def main_kernel(
    z_size, y_size,
    q_hbm, k_hbm, v_hbm, x_hbm, w_hbm, coef_hbm, rate_hbm, g_hbm,
    dq_ref, dk_ref, dv_ref, dx_ref, gate_ref, coef_out, rate_out,
    q_ref, k_ref, v_ref, x_ref, g_ref, w_ref, coef_ref, rate_ref,
    qn, gn, lbuf, tot, tot_in, s1_out, ss_out, s1_in, ss_in, p_out, r_out, t_out, p_in, r_in, t_in,
    dqn_out, dqn_in, dan_out, dan_in,
    lrow, lx, gamma_x, blast_x, qf, wk, gq, s1c, u0c, c1c, m_in, m_mid, n_mid, n_end, z_end,
    dqf, dwk, dvf, gmat, xmat, coef_sum,
    mine, first, second, third, done,
    load_sem, send_sem, recv_sem, sum_send, sum_recv,
):
    place, dp = lax.axis_index("seq"), lax.axis_index("dp")
    z, y, core = dp // (y_size * 2), (dp // 2) % y_size, dp % 2
    last = 3

    loads = [
        pltpu.make_async_copy(source, target, load_sem.at[index])
        for index, (source, target) in enumerate(
            (
                (x_hbm, x_ref), (w_hbm, w_ref), (rate_hbm, rate_ref), (coef_hbm, coef_ref),
                (k_hbm, k_ref), (q_hbm, q_ref), (v_hbm, v_ref), (g_hbm, g_ref),
            )
        )
    ]
    for load in loads:
        load.start()
    def copy(source, target, message, to):
        return pltpu.make_async_remote_copy(
            src_ref=source,
            dst_ref=target,
            send_sem=send_sem.at[message],
            recv_sem=recv_sem.at[message],
            device_id={"seq": to},
            device_id_type=MESH,
        )

    up1, up2, up3 = place - 1, place - 2, place - 3
    dn1, dn2, dn3 = place + 1, place + 2, place + 3
    around = [lax.rem(place + 4 - hop, 4) for hop in (1, 2, 3)]
    copies = {
        Q_UP: (copy(q_ref.at[pl.ds(0, BLOCK)], qn, Q_UP, up1), 1),
        G_UP: (copy(g_ref.at[pl.ds(0, BLOCK)], gn, G_UP, up1), 1),
        L_UP: (copy(lbuf.at[pl.ds(0, BLOCK)], lbuf.at[pl.ds(2 * BLOCK, BLOCK)], L_UP, up1), 1),
        S_UP: (copy(s1_out, s1_in, S_UP, up1), 1),
        SS2_UP: (copy(ss_out, ss_in.at[0], SS2_UP, up2), 2),
        SS3_UP: (copy(ss_out, ss_in.at[1], SS3_UP, up3), 3),
        TOT1: (copy(tot, tot_in.at[0], TOT1, around[0]), 0),
        TOT2: (copy(tot, tot_in.at[1], TOT2, around[1]), 0),
        TOT3: (copy(tot, tot_in.at[2], TOT3, around[2]), 0),
        P_DN: (copy(p_out, p_in, P_DN, dn1), -1),
        R_DN: (copy(r_out, r_in, R_DN, dn1), -1),
        T2_DN: (copy(t_out, t_in.at[0], T2_DN, dn2), -2),
        T3_DN: (copy(t_out, t_in.at[1], T3_DN, dn3), -3),
        DQ_DN: (copy(dqn_out, dqn_in, DQ_DN, dn1), -1),
        DA_DN: (copy(dan_out, dan_in, DA_DN, dn1), -1),
    }

    def guarded(steps, action):
        if steps == 0:
            action()
        elif steps > 0:
            pl.when(place >= steps)(action)
        else:
            pl.when(place <= last + steps)(action)

    def send(*messages):
        for message in messages:
            description, steps = copies[message]
            guarded(steps, description.start)

    def sent(message):
        description, steps = copies[message]
        guarded(steps, description.wait_send)

    def received(*messages):
        for message in messages:
            description, steps = copies[message]
            guarded(-steps, description.wait_recv)

    eight = place * 2 + core

    def octet(hop):
        other = lax.rem(eight + hop, 8)
        return {"dp": (z * y_size + y) * 2 + other % 2, "seq": other // 2}

    def along_y(hop):
        return {"dp": (z * y_size + lax.rem(y + hop, y_size)) * 2 + core, "seq": place}

    def along_z(hop):
        return {"dp": (lax.rem(z + hop, z_size) * y_size + y) * 2 + core, "seq": place}

    barrier = pltpu.get_barrier_semaphore()
    partners = 0
    for where, size in ((octet, 8), (along_y, y_size), (along_z, z_size)):
        for hop in range(1, size):
            pl.semaphore_signal(barrier, inc=1, device_id=where(hop), device_id_type=MESH)
            partners += 1

    @pl.when(place == last)
    def _():
        qn[...] = jnp.zeros_like(qn)
        gn[...] = jnp.zeros_like(gn)
        lbuf[pl.ds(2 * BLOCK, BLOCK), :] = jnp.zeros((BLOCK, LANES), F32)
        s1_in[...] = jnp.zeros_like(s1_in)

    for hop in (2, 3):
        @pl.when(place > last - hop)
        def _():
            ss_in[hop - 2] = jnp.zeros(ss_in.shape[1:], BF16)

        @pl.when(place < hop)
        def _():
            t_in[hop - 2] = jnp.zeros(t_in.shape[1:], BF16)

    @pl.when(place == 0)
    def _():
        p_in[...] = jnp.zeros_like(p_in)
        r_in[...] = jnp.zeros_like(r_in)
        dqn_in[...] = jnp.zeros_like(dqn_in)
        dan_in[...] = jnp.zeros_like(dan_in)

    row, col = iota((LANES, LANES), 0), iota((LANES, LANES), 1)
    same = (row // BLOCK) == (col // BLOCK)
    tri = flag(same & (col <= row))
    head_row = iota((LANES, WIDTH), 0)
    head_lane = iota((LANES, WIDTH), 1) // BLOCK
    spread = flag(head_row == head_lane)
    spread_gate = flag(head_row == head_lane + HEADS)
    left = iota((BLOCK, LANES), 1) < BLOCK
    left1 = iota((1, LANES), 1) < BLOCK
    srow, scol = iota((BLOCK, BLOCK), 0), iota((BLOCK, BLOCK), 1)
    upper_in = flag(scol >= srow)
    lower = flag(scol < srow)
    at_or_before = flag(scol <= srow)
    after = flag(scol > srow)

    loads[0].wait()
    loads[1].wait()
    loads[2].wait()
    w_hi, w_lo = pieces(
        jnp.concatenate([w_ref[...], jnp.zeros((LANES - 2 * HEADS, WIDTH), F32)], axis=0), 2
    )
    x = x_ref[...]
    logits = nt(x, w_hi) + nt(x, w_lo)
    small = jnp.exp(-jnp.abs(logits))
    soft = jnp.maximum(logits, 0.0) + jnp.log1p(small)
    sig = jnp.where(logits >= 0.0, 1.0, small) / (1.0 + small)
    rate = jnp.concatenate([rate_ref[...], jnp.zeros((1, LANES - HEADS), F32)], axis=1)
    decay = -rate * soft
    gamma = sig * (1.0 / BLOCK)
    log_own = sum(nn(tri, part) for part in pieces(decay, 3))
    lbuf[pl.ds(0, LANES), :] = log_own
    tot[...] = jnp.zeros_like(tot)
    tot[0:1, :] = log_own[BLOCK - 1 : BLOCK]
    tot[1:2, :] = log_own[LANES - 1 :]

    def expand(a, count):
        return sum(nn(part, spread) for part in pieces(a, count))

    def block_rows(logs, block, offset):
        pick = flag(row == (col % BLOCK) + offset)
        turned = sum(tn(part, pick) for part in pieces(logs, 3))
        for pair in range(PAIRS):
            lrow[block : block + 1, pl.ds(pair * LANES, LANES)] = jnp.where(
                left1, turned[2 * pair : 2 * pair + 1], turned[2 * pair + 1 : 2 * pair + 2]
            )

    lx[pl.ds(0, LANES), :] = expand(log_own, 3)
    gamma_x[...] = sum(nn(part, spread_gate) for part in pieces(gamma, 2))

    tail0 = jnp.exp(log_own[BLOCK - 1 : BLOCK] - log_own[:BLOCK])
    tail1 = jnp.exp(log_own[LANES - 1 :] - log_own[BLOCK:])

    def ending(mask, tail):
        return expand(sum(nn(mask, part) for part in pieces(tail, 2)), 2)

    blast_x[pl.ds(0, BLOCK), :] = ending(upper_in, tail0)
    blast_x[pl.ds(BLOCK, BLOCK), :] = ending(lower, tail1)
    blast_x[pl.ds(2 * BLOCK, BLOCK), :] = ending(upper_in, tail1)

    def each_pair(step):
        lax.fori_loop(0, PAIRS, step, 0, unroll=PAIRS)

    def lanes_of(pair):
        return pl.ds(pl.multiple_of(pair * LANES, LANES), LANES)

    def phi(raw, coef):
        value = raw.astype(F32)
        return 0.125 * (value + coef * value * value)

    def compact(full):
        return jnp.where(left, full[:BLOCK], full[BLOCK:])

    def diagonal(value):
        none = jnp.zeros_like(value)
        return jnp.concatenate([jnp.where(left, value, none), jnp.where(left, none, value)], axis=0)

    def weighted(a, weights):
        return (a.astype(F32) * weights).astype(BF16)

    for load in loads[3:]:
        load.wait()

    def own_step(pair, carry):
        at = lanes_of(pair)
        coef = coef_ref[:, at]
        q_feat = phi(q_ref[:, at], coef).astype(BF16)
        qf[pl.ds(0, LANES), at] = q_feat
        keys = (phi(k_ref[:, at], coef) * gamma_x[:, at]).astype(BF16)
        wk[:, at] = keys
        logs = lx[pl.ds(0, LANES), at]
        scaled = weighted(g_ref[:, at], jnp.exp(logs))
        gq[:, at] = scaled
        s0 = compact(tn(q_feat[:BLOCK], scaled[:BLOCK]))
        s1 = compact(tn(q_feat[BLOCK:], scaled[BLOCK:]))
        fall0 = jnp.exp(logs[BLOCK - 1 : BLOCK])
        fall1 = jnp.exp(logs[LANES - 1 :])
        s1_out[:, at] = s1.astype(BF16)
        ss_out[:, at] = (s0 + fall0 * s1).astype(BF16)
        values = v_ref[:, at]
        weights = blast_x[pl.ds(0, 3 * BLOCK), at]
        carried0 = weighted(keys[:BLOCK], weights[:BLOCK])
        carried1 = weighted(keys, weights[BLOCK:])
        u0 = compact(tn(carried0, values[:BLOCK]))
        c1 = fall1 * u0 + compact(tn(carried1, values))
        u0c[:, at] = u0
        c1c[:, at] = c1
        s1c[:, at] = s1
        p_out[:, at] = c1.astype(BF16)
        return carry

    each_pair(own_step)
    pl.semaphore_wait(barrier, partners)
    send(L_UP, TOT1, TOT2, TOT3, Q_UP, G_UP, S_UP, SS2_UP, SS3_UP, P_DN)

    block_rows(log_own, 0, 0)
    block_rows(log_own, 1, BLOCK)

    step = col % BLOCK
    cur_mask = flag(same & (row % BLOCK >= step))
    prev_mask = flag(same & (row % BLOCK < step))
    both_mask = jnp.concatenate([cur_mask, prev_mask], axis=1)
    causal = (iota((LANES, LANES), 1) % BLOCK) <= (iota((LANES, LANES), 0) % BLOCK)

    def spans(rows):
        return pl.ds(rows.start, rows.stop - rows.start)

    first_rows, last_rows = slice(0, BLOCK), slice(BLOCK, LANES)

    def tile(keys_bd, values_bd, queries, grads, kernel):
        scores = nt(queries, keys_bd)
        d_weights = nt(grads, values_bd).astype(BF16).astype(F32)
        weights = (scores * kernel).astype(BF16)
        d_scores = (d_weights * kernel).astype(BF16)
        d_kernel = (d_weights * scores).astype(BF16)
        return (
            nn(d_scores, keys_bd),
            compact(tn(weights, grads)),
            compact(tn(d_scores, queries)),
            d_kernel,
        )

    def window_step(pair, carry):
        at = lanes_of(pair)
        keys, values = wk[:, at], v_ref[:, at]
        queries, grads = qf[pl.ds(0, LANES), at], g_ref[:, at]
        rows = jnp.concatenate(
            [jnp.broadcast_to(lrow[b : b + 1, at], (BLOCK, LANES)) for b in range(2)], axis=0
        )
        gaps = jnp.where(causal, lx[pl.ds(0, LANES), at] - rows, 0.0)
        decays = jnp.where(causal, jnp.exp(gaps), 0.0)
        low = decays.astype(BF16)
        start = nn(low[:BLOCK], cur_mask)
        middle = nn(low[BLOCK:], both_mask)
        dq0, dv0, dk0, db0 = tile(
            diagonal(keys[:BLOCK]), diagonal(values[:BLOCK]), queries, grads,
            jnp.concatenate([start, middle[:, LANES:]], axis=0),
        )
        dq1, dv1, dk1, db1 = tile(
            diagonal(keys[BLOCK:]), diagonal(values[BLOCK:]), queries[BLOCK:], grads[BLOCK:],
            middle[:, :LANES],
        )
        dvf[pl.ds(0, BLOCK), at] = dv0
        dvf[pl.ds(BLOCK, BLOCK), at] = dv1
        dwk[pl.ds(0, BLOCK), at] = dk0
        dwk[pl.ds(BLOCK, BLOCK), at] = dk1
        dqf[pl.ds(0, BLOCK), at] = dq0[:BLOCK]
        dqf[pl.ds(BLOCK, BLOCK), at] = dq0[BLOCK:] + dq1
        d_decays = jnp.concatenate(
            [
                nt(db0[:BLOCK], cur_mask),
                nt(jnp.concatenate([db1, db0[BLOCK:]], axis=1), both_mask),
            ],
            axis=0,
        )
        gmat[pl.ds(0, LANES), at] = (d_decays * decays).astype(BF16)
        return carry

    received(L_UP)
    log_next = lbuf[pl.ds(2 * BLOCK, BLOCK), :]
    lx[pl.ds(LANES, BLOCK), :] = expand(log_next, 3)
    tail2 = jnp.exp(log_next[BLOCK - 1 :] - log_next)
    blast_x[pl.ds(3 * BLOCK, BLOCK), :] = ending(lower, tail2)

    def next_step(pair, carry):
        at = lanes_of(pair)
        fall2 = jnp.exp(lx[3 * BLOCK - 1 : 3 * BLOCK, at])
        carried = weighted(wk[pl.ds(BLOCK, BLOCK), at], blast_x[pl.ds(3 * BLOCK, BLOCK), at])
        r = compact(tn(carried, v_ref[pl.ds(BLOCK, BLOCK), at]))
        r_out[:, at] = r.astype(BF16)
        t_out[:, at] = (fall2 * c1c[:, at] + r).astype(BF16)
        return carry

    each_pair(next_step)
    send(T2_DN, T3_DN, R_DN)

    each_pair(window_step)
    block_rows(lbuf[pl.ds(BLOCK, LANES), :], 2, BLOCK)

    received(Q_UP, G_UP)

    def cross_step(pair, carry):
        at = lanes_of(pair)
        queries = phi(qn[:, at], coef_ref[:, at]).astype(BF16)
        grads = gn[:, at]
        logs = lx[pl.ds(LANES, BLOCK), at]
        held = causal[:BLOCK]
        decays = jnp.where(held, jnp.exp(jnp.where(held, logs - lrow[2:3, at], 0.0)), 0.0)
        dq, dv, dk, db = tile(
            diagonal(wk[pl.ds(BLOCK, BLOCK), at]), diagonal(v_ref[pl.ds(BLOCK, BLOCK), at]),
            queries, grads, nn(decays.astype(BF16), prev_mask),
        )
        dqn_out[:, at] = dq.astype(BF16)
        dvf[pl.ds(BLOCK, BLOCK), at] = dvf[pl.ds(BLOCK, BLOCK), at] + dv
        dwk[pl.ds(BLOCK, BLOCK), at] = dwk[pl.ds(BLOCK, BLOCK), at] + dk
        gmat[pl.ds(LANES, BLOCK), at] = (nt(db, prev_mask) * decays).astype(BF16)
        c1c[:, at] = compact(tn(queries, weighted(grads, jnp.exp(logs))))
        return carry

    each_pair(cross_step)
    send(DQ_DN)

    def decay_grad(block):
        later = nn(upper_in, gmat[pl.ds(block * BLOCK, BLOCK), :])
        lanes = iota((BLOCK, WIDTH), 1) % BLOCK
        kept = jnp.where(lanes < iota((BLOCK, WIDTH), 0), later, 0.0)
        return sum(nt(part, spread) for part in pieces(kept, 2))

    def twice(mask, a):
        return sum(nn(mask, part) for part in pieces(a, 2))

    received(TOT1, S_UP, TOT2, SS2_UP, SS3_UP, TOT3)
    falls = [expand(tot_in[slot], 3) for slot in range(3)]
    next1_fall1 = jnp.exp(falls[0][1:2])
    next2_all = jnp.exp(falls[1][0:1] + falls[1][1:2])
    prev1_fall1 = jnp.exp(falls[2][1:2])
    prev1_all = jnp.exp(falls[2][0:1] + falls[2][1:2])
    prev2_fall1 = jnp.exp(falls[1][1:2])
    own0 = jnp.exp(lx[BLOCK - 1 : BLOCK, :])
    own1 = jnp.exp(lx[LANES - 1 : LANES, :])
    next0 = jnp.exp(lx[3 * BLOCK - 1 :, :])
    z_grad = s1_in[...].astype(F32) + next1_fall1 * (
        ss_in[0].astype(F32) + next2_all * ss_in[1].astype(F32)
    )
    z_end[...] = z_grad.astype(BF16)
    end_grad = next0 * z_grad + c1c[...]
    mid_grad = own1 * end_grad + s1c[...]
    n_end[...] = end_grad.astype(BF16)
    n_mid[...] = mid_grad.astype(BF16)

    def enter(index, keys, d_role, at):
        weights = blast_x[pl.ds(index * BLOCK, BLOCK), at]
        own_keys = keys.astype(F32)
        d_role = d_role.astype(BF16).astype(F32)
        xmat[pl.ds(index * BLOCK, BLOCK), at] = (d_role * own_keys).astype(BF16)
        return (own_keys * weights).astype(BF16), d_role * weights

    def outer_step(pair, carry):
        at = lanes_of(pair)
        rows = pl.ds(BLOCK, BLOCK)
        grads = diagonal(z_end[:, at])
        carried, d_keys = enter(3, wk[rows, at], nt(v_ref[rows, at], grads), at)
        dwk[rows, at] = dwk[rows, at] + d_keys
        dvf[rows, at] = dvf[rows, at] + nn(carried, grads)
        return carry

    each_pair(outer_step)
    d_last = nt(xmat[pl.ds(3 * BLOCK, BLOCK), :], spread)
    dan_out[...] = decay_grad(2) + twice(lower, twice(after, d_last) * tail2)
    send(DA_DN)

    def inner_step(pair, carry):
        at = lanes_of(pair)
        keys, values = wk[:, at], v_ref[:, at]
        grads_end = diagonal(n_end[:, at])
        both = jnp.concatenate([diagonal(n_mid[:, at]), grads_end], axis=0)
        d_first = nt(values[:BLOCK], both)
        carried0, d_keys0 = enter(0, keys[:BLOCK], d_first[:, :LANES], at)
        carried1, d_keys1 = enter(1, keys[:BLOCK], d_first[:, LANES:], at)
        carried2, d_keys2 = enter(2, keys[BLOCK:], nt(values[BLOCK:], grads_end), at)
        dv_ref[pl.ds(0, BLOCK), at] = (
            dvf[pl.ds(0, BLOCK), at] + nn(jnp.concatenate([carried0, carried1], axis=1), both)
        ).astype(BF16)
        dv_ref[pl.ds(BLOCK, BLOCK), at] = (
            dvf[pl.ds(BLOCK, BLOCK), at] + nn(carried2, grads_end)
        ).astype(BF16)
        d_keys = dwk[:, at] + jnp.concatenate([d_keys0 + d_keys1, d_keys2], axis=0)
        coef = coef_ref[:, at]
        raw = k_ref[:, at].astype(F32)
        d_feat = d_keys * gamma_x[:, at]
        square = 0.125 * raw * raw
        xmat[pl.ds(6 * BLOCK, LANES), at] = (d_keys * (0.125 * raw + coef * square)).astype(BF16)
        dk_ref[:, at] = (d_feat * (0.125 + (0.25 * coef) * raw)).astype(BF16)
        coef_sum[0:1, at] = jnp.sum(d_feat * square, axis=0, keepdims=True)
        return carry

    each_pair(inner_step)
    d_enter = nt(xmat[pl.ds(0, 3 * BLOCK), :], spread)
    d_gate = nt(xmat[pl.ds(6 * BLOCK, LANES), :], spread)
    shift = flag(col == row + HEADS)
    d_gamma = sum(nn(part, shift) for part in pieces(d_gate, 2))
    d_decay0 = decay_grad(0) + twice(lower, twice(at_or_before, d_enter[:BLOCK]) * tail0)
    d_decay1 = decay_grad(1) + twice(
        lower,
        (twice(at_or_before, d_enter[2 * BLOCK :]) + twice(after, d_enter[BLOCK : 2 * BLOCK]))
        * tail1,
    )

    received(P_DN, R_DN, T2_DN, T3_DN)
    memory = (
        p_in[...].astype(F32)
        + prev1_fall1 * t_in[0].astype(F32)
        + (prev2_fall1 * prev1_all) * t_in[1].astype(F32)
    )
    middle_memory = own0 * memory + r_in[...].astype(F32) + u0c[...]
    m_in[...] = memory.astype(BF16)
    m_mid[...] = middle_memory.astype(BF16)
    fall_grad = jnp.concatenate(
        [
            own0 * jnp.sum(memory * mid_grad, axis=0, keepdims=True),
            own1 * jnp.sum(middle_memory * end_grad, axis=0, keepdims=True),
            jnp.zeros((6, WIDTH), F32),
        ],
        axis=0,
    )
    fall_grad = sum(nt(part, spread) for part in pieces(fall_grad, 2))
    received(DQ_DN)

    def query_step(pair, carry):
        at = lanes_of(pair)
        scaled = gq[:, at]
        carried = jnp.concatenate(
            [
                nt(scaled[:BLOCK], diagonal(m_in[:, at])),
                nt(scaled[BLOCK:], diagonal(m_mid[:, at])),
            ],
            axis=0,
        )
        xmat[pl.ds(4 * BLOCK, LANES), at] = (
            carried * qf[pl.ds(0, LANES), at].astype(F32)
        ).astype(BF16)
        coef = coef_ref[:, at]
        raw = q_ref[:, at].astype(F32)
        d_feat = (
            dqf[:, at]
            + carried
            + jnp.concatenate([dqn_in[:, at].astype(F32), jnp.zeros((BLOCK, LANES), F32)], axis=0)
        )
        dq_ref[:, at] = (d_feat * (0.125 + (0.25 * coef) * raw)).astype(BF16)
        coef_sum[0:1, at] = coef_sum[0:1, at] + jnp.sum(
            d_feat * (0.125 * raw * raw), axis=0, keepdims=True
        )
        return carry

    each_pair(query_step)
    d_out = nt(xmat[pl.ds(4 * BLOCK, LANES), :], spread)
    received(DA_DN)
    d_decay = jnp.concatenate(
        [
            d_decay0 + dan_in[...] + twice(upper_in, d_out[:BLOCK]) + fall_grad[0:1],
            d_decay1 + twice(upper_in, d_out[BLOCK:]) + fall_grad[1:2],
        ],
        axis=0,
    )
    is_decay = iota((LANES, LANES), 1) < HEADS
    d_logits = jnp.where(is_decay, -rate * sig * d_decay, d_gamma * gamma * (1.0 - sig))
    rates = jnp.sum(jnp.where(is_decay, -soft * d_decay, 0.0), axis=0, keepdims=True)
    d_hi, d_lo = pieces(d_logits, 2)
    gate = tn(d_hi, x) + tn(d_lo, x)

    def paired(rows):
        high = rows.astype(BF16).astype(F32)
        return jnp.concatenate([high, rows - high], axis=0).astype(BF16)

    no_rates = jnp.zeros((1, LANES), F32)
    for chunk in range(8):
        at = slice(chunk * LANES, (chunk + 1) * LANES)
        mine[chunk, 0:32, :] = gate[:32, at].astype(BF16)
        mine[chunk, 32:TALL, :] = paired(
            jnp.concatenate(
                [
                    coef_sum[0:1, at],
                    rates if chunk == 0 else no_rates,
                    jnp.zeros((6, LANES), F32),
                ],
                axis=0,
            )
        )

    def exchange(base, size, where, source, target):
        made = [
            pltpu.make_async_remote_copy(
                src_ref=source(hop),
                dst_ref=target,
                send_sem=sum_send.at[base + hop],
                recv_sem=sum_recv.at[base + hop],
                device_id=where(hop),
                device_id_type=MESH,
            )
            for hop in range(1, size)
        ]
        for one in made:
            one.start()
        return made

    def added(buffer, count):
        total = buffer[0].astype(F32)
        for index in range(1, count):
            total = total + buffer[index].astype(F32)
        return jnp.concatenate(
            [total[:32].astype(BF16), paired(total[32:40] + total[40:])], axis=0
        )

    made = exchange(0, 8, octet, lambda hop: mine.at[lax.rem(eight + hop, 8)], first.at[eight])
    first[eight] = mine[eight]
    dx_ref[...] = (nn(d_hi, w_hi) + (nn(d_hi, w_lo) + nn(d_lo, w_hi))).astype(BF16)
    for one in made:
        one.wait_recv()
    second[y] = added(first, 8)
    more = exchange(8, y_size, along_y, lambda hop: second.at[y], second.at[y])
    for one in more:
        one.wait_recv()
    made += more
    third[z] = added(second, y_size)
    more = exchange(8 + y_size, z_size, along_z, lambda hop: third.at[z], third.at[z])
    for one in more:
        one.wait_recv()
    made += more
    done[eight] = added(third, z_size)
    more = exchange(8 + y_size + z_size, 8, octet, lambda hop: done.at[eight], done.at[eight])
    for message in range(MESSAGES):
        sent(message)
    for one in more:
        one.wait_recv()
    made += more
    for chunk in range(8):
        at = slice(chunk * LANES, (chunk + 1) * LANES)
        total = done[chunk].astype(F32)
        gate_ref[:, at] = total[:32]
        rest = total[32:40] + total[40:]
        coef_out[:, at] = rest[0:1]
        if chunk == 0:
            rate_out[...] = rest[1:2, :HEADS]
    for one in made:
        one.wait_send()


def main_call(sizes, queries, keys, values, inputs, gate, coef, rate, cotangent):
    z_size, y_size = sizes
    rows = queries.shape[0]
    anywhere = pl.BlockSpec(memory_space=pltpu.HBM)
    block, full = (BLOCK, WIDTH), (LANES, WIDTH)
    out = jax.ShapeDtypeStruct((rows, WIDTH), BF16)
    tile = (TALL, LANES)
    scratch = [
        (full, BF16), (full, BF16), (full, BF16), (full, BF16), (full, BF16),
        (gate.shape, F32), (coef.shape, F32), (rate.shape, F32),
        (block, BF16), (block, BF16), ((3 * BLOCK, LANES), F32), ((8, LANES), F32), ((3, 8, LANES), F32),
        (block, BF16), (block, BF16), (block, BF16), ((2,) + block, BF16),
        (block, BF16), (block, BF16), (block, BF16), (block, BF16), (block, BF16), ((2,) + block, BF16),
        (block, BF16), (block, BF16), ((BLOCK, LANES), F32), ((BLOCK, LANES), F32),
        ((8, WIDTH), F32), ((3 * BLOCK, WIDTH), F32), (full, F32), ((4 * BLOCK, WIDTH), F32),
        (full, BF16), (full, BF16), (full, BF16),
        (block, F32), (block, F32), (block, F32),
        (block, BF16), (block, BF16), (block, BF16), (block, BF16), (block, BF16),
        (full, F32), (full, F32), (full, F32),
        ((3 * BLOCK, WIDTH), BF16), ((8 * BLOCK, WIDTH), BF16), ((8, WIDTH), F32),
        ((8,) + tile, BF16), ((8,) + tile, BF16), ((y_size,) + tile, BF16), ((z_size,) + tile, BF16),
        ((8,) + tile, BF16),
    ]
    count = 16 + y_size + z_size
    return pl.pallas_call(
        functools.partial(main_kernel, z_size, y_size),
        out_shape=[out, out, out, out]
        + [jax.ShapeDtypeStruct(a.shape, F32) for a in (gate, coef, rate)],
        in_specs=[anywhere] * 8,
        out_specs=[pl.BlockSpec(memory_space=pltpu.VMEM)] * 7,
        scratch_shapes=[pltpu.VMEM(shape, dtype) for shape, dtype in scratch]
        + [
            pltpu.SemaphoreType.DMA((number,))
            for number in (LOADS, MESSAGES, MESSAGES, count, count)
        ],
        compiler_params=pltpu.CompilerParams(
            collective_id=0, has_side_effects=True, vmem_limit_bytes=56 * 2**20
        ),
        name="window_backward",
    )(queries, keys, values, inputs, gate, coef, rate, cotangent)


def hand_out_kernel(*refs):
    count = 7
    sources, targets, sem = refs[:count], refs[count : 2 * count], refs[2 * count]
    copies = [
        pltpu.make_async_copy(source, target, sem.at[index])
        for index, (source, target) in enumerate(zip(sources, targets))
    ]
    for one in copies:
        one.start()
    for one in copies:
        one.wait()


def hand_out(results):
    anywhere = pl.BlockSpec(memory_space=pltpu.HBM)
    return pl.pallas_call(
        hand_out_kernel,
        out_shape=[jax.ShapeDtypeStruct(a.shape, a.dtype) for a in results],
        in_specs=[pl.BlockSpec(memory_space=pltpu.VMEM)] * len(results),
        out_specs=[anywhere] * len(results),
        scratch_shapes=[pltpu.SemaphoreType.DMA((len(results),))],
        name="hand_out",
    )(*results)


def on_device(sizes, queries, keys, values, inputs, gate, coef, rate, cotangent):
    results = main_call(
        sizes,
        queries[0], keys[0], values[0], inputs[0], gate.T, coef[None], rate[None], cotangent[0],
    )
    dq, dk, dv, dx, d_gate, d_coef, d_rate = hand_out(results)
    return (dq[None], dk[None], dv[None], dx[None], d_gate.T, d_coef[0], d_rate[0])


def solution(mesh):
    rows = P("dp", "seq", None)
    y_size = min(4, max(1, mesh.shape["dp"] // 2))
    sizes = (mesh.shape["dp"] // (2 * y_size), y_size)
    return jax.shard_map(
        functools.partial(on_device, sizes),
        mesh=mesh,
        in_specs=(rows, rows, rows, rows, P(), P(), P(), rows),
        out_specs=(rows, rows, rows, rows, P(), P(), P()),
        check_vma=False,
    )
```

```python
import functools

import jax
import jax.numpy as jnp
from jax import lax
from jax.experimental import pallas as pl
from jax.experimental.pallas import tpu as pltpu
from jax.sharding import PartitionSpec as P

BLOCK = 64
LANES = 128
WIDTH = 1024
PAIRS = WIDTH // LANES
HEADS = 16
F32 = jnp.float32
BF16 = jnp.bfloat16
MESH = pl.DeviceIdType.MESH


def nn(a, b):
    return lax.dot_general(a, b, (((1,), (0,)), ((), ())), preferred_element_type=F32)


def nt(a, b):
    return lax.dot_general(a, b, (((1,), (1,)), ((), ())), preferred_element_type=F32)


def tn(a, b):
    return lax.dot_general(a, b, (((0,), (0,)), ((), ())), preferred_element_type=F32)


def pieces(a, count):
    parts = []
    for _ in range(count):
        part = a.astype(BF16)
        parts.append(part)
        a = a - part.astype(F32)
    return parts


def flag(condition):
    return jnp.where(condition, 1.0, 0.0).astype(BF16)


def iota(shape, dimension):
    return lax.broadcasted_iota(jnp.int32, shape, dimension)


Q_UP, G_UP, L_UP, S_UP, SS2_UP, SS3_UP, TOT1, TOT2, TOT3 = range(9)
P_DN, R_DN, T2_DN, T3_DN, DQ_DN, DA_DN = range(9, 15)
MESSAGES = 15
LOADS = 8
STORES = 5
TALL = 48
NEVER = -1e30


def main_kernel(
    z_size, y_size,
    q_hbm, k_hbm, v_hbm, x_hbm, w_hbm, coef_hbm, rate_hbm, g_hbm,
    dq_hbm, dk_hbm, dv_hbm, dx_hbm, done_hbm,
    q_ref, k_ref, v_ref, x_ref, g_ref, w_ref, coef_ref, rate_ref,
    dq_ref, dk_ref, dv_ref, dx_ref,
    qn, gn, lbuf, tot, tot_in, s1_out, ss_out, s1_in, ss_in, p_out, r_out, t_out, p_in, r_in, t_in,
    dqn_out, dqn_in, dan_out, dan_in,
    lrow, lx, gamma_x, blast_x, qf, wk, gq, s1c, u0c, c1c, m_in, m_mid, n_mid, n_end, z_end,
    dqf, dwk, dvf, gmat, xmat, coef_sum,
    mine, first, second, third, done,
    load_sem, store_sem, send_sem, recv_sem, sum_send, sum_recv,
):
    place, dp = lax.axis_index("seq"), lax.axis_index("dp")
    z, y, core = dp // (y_size * 2), (dp // 2) % y_size, dp % 2
    last = 3

    loads = [
        pltpu.make_async_copy(source, target, load_sem.at[index])
        for index, (source, target) in enumerate(
            (
                (x_hbm, x_ref), (w_hbm, w_ref), (rate_hbm, rate_ref), (coef_hbm, coef_ref),
                (k_hbm, k_ref), (q_hbm, q_ref), (v_hbm, v_ref), (g_hbm, g_ref),
            )
        )
    ]
    for load in loads:
        load.start()
    stores = [
        pltpu.make_async_copy(source, target, store_sem.at[index])
        for index, (source, target) in enumerate(
            ((dq_ref, dq_hbm), (dk_ref, dk_hbm), (dv_ref, dv_hbm), (dx_ref, dx_hbm))
        )
    ]

    def copy(source, target, message, to):
        return pltpu.make_async_remote_copy(
            src_ref=source,
            dst_ref=target,
            send_sem=send_sem.at[message],
            recv_sem=recv_sem.at[message],
            device_id={"seq": to},
            device_id_type=MESH,
        )

    up1, up2, up3 = place - 1, place - 2, place - 3
    dn1, dn2, dn3 = place + 1, place + 2, place + 3
    around = [lax.rem(place + 4 - hop, 4) for hop in (1, 2, 3)]
    copies = {
        Q_UP: (copy(q_ref.at[pl.ds(0, BLOCK)], qn, Q_UP, up1), 1),
        G_UP: (copy(g_ref.at[pl.ds(0, BLOCK)], gn, G_UP, up1), 1),
        L_UP: (copy(lbuf.at[pl.ds(0, BLOCK)], lbuf.at[pl.ds(2 * BLOCK, BLOCK)], L_UP, up1), 1),
        S_UP: (copy(s1_out, s1_in, S_UP, up1), 1),
        SS2_UP: (copy(ss_out, ss_in.at[0], SS2_UP, up2), 2),
        SS3_UP: (copy(ss_out, ss_in.at[1], SS3_UP, up3), 3),
        TOT1: (copy(tot, tot_in.at[0], TOT1, around[0]), 0),
        TOT2: (copy(tot, tot_in.at[1], TOT2, around[1]), 0),
        TOT3: (copy(tot, tot_in.at[2], TOT3, around[2]), 0),
        P_DN: (copy(p_out, p_in, P_DN, dn1), -1),
        R_DN: (copy(r_out, r_in, R_DN, dn1), -1),
        T2_DN: (copy(t_out, t_in.at[0], T2_DN, dn2), -2),
        T3_DN: (copy(t_out, t_in.at[1], T3_DN, dn3), -3),
        DQ_DN: (copy(dqn_out, dqn_in, DQ_DN, dn1), -1),
        DA_DN: (copy(dan_out, dan_in, DA_DN, dn1), -1),
    }

    def guarded(steps, action):
        if steps == 0:
            action()
        elif steps > 0:
            pl.when(place >= steps)(action)
        else:
            pl.when(place <= last + steps)(action)

    def send(*messages):
        for message in messages:
            description, steps = copies[message]
            guarded(steps, description.start)

    def sent(message):
        description, steps = copies[message]
        guarded(steps, description.wait_send)

    def received(*messages):
        for message in messages:
            description, steps = copies[message]
            guarded(-steps, description.wait_recv)

    eight = place * 2 + core

    def octet(hop):
        other = lax.rem(eight + hop, 8)
        return {"dp": (z * y_size + y) * 2 + other % 2, "seq": other // 2}

    def along_y(hop):
        return {"dp": (z * y_size + lax.rem(y + hop, y_size)) * 2 + core, "seq": place}

    def along_z(hop):
        return {"dp": (lax.rem(z + hop, z_size) * y_size + y) * 2 + core, "seq": place}

    barrier = pltpu.get_barrier_semaphore()
    partners = 0
    for where, size in ((octet, 8), (along_y, y_size), (along_z, z_size)):
        for hop in range(1, size):
            pl.semaphore_signal(barrier, inc=1, device_id=where(hop), device_id_type=MESH)
            partners += 1

    @pl.when(place == last)
    def _():
        qn[...] = jnp.zeros_like(qn)
        gn[...] = jnp.zeros_like(gn)
        lbuf[pl.ds(2 * BLOCK, BLOCK), :] = jnp.zeros((BLOCK, LANES), F32)
        s1_in[...] = jnp.zeros_like(s1_in)

    for hop in (2, 3):
        @pl.when(place > last - hop)
        def _():
            ss_in[hop - 2] = jnp.zeros(ss_in.shape[1:], BF16)

        @pl.when(place < hop)
        def _():
            t_in[hop - 2] = jnp.zeros(t_in.shape[1:], BF16)

    @pl.when(place == 0)
    def _():
        p_in[...] = jnp.zeros_like(p_in)
        r_in[...] = jnp.zeros_like(r_in)
        dqn_in[...] = jnp.zeros_like(dqn_in)
        dan_in[...] = jnp.zeros_like(dan_in)

    row, col = iota((LANES, LANES), 0), iota((LANES, LANES), 1)
    same = (row // BLOCK) == (col // BLOCK)
    tri = flag(same & (col <= row))
    head_row = iota((LANES, WIDTH), 0)
    head_lane = iota((LANES, WIDTH), 1) // BLOCK
    spread = flag(head_row == head_lane)
    spread_gate = flag(head_row == head_lane + HEADS)
    spread_pieces = flag(head_row % 32 == head_lane)
    head_lanes = iota((BLOCK, LANES), 1) < HEADS
    left = iota((BLOCK, LANES), 1) < BLOCK
    left1 = iota((1, LANES), 1) < BLOCK
    srow, scol = iota((BLOCK, BLOCK), 0), iota((BLOCK, BLOCK), 1)
    upper_in = flag(scol >= srow)
    lower = flag(scol < srow)
    at_or_before = flag(scol <= srow)
    after = flag(scol > srow)

    loads[0].wait()
    loads[1].wait()
    loads[2].wait()
    w_hi, w_lo = pieces(w_ref[...], 2)
    no_rows = jnp.zeros((32, WIDTH), BF16)
    x = x_ref[...]
    logits = nt(x, jnp.concatenate([w_hi, no_rows, w_lo, no_rows], axis=0))
    logits = logits + jnp.concatenate([logits[:, BLOCK:], logits[:, :BLOCK]], axis=1)
    small = jnp.exp(-jnp.abs(logits))
    soft = jnp.maximum(logits, 0.0) + jnp.log1p(small)
    sig = jnp.where(logits >= 0.0, 1.0, small) / (1.0 + small)
    rate = jnp.concatenate([rate_ref[...], jnp.zeros((1, LANES - HEADS), F32)], axis=1)
    decay = -rate * soft
    gamma = sig * (1.0 / BLOCK)
    log_own = sum(nn(tri, part) for part in pieces(decay, 3))
    lbuf[pl.ds(0, LANES), :] = log_own
    tot[...] = jnp.zeros_like(tot)
    tot[0:1, :] = log_own[BLOCK - 1 : BLOCK]
    tot[1:2, :] = log_own[LANES - 1 :]

    for load in loads[3:]:
        load.wait()
    pl.semaphore_wait(barrier, partners)
    send(L_UP, TOT1, TOT2, TOT3, Q_UP, G_UP)

    def beside(a):
        parts = [part[:, :32] for part in pieces(a, 3)]
        return jnp.concatenate(parts + [jnp.zeros((a.shape[0], 32), BF16)], axis=1)

    def expand(a):
        return nn(beside(a), spread_pieces)

    def block_rows(logs, block, offset):
        pick = flag(row == (col % BLOCK) + offset)
        turned = sum(tn(part, pick) for part in pieces(logs, 3))
        for pair in range(PAIRS):
            lrow[block : block + 1, pl.ds(pair * LANES, LANES)] = jnp.where(
                left1, turned[2 * pair : 2 * pair + 1], turned[2 * pair + 1 : 2 * pair + 2]
            )

    tail0 = jnp.exp(log_own[BLOCK - 1 : BLOCK] - log_own[:BLOCK])
    tail1 = jnp.exp(log_own[LANES - 1 :] - log_own[BLOCK:])

    def twice(mask, a):
        return nn(
            jnp.concatenate([mask, mask], axis=1), jnp.concatenate(pieces(a, 2), axis=0)
        )

    def ending(mask, tail):
        return jnp.where(head_lanes, twice(mask, tail), 0.0)

    gamma_first = jnp.concatenate([gamma[:, HEADS:32], jnp.zeros((LANES, LANES - HEADS), F32)], axis=1)
    expanded = expand(
        jnp.concatenate(
            [log_own, gamma_first, ending(upper_in, tail0), ending(lower, tail1), ending(upper_in, tail1)],
            axis=0,
        )
    )
    lx[pl.ds(0, LANES), :] = expanded[:LANES]
    gamma_x[...] = expanded[LANES : 2 * LANES]
    blast_x[pl.ds(0, 3 * BLOCK), :] = expanded[2 * LANES :]

    def each_pair(step, begin=0, end=PAIRS):
        lax.fori_loop(begin, end, step, 0, unroll=end - begin)

    def lanes_of(pair):
        return pl.ds(pl.multiple_of(pair * LANES, LANES), LANES)

    def phi(raw, coef):
        value = raw.astype(F32)
        return 0.125 * (value + coef * value * value)

    def compact(full):
        return jnp.where(left, full[:BLOCK], full[BLOCK:])

    def diagonal(value):
        none = jnp.zeros_like(value)
        return jnp.concatenate([jnp.where(left, value, none), jnp.where(left, none, value)], axis=0)

    def weighted(a, weights):
        return (a.astype(F32) * weights).astype(BF16)

    def own_step(pair, carry):
        at = lanes_of(pair)
        coef = coef_ref[:, at]
        q_feat = phi(q_ref[:, at], coef).astype(BF16)
        qf[pl.ds(0, LANES), at] = q_feat
        keys = (phi(k_ref[:, at], coef) * gamma_x[:, at]).astype(BF16)
        wk[:, at] = keys
        logs = lx[pl.ds(0, LANES), at]
        scaled = weighted(g_ref[:, at], jnp.exp(logs))
        gq[:, at] = scaled
        s0 = compact(tn(q_feat[:BLOCK], scaled[:BLOCK]))
        s1 = compact(tn(q_feat[BLOCK:], scaled[BLOCK:]))
        fall0 = jnp.exp(logs[BLOCK - 1 : BLOCK])
        fall1 = jnp.exp(logs[LANES - 1 :])
        s1_out[:, at] = s1.astype(BF16)
        ss_out[:, at] = (s0 + fall0 * s1).astype(BF16)
        values = v_ref[:, at]
        weights = blast_x[pl.ds(0, 3 * BLOCK), at]
        carried0 = weighted(keys[:BLOCK], weights[:BLOCK])
        carried1 = weighted(keys, weights[BLOCK:])
        u0 = compact(tn(carried0, values[:BLOCK]))
        c1 = fall1 * u0 + compact(tn(carried1, values))
        u0c[:, at] = u0
        c1c[:, at] = c1
        s1c[:, at] = s1
        p_out[:, at] = c1.astype(BF16)
        return carry

    each_pair(own_step)
    send(S_UP, SS2_UP, SS3_UP, P_DN)

    block_rows(log_own, 0, 0)
    block_rows(log_own, 1, BLOCK)

    step = col % BLOCK
    cur_mask = flag(same & (row % BLOCK >= step))
    prev_mask = flag(same & (row % BLOCK < step))
    both_mask = jnp.concatenate([cur_mask, prev_mask], axis=1)
    causal = (iota((LANES, LANES), 1) % BLOCK) <= (iota((LANES, LANES), 0) % BLOCK)

    def spans(rows):
        return pl.ds(rows.start, rows.stop - rows.start)

    first_rows, last_rows = slice(0, BLOCK), slice(BLOCK, LANES)

    def tile(keys_bd, values_bd, queries, grads, kernel):
        scores = nt(queries, keys_bd)
        d_weights = nt(grads, values_bd)
        weights = (scores * kernel).astype(BF16)
        d_scores = (d_weights * kernel).astype(BF16)
        d_kernel = (d_weights * scores).astype(BF16)
        return (
            nn(d_scores, keys_bd),
            compact(tn(weights, grads)),
            compact(tn(d_scores, queries)),
            d_kernel,
        )

    def window_step(pair, carry):
        at = lanes_of(pair)
        keys, values = wk[:, at], v_ref[:, at]
        queries, grads = qf[pl.ds(0, LANES), at], g_ref[:, at]
        rows = jnp.concatenate(
            [jnp.broadcast_to(lrow[b : b + 1, at], (BLOCK, LANES)) for b in range(2)], axis=0
        )
        decays = jnp.exp(jnp.where(causal, lx[pl.ds(0, LANES), at] - rows, NEVER))
        low = decays.astype(BF16)
        start = nn(low[:BLOCK], cur_mask)
        middle = nn(low[BLOCK:], both_mask)
        dq0, dv0, dk0, db0 = tile(
            diagonal(keys[:BLOCK]), diagonal(values[:BLOCK]), queries, grads,
            jnp.concatenate([start, middle[:, LANES:]], axis=0),
        )
        dq1, dv1, dk1, db1 = tile(
            diagonal(keys[BLOCK:]), diagonal(values[BLOCK:]), queries[BLOCK:], grads[BLOCK:],
            middle[:, :LANES],
        )
        dvf[pl.ds(0, BLOCK), at] = dv0
        dvf[pl.ds(BLOCK, BLOCK), at] = dv1
        dwk[pl.ds(0, BLOCK), at] = dk0
        dwk[pl.ds(BLOCK, BLOCK), at] = dk1
        dqf[pl.ds(0, BLOCK), at] = dq0[:BLOCK]
        dqf[pl.ds(BLOCK, BLOCK), at] = dq0[BLOCK:] + dq1
        d_decays = jnp.concatenate(
            [
                nt(db0[:BLOCK], cur_mask),
                nt(jnp.concatenate([db1, db0[BLOCK:]], axis=1), both_mask),
            ],
            axis=0,
        )
        gmat[pl.ds(0, LANES), at] = (d_decays * decays).astype(BF16)
        return carry

    each_pair(window_step, 0, 3)

    received(L_UP)
    log_next = lbuf[pl.ds(2 * BLOCK, BLOCK), :]
    tail2 = jnp.exp(log_next[BLOCK - 1 :] - log_next)
    expanded = expand(jnp.concatenate([log_next, ending(lower, tail2)], axis=0))
    lx[pl.ds(LANES, BLOCK), :] = expanded[:BLOCK]
    blast_x[pl.ds(3 * BLOCK, BLOCK), :] = expanded[BLOCK:]

    def next_step(pair, carry):
        at = lanes_of(pair)
        fall2 = jnp.exp(lx[3 * BLOCK - 1 : 3 * BLOCK, at])
        carried = weighted(wk[pl.ds(BLOCK, BLOCK), at], blast_x[pl.ds(3 * BLOCK, BLOCK), at])
        r = compact(tn(carried, v_ref[pl.ds(BLOCK, BLOCK), at]))
        r_out[:, at] = r.astype(BF16)
        t_out[:, at] = (fall2 * c1c[:, at] + r).astype(BF16)
        return carry

    each_pair(next_step)
    send(T2_DN, T3_DN, R_DN)

    each_pair(window_step, 3, PAIRS)
    block_rows(lbuf[pl.ds(BLOCK, LANES), :], 2, BLOCK)

    received(Q_UP, G_UP)

    def cross_step(pair, carry):
        at = lanes_of(pair)
        queries = phi(qn[:, at], coef_ref[:, at]).astype(BF16)
        grads = gn[:, at]
        logs = lx[pl.ds(LANES, BLOCK), at]
        held = causal[:BLOCK]
        decays = jnp.exp(jnp.where(held, logs - lrow[2:3, at], NEVER))
        dq, dv, dk, db = tile(
            diagonal(wk[pl.ds(BLOCK, BLOCK), at]), diagonal(v_ref[pl.ds(BLOCK, BLOCK), at]),
            queries, grads, nn(decays.astype(BF16), prev_mask),
        )
        dqn_out[:, at] = dq.astype(BF16)
        raw = qn[:, at].astype(F32)
        coef_sum[1:2, at] = jnp.sum(dq * (0.125 * raw * raw), axis=0, keepdims=True)
        dvf[pl.ds(BLOCK, BLOCK), at] = dvf[pl.ds(BLOCK, BLOCK), at] + dv
        dwk[pl.ds(BLOCK, BLOCK), at] = dwk[pl.ds(BLOCK, BLOCK), at] + dk
        gmat[pl.ds(LANES, BLOCK), at] = (nt(db, prev_mask) * decays).astype(BF16)
        c1c[:, at] = compact(tn(queries, weighted(grads, jnp.exp(logs))))
        return carry

    each_pair(cross_step)
    send(DQ_DN)

    def decay_grad(block):
        later = nn(upper_in, gmat[pl.ds(block * BLOCK, BLOCK), :])
        lanes = iota((BLOCK, WIDTH), 1) % BLOCK
        kept = jnp.where(lanes < iota((BLOCK, WIDTH), 0), later, 0.0)
        return nt(kept.astype(BF16), spread)

    received(TOT1, S_UP, TOT2, SS2_UP, SS3_UP, TOT3)
    falls = expand(jnp.concatenate([tot_in[slot] for slot in range(3)], axis=0))
    falls = [falls[8 * slot : 8 * slot + 8] for slot in range(3)]
    next1_fall1 = jnp.exp(falls[0][1:2])
    next2_all = jnp.exp(falls[1][0:1] + falls[1][1:2])
    prev1_fall1 = jnp.exp(falls[2][1:2])
    prev1_all = jnp.exp(falls[2][0:1] + falls[2][1:2])
    prev2_fall1 = jnp.exp(falls[1][1:2])
    own0 = jnp.exp(lx[BLOCK - 1 : BLOCK, :])
    own1 = jnp.exp(lx[LANES - 1 : LANES, :])
    next0 = jnp.exp(lx[3 * BLOCK - 1 :, :])
    z_grad = s1_in[...].astype(F32) + next1_fall1 * (
        ss_in[0].astype(F32) + next2_all * ss_in[1].astype(F32)
    )
    z_end[...] = z_grad.astype(BF16)
    end_grad = next0 * z_grad + c1c[...]
    mid_grad = own1 * end_grad + s1c[...]
    n_end[...] = end_grad.astype(BF16)
    n_mid[...] = mid_grad.astype(BF16)

    def enter(index, keys, d_role, at):
        weights = blast_x[pl.ds(index * BLOCK, BLOCK), at]
        own_keys = keys.astype(F32)
        xmat[pl.ds(index * BLOCK, BLOCK), at] = (d_role * own_keys).astype(BF16)
        return (own_keys * weights).astype(BF16), d_role * weights

    def outer_step(pair, carry):
        at = lanes_of(pair)
        rows = pl.ds(BLOCK, BLOCK)
        grads = diagonal(z_end[:, at])
        carried, d_keys = enter(3, wk[rows, at], nt(v_ref[rows, at], grads), at)
        dwk[rows, at] = dwk[rows, at] + d_keys
        dvf[rows, at] = dvf[rows, at] + nn(carried, grads)
        return carry

    each_pair(outer_step)
    d_last = nt(xmat[pl.ds(3 * BLOCK, BLOCK), :], spread)
    dan_out[...] = decay_grad(2) + twice(lower, twice(after, d_last) * tail2)
    send(DA_DN)

    def inner_step(pair, carry):
        at = lanes_of(pair)
        keys, values = wk[:, at], v_ref[:, at]
        grads_end = diagonal(n_end[:, at])
        both = jnp.concatenate([diagonal(n_mid[:, at]), grads_end], axis=0)
        d_first = nt(values[:BLOCK], both)
        carried0, d_keys0 = enter(0, keys[:BLOCK], d_first[:, :LANES], at)
        carried1, d_keys1 = enter(1, keys[:BLOCK], d_first[:, LANES:], at)
        carried2, d_keys2 = enter(2, keys[BLOCK:], nt(values[BLOCK:], grads_end), at)
        dv_ref[pl.ds(0, BLOCK), at] = (
            dvf[pl.ds(0, BLOCK), at] + nn(jnp.concatenate([carried0, carried1], axis=1), both)
        ).astype(BF16)
        dv_ref[pl.ds(BLOCK, BLOCK), at] = (
            dvf[pl.ds(BLOCK, BLOCK), at] + nn(carried2, grads_end)
        ).astype(BF16)
        d_keys = dwk[:, at] + jnp.concatenate([d_keys0 + d_keys1, d_keys2], axis=0)
        coef = coef_ref[:, at]
        raw = k_ref[:, at].astype(F32)
        d_feat = d_keys * gamma_x[:, at]
        square = 0.125 * raw * raw
        xmat[pl.ds(6 * BLOCK, LANES), at] = (d_keys * (0.125 * raw + coef * square)).astype(BF16)
        dk_ref[:, at] = (d_feat * (0.125 + (0.25 * coef) * raw)).astype(BF16)
        coef_sum[0:1, at] = jnp.sum(d_feat * square, axis=0, keepdims=True)
        return carry

    each_pair(inner_step)
    stores[1].start()
    stores[2].start()
    d_enter = nt(xmat[pl.ds(0, 3 * BLOCK), :], spread)
    d_gamma = nt(xmat[pl.ds(6 * BLOCK, LANES), :], spread_gate)
    d_decay0 = decay_grad(0) + twice(lower, twice(at_or_before, d_enter[:BLOCK]) * tail0)
    entered = nn(
        jnp.concatenate([at_or_before, at_or_before, after, after], axis=1),
        jnp.concatenate(pieces(d_enter[2 * BLOCK :], 2) + pieces(d_enter[BLOCK : 2 * BLOCK], 2), axis=0),
    )
    d_decay1 = decay_grad(1) + twice(lower, entered * tail1)

    received(P_DN, R_DN, T2_DN, T3_DN)
    memory = (
        p_in[...].astype(F32)
        + prev1_fall1 * t_in[0].astype(F32)
        + (prev2_fall1 * prev1_all) * t_in[1].astype(F32)
    )
    middle_memory = own0 * memory + r_in[...].astype(F32) + u0c[...]
    m_in[...] = memory.astype(BF16)
    m_mid[...] = middle_memory.astype(BF16)
    fall_grad = jnp.concatenate(
        [
            own0 * jnp.sum(memory * mid_grad, axis=0, keepdims=True),
            own1 * jnp.sum(middle_memory * end_grad, axis=0, keepdims=True),
            jnp.zeros((6, WIDTH), F32),
        ],
        axis=0,
    )
    fall_grad = sum(nt(part, spread) for part in pieces(fall_grad, 2))

    def query_step(pair, carry):
        at = lanes_of(pair)
        scaled = gq[:, at]
        carried = jnp.concatenate(
            [
                nt(scaled[:BLOCK], diagonal(m_in[:, at])),
                nt(scaled[BLOCK:], diagonal(m_mid[:, at])),
            ],
            axis=0,
        )
        xmat[pl.ds(4 * BLOCK, LANES), at] = (
            carried * qf[pl.ds(0, LANES), at].astype(F32)
        ).astype(BF16)
        raw = q_ref[:, at].astype(F32)
        d_feat = dqf[:, at] + carried
        dqf[:, at] = d_feat
        coef_sum[0:1, at] = (
            coef_sum[0:1, at]
            + coef_sum[1:2, at]
            + jnp.sum(d_feat * (0.125 * raw * raw), axis=0, keepdims=True)
        )
        return carry

    each_pair(query_step)
    d_out = nt(xmat[pl.ds(4 * BLOCK, LANES), :], spread)
    received(DA_DN)
    d_decay = jnp.concatenate(
        [
            d_decay0 + dan_in[...] + twice(upper_in, d_out[:BLOCK]) + fall_grad[0:1],
            d_decay1 + twice(upper_in, d_out[BLOCK:]) + fall_grad[1:2],
        ],
        axis=0,
    )
    is_decay = iota((LANES, LANES), 1) < HEADS
    d_logits = jnp.where(is_decay, -rate * sig * d_decay, d_gamma * gamma * (1.0 - sig))
    rates = jnp.sum(jnp.where(is_decay, -soft * d_decay, 0.0), axis=0, keepdims=True)
    gate = nn(jnp.concatenate(pieces(d_logits.T[:32], 2), axis=0), x)
    gate = gate[:32] + gate[32:]

    def paired(rows):
        high = rows.astype(BF16).astype(F32)
        return jnp.concatenate([high, rows - high], axis=0).astype(BF16)

    no_rates = jnp.zeros((1, LANES), F32)
    for chunk in range(8):
        at = slice(chunk * LANES, (chunk + 1) * LANES)
        mine[chunk, 0:32, :] = gate[:32, at].astype(BF16)
        mine[chunk, 32:TALL, :] = paired(
            jnp.concatenate(
                [
                    coef_sum[0:1, at],
                    rates if chunk == 0 else no_rates,
                    jnp.zeros((6, LANES), F32),
                ],
                axis=0,
            )
        )

    def exchange(base, size, where, source, target, reach=1):
        made = [
            pltpu.make_async_remote_copy(
                src_ref=source(hop),
                dst_ref=target,
                send_sem=sum_send.at[base + hop],
                recv_sem=sum_recv.at[base + hop],
                device_id=where(hop),
                device_id_type=MESH,
            )
            for hop in sorted(range(1, size), key=lambda hop: -min(hop // reach, (size - hop) // reach))
        ]
        for one in made:
            one.start()
        return made

    def added(buffer, count):
        total = buffer[0].astype(F32)
        for index in range(1, count):
            total = total + buffer[index].astype(F32)
        return jnp.concatenate(
            [total[:32].astype(BF16), paired(total[32:40] + total[40:])], axis=0
        )

    made = exchange(0, 8, octet, lambda hop: mine.at[lax.rem(eight + hop, 8)], first.at[eight], 2)
    first[eight] = mine[eight]
    d_hi, d_lo = [part[:, :32] for part in pieces(d_logits, 2)]
    dx_ref[...] = nn(
        jnp.concatenate([d_hi, d_lo, d_hi, jnp.zeros((LANES, 32), BF16)], axis=1),
        jnp.concatenate([w_hi, w_hi, w_lo, no_rows], axis=0),
    ).astype(BF16)
    stores[3].start()
    received(DQ_DN)

    def last_step(pair, carry):
        at = lanes_of(pair)
        raw = q_ref[:, at].astype(F32)
        d_feat = dqf[:, at] + jnp.concatenate(
            [dqn_in[:, at].astype(F32), jnp.zeros((BLOCK, LANES), F32)], axis=0
        )
        dq_ref[:, at] = (d_feat * (0.125 + (0.25 * coef_ref[:, at]) * raw)).astype(BF16)
        return carry

    each_pair(last_step)
    stores[0].start()
    for one in made:
        one.wait_recv()
    second[y] = added(first, 8)
    more = exchange(8, y_size, along_y, lambda hop: second.at[y], second.at[y])
    for one in more:
        one.wait_recv()
    made += more
    third[z] = added(second, y_size)
    more = exchange(8 + y_size, z_size, along_z, lambda hop: third.at[z], third.at[z])
    for one in more:
        one.wait_recv()
    made += more
    done[...] = added(third, z_size)
    own = pltpu.make_async_copy(done, done_hbm.at[eight], store_sem.at[4])
    own.start()
    more = exchange(
        8 + y_size + z_size, 8, octet, lambda hop: done, done_hbm.at[eight], 2
    )
    for message in range(MESSAGES):
        sent(message)
    for store in stores:
        store.wait()
    own.wait()
    for one in made:
        one.wait_send()
    for one in more:
        one.wait()


def main_call(sizes, queries, keys, values, inputs, gate, coef, rate, cotangent):
    z_size, y_size = sizes
    rows = queries.shape[0]
    anywhere = pl.BlockSpec(memory_space=pltpu.HBM)
    block, full = (BLOCK, WIDTH), (LANES, WIDTH)
    out = jax.ShapeDtypeStruct((rows, WIDTH), BF16)
    tile = (TALL, LANES)
    scratch = [
        (full, BF16), (full, BF16), (full, BF16), (full, BF16), (full, BF16),
        (gate.shape, F32), (coef.shape, F32), (rate.shape, F32),
        (full, BF16), (full, BF16), (full, BF16), (full, BF16),
        (block, BF16), (block, BF16), ((3 * BLOCK, LANES), F32), ((8, LANES), F32), ((3, 8, LANES), F32),
        (block, BF16), (block, BF16), (block, BF16), ((2,) + block, BF16),
        (block, BF16), (block, BF16), (block, BF16), (block, BF16), (block, BF16), ((2,) + block, BF16),
        (block, BF16), (block, BF16), ((BLOCK, LANES), F32), ((BLOCK, LANES), F32),
        ((8, WIDTH), F32), ((3 * BLOCK, WIDTH), F32), (full, F32), ((4 * BLOCK, WIDTH), F32),
        (full, BF16), (full, BF16), (full, BF16),
        (block, F32), (block, F32), (block, F32),
        (block, BF16), (block, BF16), (block, BF16), (block, BF16), (block, BF16),
        (full, F32), (full, F32), (full, F32),
        ((3 * BLOCK, WIDTH), BF16), ((8 * BLOCK, WIDTH), BF16), ((8, WIDTH), F32),
        ((8,) + tile, BF16), ((8,) + tile, BF16), ((y_size,) + tile, BF16), ((z_size,) + tile, BF16),
        (tile, BF16),
    ]
    count = 16 + y_size + z_size
    return pl.pallas_call(
        functools.partial(main_kernel, z_size, y_size),
        out_shape=[out, out, out, out, jax.ShapeDtypeStruct((8,) + tile, BF16)],
        in_specs=[anywhere] * 8,
        out_specs=[anywhere] * 5,
        scratch_shapes=[pltpu.VMEM(shape, dtype) for shape, dtype in scratch]
        + [
            pltpu.SemaphoreType.DMA((number,))
            for number in (LOADS, STORES, MESSAGES, MESSAGES, count, count)
        ],
        compiler_params=pltpu.CompilerParams(
            collective_id=0, has_side_effects=True, vmem_limit_bytes=56 * 2**20
        ),
        name="window_backward",
    )(queries, keys, values, inputs, gate, coef, rate, cotangent)


def hand_out_kernel(*refs):
    sources, targets, held = refs[:5], refs[5:12], refs[12:20]
    load_sem, store_sem = refs[20:]
    loads = [
        pltpu.make_async_copy(sources[index], held[index], load_sem.at[index]) for index in range(5)
    ]
    stores = [
        pltpu.make_async_copy(held[index if index < 4 else index + 1], targets[index], store_sem.at[index])
        for index in range(7)
    ]
    for load in loads[::-1]:
        load.start()
    done, gate, coef, rate = held[4:]
    loads[4].wait()
    for chunk in range(8):
        at = slice(chunk * LANES, (chunk + 1) * LANES)
        total = done[chunk].astype(F32)
        gate[:, at] = total[:32]
        rest = total[32:40] + total[40:]
        coef[:, at] = rest[0:1]
        if chunk == 0:
            rate[...] = rest[1:2, :HEADS]
    for store in stores[4:]:
        store.start()
    for index in range(3, -1, -1):
        loads[index].wait()
        stores[index].start()
    for store in stores:
        store.wait()


def hand_out(results):
    anywhere = pl.BlockSpec(memory_space=pltpu.HBM)
    params = [jax.ShapeDtypeStruct(shape, F32) for shape in ((32, WIDTH), (1, WIDTH), (1, HEADS))]
    shapes = [jax.ShapeDtypeStruct(a.shape, a.dtype) for a in results]
    return pl.pallas_call(
        hand_out_kernel,
        out_shape=shapes[:4] + params,
        in_specs=[anywhere] * 5,
        out_specs=[anywhere] * 7,
        scratch_shapes=[pltpu.VMEM(a.shape, a.dtype) for a in shapes + params]
        + [pltpu.SemaphoreType.DMA((5,)), pltpu.SemaphoreType.DMA((7,))],
        compiler_params=pltpu.CompilerParams(vmem_limit_bytes=56 * 2**20),
        name="hand_out",
    )(*results)


def on_device(sizes, queries, keys, values, inputs, gate, coef, rate, cotangent):
    results = main_call(
        sizes,
        queries[0], keys[0], values[0], inputs[0], gate.T, coef[None], rate[None], cotangent[0],
    )
    dq, dk, dv, dx, d_gate, d_coef, d_rate = hand_out(results)
    return (dq[None], dk[None], dv[None], dx[None], d_gate.T, d_coef[0], d_rate[0])


def solution(mesh):
    rows = P("dp", "seq", None)
    y_size = min(4, max(1, mesh.shape["dp"] // 2))
    sizes = (mesh.shape["dp"] // (2 * y_size), y_size)
    return jax.shard_map(
        functools.partial(on_device, sizes),
        mesh=mesh,
        in_specs=(rows, rows, rows, rows, P(), P(), P(), rows),
        out_specs=(rows, rows, rows, rows, P(), P(), P()),
        check_vma=False,
    )
```

```python
import functools

import jax
import jax.numpy as jnp
from jax import lax
from jax.experimental import pallas as pl
from jax.experimental.pallas import tpu as pltpu
from jax.sharding import PartitionSpec as P

BLOCK = 64
LANES = 128
WIDTH = 1024
PAIRS = WIDTH // LANES
HEADS = 16
F32 = jnp.float32
BF16 = jnp.bfloat16
MESH = pl.DeviceIdType.MESH


def nn(a, b):
    return lax.dot_general(a, b, (((1,), (0,)), ((), ())), preferred_element_type=F32)


def nt(a, b):
    return lax.dot_general(a, b, (((1,), (1,)), ((), ())), preferred_element_type=F32)


def tn(a, b):
    return lax.dot_general(a, b, (((0,), (0,)), ((), ())), preferred_element_type=F32)


def pieces(a, count):
    parts = []
    for _ in range(count):
        part = a.astype(BF16)
        parts.append(part)
        a = a - part.astype(F32)
    return parts


def flag(condition):
    return jnp.where(condition, 1.0, 0.0).astype(BF16)


def iota(shape, dimension):
    return lax.broadcasted_iota(jnp.int32, shape, dimension)


Q_UP, G_UP, L_UP, S_UP, SS1_UP, SS2_UP, SS3_UP, TOT1, TOT2, TOT3 = range(10)
P_DN, R_DN, T2_DN, T3_DN, DQ_DN, DA_DN = range(10, 16)
MESSAGES = 16
LOADS = 8
STORES = 5
TALL = 48
NEVER = -1e30


def main_kernel(
    z_size, y_size,
    q_hbm, k_hbm, v_hbm, x_hbm, w_hbm, coef_hbm, rate_hbm, g_hbm,
    dq_hbm, dk_hbm, dv_hbm, dx_hbm, done_hbm,
    q_ref, k_ref, v_ref, x_ref, g_ref, w_ref, coef_ref, rate_ref,
    dq_ref, dk_ref, dv_ref, dx_ref,
    qn, gn, lbuf, tot, tot_in, s1_out, ss_out, s1_in, ss_held, ss_in, p_out, r_out, t_out, p_in, r_in, t_in,
    dqn_out, dqn_in, dan_out, dan_in,
    lrow, lx, gamma_x, blast_x, qf, wk, gq, s1c, u0c, c1c, m_in, m_mid, n_mid, n_end, z_end,
    dqf, dwk, dvf, gmat, xmat, coef_sum,
    mine, first, second, third, done,
    load_sem, store_sem, send_sem, recv_sem, sum_send, sum_recv, ring_sem,
):
    place, dp = lax.axis_index("seq"), lax.axis_index("dp")
    z, y, core = dp // (y_size * 2), (dp // 2) % y_size, dp % 2
    last = 3

    loads = [
        pltpu.make_async_copy(source, target, load_sem.at[index])
        for index, (source, target) in enumerate(
            (
                (x_hbm, x_ref), (w_hbm, w_ref), (rate_hbm, rate_ref), (coef_hbm, coef_ref),
                (k_hbm, k_ref), (q_hbm, q_ref), (v_hbm, v_ref), (g_hbm, g_ref),
            )
        )
    ]
    for load in loads:
        load.start()
    stores = [
        pltpu.make_async_copy(source, target, store_sem.at[index])
        for index, (source, target) in enumerate(
            ((dq_ref, dq_hbm), (dk_ref, dk_hbm), (dv_ref, dv_hbm), (dx_ref, dx_hbm))
        )
    ]

    def copy(source, target, message, to):
        return pltpu.make_async_remote_copy(
            src_ref=source,
            dst_ref=target,
            send_sem=send_sem.at[message],
            recv_sem=recv_sem.at[message],
            device_id={"seq": to},
            device_id_type=MESH,
        )

    up1, up2, up3 = place - 1, place - 2, place - 3
    dn1, dn2, dn3 = place + 1, place + 2, place + 3
    around = [lax.rem(place + 4 - hop, 4) for hop in (1, 2, 3)]
    always = place >= 0
    later, earlier = place >= 1, place < last
    messages = {
        Q_UP: (copy(q_ref.at[pl.ds(0, BLOCK)], qn, Q_UP, up1), later, earlier),
        G_UP: (copy(g_ref.at[pl.ds(0, BLOCK)], gn, G_UP, up1), later, earlier),
        L_UP: (
            copy(lbuf.at[pl.ds(0, BLOCK)], lbuf.at[pl.ds(2 * BLOCK, BLOCK)], L_UP, up1), later, earlier
        ),
        S_UP: (copy(s1_out, s1_in, S_UP, up1), later, earlier),
        SS1_UP: (copy(ss_out, ss_held, SS1_UP, up1), place == 3, place == 2),
        SS2_UP: (copy(ss_out, ss_in.at[0], SS2_UP, up2), place == 2, place == 0),
        SS3_UP: (copy(ss_out, ss_in.at[1], SS3_UP, up3), place == 3, place == 0),
        TOT1: (copy(tot, tot_in.at[0], TOT1, around[0]), always, always),
        TOT2: (copy(tot, tot_in.at[1], TOT2, around[1]), always, always),
        TOT3: (copy(tot, tot_in.at[2], TOT3, around[2]), always, always),
        P_DN: (copy(p_out, p_in, P_DN, dn1), earlier, later),
        R_DN: (copy(r_out, r_in, R_DN, dn1), earlier, later),
        T2_DN: (copy(t_out, t_in.at[0], T2_DN, dn2), place == 1, place == 3),
        T3_DN: (copy(t_out, t_in.at[1], T3_DN, dn3), place == 0, place == 3),
        DQ_DN: (copy(dqn_out, dqn_in, DQ_DN, dn1), earlier, later),
        DA_DN: (copy(dan_out, dan_in, DA_DN, dn1), earlier, later),
    }

    def send(*which, places=always):
        for message in which:
            description, senders, _ = messages[message]
            pl.when(senders & places)(description.start)

    def sent(message):
        description, senders, _ = messages[message]
        pl.when(senders)(description.wait_send)

    def received(*which, places=always):
        for message in which:
            description, _, getters = messages[message]
            pl.when(getters & places)(description.wait_recv)

    eight = place * 2 + core

    def octet(hop):
        other = lax.rem(eight + hop, 8)
        return {"dp": (z * y_size + y) * 2 + other % 2, "seq": other // 2}

    def along_y(hop):
        return {"dp": (z * y_size + lax.rem(y + hop, y_size)) * 2 + core, "seq": place}

    def along_z(hop):
        return {"dp": (lax.rem(z + hop, z_size) * y_size + y) * 2 + core, "seq": place}

    barrier = pltpu.get_barrier_semaphore()
    partners = 0
    ring = z_size == 8
    near = (1, z_size - 1) if ring else range(1, z_size)
    for where, hops in ((octet, range(1, 8)), (along_y, range(1, y_size)), (along_z, near)):
        for hop in hops:
            pl.semaphore_signal(barrier, inc=1, device_id=where(hop), device_id_type=MESH)
            partners += 1

    def tell(index, hop):
        if ring:
            pl.semaphore_signal(ring_sem.at[index], inc=1, device_id=along_z(hop), device_id_type=MESH)

    def told(index):
        if ring:
            pl.semaphore_wait(ring_sem.at[index], 1)

    @pl.when(place == last)
    def _():
        qn[...] = jnp.zeros_like(qn)
        gn[...] = jnp.zeros_like(gn)
        lbuf[pl.ds(2 * BLOCK, BLOCK), :] = jnp.zeros((BLOCK, LANES), F32)
        s1_in[...] = jnp.zeros_like(s1_in)

    @pl.when(place != 0)
    def _():
        ss_in[...] = jnp.zeros_like(ss_in)

    @pl.when(place != last)
    def _():
        t_in[...] = jnp.zeros_like(t_in)

    @pl.when(place == 0)
    def _():
        p_in[...] = jnp.zeros_like(p_in)
        r_in[...] = jnp.zeros_like(r_in)
        dqn_in[...] = jnp.zeros_like(dqn_in)
        dan_in[...] = jnp.zeros_like(dan_in)

    row, col = iota((LANES, LANES), 0), iota((LANES, LANES), 1)
    same = (row // BLOCK) == (col // BLOCK)
    tri = flag(same & (col <= row))
    head_row = iota((LANES, WIDTH), 0)
    head_lane = iota((LANES, WIDTH), 1) // BLOCK
    spread = flag(head_row == head_lane)
    spread_gate = flag(head_row == head_lane + HEADS)
    spread_pieces = flag(head_row % 32 == head_lane)
    head_lanes = iota((BLOCK, LANES), 1) < HEADS
    left = iota((BLOCK, LANES), 1) < BLOCK
    left1 = iota((1, LANES), 1) < BLOCK
    srow, scol = iota((BLOCK, BLOCK), 0), iota((BLOCK, BLOCK), 1)
    upper_in = flag(scol >= srow)
    lower = flag(scol < srow)
    at_or_before = flag(scol <= srow)
    after = flag(scol > srow)

    loads[0].wait()
    loads[1].wait()
    loads[2].wait()
    w_hi, w_lo = pieces(w_ref[...], 2)
    no_rows = jnp.zeros((32, WIDTH), BF16)
    x = x_ref[...]
    logits = nt(x, jnp.concatenate([w_hi, no_rows, w_lo, no_rows], axis=0))
    logits = logits + jnp.concatenate([logits[:, BLOCK:], logits[:, :BLOCK]], axis=1)
    small = jnp.exp(-jnp.abs(logits))
    soft = jnp.maximum(logits, 0.0) + jnp.log1p(small)
    sig = jnp.where(logits >= 0.0, 1.0, small) / (1.0 + small)
    rate = jnp.concatenate([rate_ref[...], jnp.zeros((1, LANES - HEADS), F32)], axis=1)
    decay = -rate * soft
    gamma = sig * (1.0 / BLOCK)
    log_own = sum(nn(tri, part) for part in pieces(decay, 3))
    lbuf[pl.ds(0, LANES), :] = log_own
    tot[...] = jnp.zeros_like(tot)
    tot[0:1, :] = log_own[BLOCK - 1 : BLOCK]
    tot[1:2, :] = log_own[LANES - 1 :]

    for load in loads[3:]:
        load.wait()
    pl.semaphore_wait(barrier, partners)
    send(L_UP, TOT1, TOT2, TOT3)
    send(Q_UP, G_UP, places=place < last)
    tell(0, 1)
    tell(1, z_size - 1)

    def beside(a):
        parts = [part[:, :32] for part in pieces(a, 3)]
        return jnp.concatenate(parts + [jnp.zeros((a.shape[0], 32), BF16)], axis=1)

    def expand(a):
        return nn(beside(a), spread_pieces)

    def block_rows(logs, block, offset):
        pick = flag(row == (col % BLOCK) + offset)
        turned = sum(tn(part, pick) for part in pieces(logs, 3))
        for pair in range(PAIRS):
            lrow[block : block + 1, pl.ds(pair * LANES, LANES)] = jnp.where(
                left1, turned[2 * pair : 2 * pair + 1], turned[2 * pair + 1 : 2 * pair + 2]
            )

    tail0 = jnp.exp(log_own[BLOCK - 1 : BLOCK] - log_own[:BLOCK])
    tail1 = jnp.exp(log_own[LANES - 1 :] - log_own[BLOCK:])

    def twice(mask, a):
        return nn(
            jnp.concatenate([mask, mask], axis=1), jnp.concatenate(pieces(a, 2), axis=0)
        )

    def ending(mask, tail):
        return jnp.where(head_lanes, twice(mask, tail), 0.0)

    gamma_first = jnp.concatenate([gamma[:, HEADS:32], jnp.zeros((LANES, LANES - HEADS), F32)], axis=1)
    expanded = expand(
        jnp.concatenate(
            [log_own, gamma_first, ending(upper_in, tail0), ending(lower, tail1), ending(upper_in, tail1)],
            axis=0,
        )
    )
    lx[pl.ds(0, LANES), :] = expanded[:LANES]
    gamma_x[...] = expanded[LANES : 2 * LANES]
    blast_x[pl.ds(0, 3 * BLOCK), :] = expanded[2 * LANES :]

    def each_pair(step, begin=0, end=PAIRS):
        lax.fori_loop(begin, end, step, 0, unroll=end - begin)

    def lanes_of(pair):
        return pl.ds(pl.multiple_of(pair * LANES, LANES), LANES)

    def phi(raw, coef):
        value = raw.astype(F32)
        return 0.125 * (value + coef * value * value)

    def compact(full):
        return jnp.where(left, full[:BLOCK], full[BLOCK:])

    def diagonal(value):
        none = jnp.zeros_like(value)
        return jnp.concatenate([jnp.where(left, value, none), jnp.where(left, none, value)], axis=0)

    def weighted(a, weights):
        return (a.astype(F32) * weights).astype(BF16)

    def own_step(pair, carry):
        at = lanes_of(pair)
        coef = coef_ref[:, at]
        q_feat = phi(q_ref[:, at], coef).astype(BF16)
        qf[pl.ds(0, LANES), at] = q_feat
        keys = (phi(k_ref[:, at], coef) * gamma_x[:, at]).astype(BF16)
        wk[:, at] = keys
        logs = lx[pl.ds(0, LANES), at]
        scaled = weighted(g_ref[:, at], jnp.exp(logs))
        gq[:, at] = scaled
        s0 = compact(tn(q_feat[:BLOCK], scaled[:BLOCK]))
        s1 = compact(tn(q_feat[BLOCK:], scaled[BLOCK:]))
        fall0 = jnp.exp(logs[BLOCK - 1 : BLOCK])
        fall1 = jnp.exp(logs[LANES - 1 :])
        s1_out[:, at] = s1.astype(BF16)
        ss_out[:, at] = (s0 + fall0 * s1).astype(BF16)
        values = v_ref[:, at]
        weights = blast_x[pl.ds(0, 3 * BLOCK), at]
        carried0 = weighted(keys[:BLOCK], weights[:BLOCK])
        carried1 = weighted(keys, weights[BLOCK:])
        u0 = compact(tn(carried0, values[:BLOCK]))
        c1 = fall1 * u0 + compact(tn(carried1, values))
        u0c[:, at] = u0
        c1c[:, at] = c1
        s1c[:, at] = s1
        p_out[:, at] = c1.astype(BF16)
        return carry

    each_pair(own_step)
    send(SS1_UP, SS2_UP, SS3_UP)
    send(Q_UP, G_UP, places=place == last)
    send(S_UP, places=place != 2)
    send(P_DN, places=place != 1)

    block_rows(log_own, 0, 0)
    block_rows(log_own, 1, BLOCK)

    step = col % BLOCK
    cur_mask = flag(same & (row % BLOCK >= step))
    prev_mask = flag(same & (row % BLOCK < step))
    both_mask = jnp.concatenate([cur_mask, prev_mask], axis=1)
    causal = (iota((LANES, LANES), 1) % BLOCK) <= (iota((LANES, LANES), 0) % BLOCK)

    def spans(rows):
        return pl.ds(rows.start, rows.stop - rows.start)

    first_rows, last_rows = slice(0, BLOCK), slice(BLOCK, LANES)

    def tile(keys_bd, values_bd, queries, grads, kernel):
        scores = nt(queries, keys_bd)
        d_weights = nt(grads, values_bd)
        weights = (scores * kernel).astype(BF16)
        d_scores = (d_weights * kernel).astype(BF16)
        d_kernel = (d_weights * scores).astype(BF16)
        return (
            nn(d_scores, keys_bd),
            compact(tn(weights, grads)),
            compact(tn(d_scores, queries)),
            d_kernel,
        )

    def window_step(pair, carry):
        at = lanes_of(pair)
        keys, values = wk[:, at], v_ref[:, at]
        queries, grads = qf[pl.ds(0, LANES), at], g_ref[:, at]
        rows = jnp.concatenate(
            [jnp.broadcast_to(lrow[b : b + 1, at], (BLOCK, LANES)) for b in range(2)], axis=0
        )
        decays = jnp.exp(jnp.where(causal, lx[pl.ds(0, LANES), at] - rows, NEVER))
        low = decays.astype(BF16)
        start = nn(low[:BLOCK], cur_mask)
        middle = nn(low[BLOCK:], both_mask)
        dq0, dv0, dk0, db0 = tile(
            diagonal(keys[:BLOCK]), diagonal(values[:BLOCK]), queries, grads,
            jnp.concatenate([start, middle[:, LANES:]], axis=0),
        )
        dq1, dv1, dk1, db1 = tile(
            diagonal(keys[BLOCK:]), diagonal(values[BLOCK:]), queries[BLOCK:], grads[BLOCK:],
            middle[:, :LANES],
        )
        dvf[pl.ds(0, BLOCK), at] = dv0
        dvf[pl.ds(BLOCK, BLOCK), at] = dv1
        dwk[pl.ds(0, BLOCK), at] = dk0
        dwk[pl.ds(BLOCK, BLOCK), at] = dk1
        dqf[pl.ds(0, BLOCK), at] = dq0[:BLOCK]
        dqf[pl.ds(BLOCK, BLOCK), at] = dq0[BLOCK:] + dq1
        d_decays = jnp.concatenate(
            [
                nt(db0[:BLOCK], cur_mask),
                nt(jnp.concatenate([db1, db0[BLOCK:]], axis=1), both_mask),
            ],
            axis=0,
        )
        gmat[pl.ds(0, LANES), at] = (d_decays * decays).astype(BF16)
        return carry

    each_pair(window_step, 0, 3)

    received(L_UP)
    log_next = lbuf[pl.ds(2 * BLOCK, BLOCK), :]
    tail2 = jnp.exp(log_next[BLOCK - 1 :] - log_next)
    expanded = expand(jnp.concatenate([log_next, ending(lower, tail2)], axis=0))
    lx[pl.ds(LANES, BLOCK), :] = expanded[:BLOCK]
    blast_x[pl.ds(3 * BLOCK, BLOCK), :] = expanded[BLOCK:]

    def next_step(pair, carry):
        at = lanes_of(pair)
        fall2 = jnp.exp(lx[3 * BLOCK - 1 : 3 * BLOCK, at])
        carried = weighted(wk[pl.ds(BLOCK, BLOCK), at], blast_x[pl.ds(3 * BLOCK, BLOCK), at])
        r = compact(tn(carried, v_ref[pl.ds(BLOCK, BLOCK), at]))
        r_out[:, at] = r.astype(BF16)
        t_out[:, at] = (fall2 * c1c[:, at] + r).astype(BF16)
        return carry

    each_pair(next_step)
    send(T2_DN, T3_DN, R_DN)

    told(0)
    told(1)
    tell(2, 1)
    tell(3, z_size - 1)
    each_pair(window_step, 3, PAIRS)
    told(2)
    told(3)
    tell(4, 1)
    own0 = jnp.exp(lx[BLOCK - 1 : BLOCK, :])
    own1 = jnp.exp(lx[LANES - 1 : LANES, :])

    @pl.when(place == 2)
    def _():
        messages[SS1_UP][0].wait_recv()
        s1_out[...] = (s1c[...] + own1 * ss_held[...].astype(F32)).astype(BF16)
        messages[S_UP][0].start()

    @pl.when(place == 1)
    def _():
        messages[P_DN][0].wait_recv()
        messages[R_DN][0].wait_recv()
        entered = own0 * p_in[...].astype(F32) + r_in[...].astype(F32)
        p_out[...] = (c1c[...] + own1 * entered).astype(BF16)
        messages[P_DN][0].start()

    block_rows(lbuf[pl.ds(BLOCK, LANES), :], 2, BLOCK)

    received(Q_UP, G_UP)

    def cross_step(pair, carry):
        at = lanes_of(pair)
        queries = phi(qn[:, at], coef_ref[:, at]).astype(BF16)
        grads = gn[:, at]
        logs = lx[pl.ds(LANES, BLOCK), at]
        held = causal[:BLOCK]
        decays = jnp.exp(jnp.where(held, logs - lrow[2:3, at], NEVER))
        dq, dv, dk, db = tile(
            diagonal(wk[pl.ds(BLOCK, BLOCK), at]), diagonal(v_ref[pl.ds(BLOCK, BLOCK), at]),
            queries, grads, nn(decays.astype(BF16), prev_mask),
        )
        dqn_out[:, at] = dq.astype(BF16)
        raw = qn[:, at].astype(F32)
        coef_sum[1:2, at] = jnp.sum(dq * (0.125 * raw * raw), axis=0, keepdims=True)
        dvf[pl.ds(BLOCK, BLOCK), at] = dvf[pl.ds(BLOCK, BLOCK), at] + dv
        dwk[pl.ds(BLOCK, BLOCK), at] = dwk[pl.ds(BLOCK, BLOCK), at] + dk
        gmat[pl.ds(LANES, BLOCK), at] = (nt(db, prev_mask) * decays).astype(BF16)
        c1c[:, at] = compact(tn(queries, weighted(grads, jnp.exp(logs))))
        return carry

    each_pair(cross_step)
    send(DQ_DN)

    def decay_grad(block):
        later = nn(upper_in, gmat[pl.ds(block * BLOCK, BLOCK), :])
        lanes = iota((BLOCK, WIDTH), 1) % BLOCK
        kept = jnp.where(lanes < iota((BLOCK, WIDTH), 0), later, 0.0)
        return nt(kept.astype(BF16), spread)

    received(TOT1, S_UP, TOT2, SS2_UP, SS3_UP, TOT3)
    falls = expand(jnp.concatenate([tot_in[slot] for slot in range(3)], axis=0))
    falls = [falls[8 * slot : 8 * slot + 8] for slot in range(3)]
    next1_fall1 = jnp.exp(falls[0][1:2])
    next2_all = jnp.exp(falls[1][0:1] + falls[1][1:2])
    prev1_fall1 = jnp.exp(falls[2][1:2])
    prev1_all = jnp.exp(falls[2][0:1] + falls[2][1:2])
    prev2_fall1 = jnp.exp(falls[1][1:2])
    next0 = jnp.exp(lx[3 * BLOCK - 1 :, :])
    z_grad = s1_in[...].astype(F32) + next1_fall1 * (
        ss_in[0].astype(F32) + next2_all * ss_in[1].astype(F32)
    )
    z_end[...] = z_grad.astype(BF16)
    end_grad = next0 * z_grad + c1c[...]
    mid_grad = own1 * end_grad + s1c[...]
    n_end[...] = end_grad.astype(BF16)
    n_mid[...] = mid_grad.astype(BF16)

    def enter(index, keys, d_role, at):
        weights = blast_x[pl.ds(index * BLOCK, BLOCK), at]
        own_keys = keys.astype(F32)
        xmat[pl.ds(index * BLOCK, BLOCK), at] = (d_role * own_keys).astype(BF16)
        return (own_keys * weights).astype(BF16), d_role * weights

    def outer_step(pair, carry):
        at = lanes_of(pair)
        rows = pl.ds(BLOCK, BLOCK)
        grads = diagonal(z_end[:, at])
        carried, d_keys = enter(3, wk[rows, at], nt(v_ref[rows, at], grads), at)
        dwk[rows, at] = dwk[rows, at] + d_keys
        dvf[rows, at] = dvf[rows, at] + nn(carried, grads)
        return carry

    each_pair(outer_step)
    d_last = nt(xmat[pl.ds(3 * BLOCK, BLOCK), :], spread)
    dan_out[...] = decay_grad(2) + twice(lower, twice(after, d_last) * tail2)
    send(DA_DN)

    def inner_step(pair, carry):
        at = lanes_of(pair)
        keys, values = wk[:, at], v_ref[:, at]
        grads_end = diagonal(n_end[:, at])
        both = jnp.concatenate([diagonal(n_mid[:, at]), grads_end], axis=0)
        d_first = nt(values[:BLOCK], both)
        carried0, d_keys0 = enter(0, keys[:BLOCK], d_first[:, :LANES], at)
        carried1, d_keys1 = enter(1, keys[:BLOCK], d_first[:, LANES:], at)
        carried2, d_keys2 = enter(2, keys[BLOCK:], nt(values[BLOCK:], grads_end), at)
        dv_ref[pl.ds(0, BLOCK), at] = (
            dvf[pl.ds(0, BLOCK), at] + nn(jnp.concatenate([carried0, carried1], axis=1), both)
        ).astype(BF16)
        dv_ref[pl.ds(BLOCK, BLOCK), at] = (
            dvf[pl.ds(BLOCK, BLOCK), at] + nn(carried2, grads_end)
        ).astype(BF16)
        d_keys = dwk[:, at] + jnp.concatenate([d_keys0 + d_keys1, d_keys2], axis=0)
        coef = coef_ref[:, at]
        raw = k_ref[:, at].astype(F32)
        d_feat = d_keys * gamma_x[:, at]
        square = 0.125 * raw * raw
        xmat[pl.ds(6 * BLOCK, LANES), at] = (d_keys * (0.125 * raw + coef * square)).astype(BF16)
        dk_ref[:, at] = (d_feat * (0.125 + (0.25 * coef) * raw)).astype(BF16)
        coef_sum[0:1, at] = jnp.sum(d_feat * square, axis=0, keepdims=True)
        return carry

    each_pair(inner_step)
    stores[1].start()
    stores[2].start()
    d_enter = nt(xmat[pl.ds(0, 3 * BLOCK), :], spread)
    d_gamma = nt(xmat[pl.ds(6 * BLOCK, LANES), :], spread_gate)
    d_decay0 = decay_grad(0) + twice(lower, twice(at_or_before, d_enter[:BLOCK]) * tail0)
    entered = nn(
        jnp.concatenate([at_or_before, at_or_before, after, after], axis=1),
        jnp.concatenate(pieces(d_enter[2 * BLOCK :], 2) + pieces(d_enter[BLOCK : 2 * BLOCK], 2), axis=0),
    )
    d_decay1 = decay_grad(1) + twice(lower, entered * tail1)

    received(P_DN, R_DN, places=place != 1)
    received(T2_DN, T3_DN)
    memory = (
        p_in[...].astype(F32)
        + prev1_fall1 * t_in[0].astype(F32)
        + (prev2_fall1 * prev1_all) * t_in[1].astype(F32)
    )
    middle_memory = own0 * memory + r_in[...].astype(F32) + u0c[...]
    m_in[...] = memory.astype(BF16)
    m_mid[...] = middle_memory.astype(BF16)
    fall_grad = jnp.concatenate(
        [
            own0 * jnp.sum(memory * mid_grad, axis=0, keepdims=True),
            own1 * jnp.sum(middle_memory * end_grad, axis=0, keepdims=True),
            jnp.zeros((6, WIDTH), F32),
        ],
        axis=0,
    )
    fall_grad = sum(nt(part, spread) for part in pieces(fall_grad, 2))

    def query_step(pair, carry):
        at = lanes_of(pair)
        scaled = gq[:, at]
        carried = jnp.concatenate(
            [
                nt(scaled[:BLOCK], diagonal(m_in[:, at])),
                nt(scaled[BLOCK:], diagonal(m_mid[:, at])),
            ],
            axis=0,
        )
        xmat[pl.ds(4 * BLOCK, LANES), at] = (
            carried * qf[pl.ds(0, LANES), at].astype(F32)
        ).astype(BF16)
        raw = q_ref[:, at].astype(F32)
        d_feat = dqf[:, at] + carried
        dqf[:, at] = d_feat
        coef_sum[0:1, at] = (
            coef_sum[0:1, at]
            + coef_sum[1:2, at]
            + jnp.sum(d_feat * (0.125 * raw * raw), axis=0, keepdims=True)
        )
        return carry

    each_pair(query_step)
    d_out = nt(xmat[pl.ds(4 * BLOCK, LANES), :], spread)
    received(DA_DN)
    d_decay = jnp.concatenate(
        [
            d_decay0 + dan_in[...] + twice(upper_in, d_out[:BLOCK]) + fall_grad[0:1],
            d_decay1 + twice(upper_in, d_out[BLOCK:]) + fall_grad[1:2],
        ],
        axis=0,
    )
    is_decay = iota((LANES, LANES), 1) < HEADS
    d_logits = jnp.where(is_decay, -rate * sig * d_decay, d_gamma * gamma * (1.0 - sig))
    rates = jnp.sum(jnp.where(is_decay, -soft * d_decay, 0.0), axis=0, keepdims=True)
    gate = nn(jnp.concatenate(pieces(d_logits.T[:32], 2), axis=0), x)
    gate = gate[:32] + gate[32:]

    def paired(rows):
        high = rows.astype(BF16).astype(F32)
        return jnp.concatenate([high, rows - high], axis=0).astype(BF16)

    no_rates = jnp.zeros((1, LANES), F32)
    for chunk in range(8):
        at = slice(chunk * LANES, (chunk + 1) * LANES)
        mine[chunk, 0:32, :] = gate[:32, at].astype(BF16)
        mine[chunk, 32:TALL, :] = paired(
            jnp.concatenate(
                [
                    coef_sum[0:1, at],
                    rates if chunk == 0 else no_rates,
                    jnp.zeros((6, LANES), F32),
                ],
                axis=0,
            )
        )

    def exchange(base, size, where, source, target, reach=1):
        made = [
            pltpu.make_async_remote_copy(
                src_ref=source(hop),
                dst_ref=target,
                send_sem=sum_send.at[base + hop],
                recv_sem=sum_recv.at[base + hop],
                device_id=where(hop),
                device_id_type=MESH,
            )
            for hop in sorted(range(1, size), key=lambda hop: -min(hop // reach, (size - hop) // reach))
        ]
        for one in made:
            one.start()
        return made

    def added(buffer, count):
        total = buffer[0].astype(F32)
        for index in range(1, count):
            total = total + buffer[index].astype(F32)
        return jnp.concatenate(
            [total[:32].astype(BF16), paired(total[32:40] + total[40:])], axis=0
        )

    made = exchange(0, 8, octet, lambda hop: mine.at[lax.rem(eight + hop, 8)], first.at[eight], 2)
    first[eight] = mine[eight]
    d_hi, d_lo = [part[:, :32] for part in pieces(d_logits, 2)]
    dx_ref[...] = nn(
        jnp.concatenate([d_hi, d_lo, d_hi, jnp.zeros((LANES, 32), BF16)], axis=1),
        jnp.concatenate([w_hi, w_hi, w_lo, no_rows], axis=0),
    ).astype(BF16)
    stores[3].start()
    received(DQ_DN)

    def last_step(pair, carry):
        at = lanes_of(pair)
        raw = q_ref[:, at].astype(F32)
        d_feat = dqf[:, at] + jnp.concatenate(
            [dqn_in[:, at].astype(F32), jnp.zeros((BLOCK, LANES), F32)], axis=0
        )
        dq_ref[:, at] = (d_feat * (0.125 + (0.25 * coef_ref[:, at]) * raw)).astype(BF16)
        return carry

    each_pair(last_step)
    stores[0].start()
    for one in made:
        one.wait_recv()
    second[y] = added(first, 8)
    more = exchange(8, y_size, along_y, lambda hop: second.at[y], second.at[y])
    for one in more:
        one.wait_recv()
    made += more
    third[z] = added(second, y_size)
    told(4)
    more = exchange(8 + y_size, z_size, along_z, lambda hop: third.at[z], third.at[z])
    for one in more:
        one.wait_recv()
    made += more
    done[...] = added(third, z_size)
    own = pltpu.make_async_copy(done, done_hbm.at[eight], store_sem.at[4])
    own.start()
    more = exchange(
        8 + y_size + z_size, 8, octet, lambda hop: done, done_hbm.at[eight], 2
    )
    for message in range(MESSAGES):
        sent(message)
    for store in stores:
        store.wait()
    own.wait()
    for one in made:
        one.wait_send()
    for one in more:
        one.wait()


def main_call(sizes, queries, keys, values, inputs, gate, coef, rate, cotangent):
    z_size, y_size = sizes
    rows = queries.shape[0]
    anywhere = pl.BlockSpec(memory_space=pltpu.HBM)
    block, full = (BLOCK, WIDTH), (LANES, WIDTH)
    out = jax.ShapeDtypeStruct((rows, WIDTH), BF16)
    tile = (TALL, LANES)
    scratch = [
        (full, BF16), (full, BF16), (full, BF16), (full, BF16), (full, BF16),
        (gate.shape, F32), (coef.shape, F32), (rate.shape, F32),
        (full, BF16), (full, BF16), (full, BF16), (full, BF16),
        (block, BF16), (block, BF16), ((3 * BLOCK, LANES), F32), ((8, LANES), F32), ((3, 8, LANES), F32),
        (block, BF16), (block, BF16), (block, BF16), (block, BF16), ((2,) + block, BF16),
        (block, BF16), (block, BF16), (block, BF16), (block, BF16), (block, BF16), ((2,) + block, BF16),
        (block, BF16), (block, BF16), ((BLOCK, LANES), F32), ((BLOCK, LANES), F32),
        ((8, WIDTH), F32), ((3 * BLOCK, WIDTH), F32), (full, F32), ((4 * BLOCK, WIDTH), F32),
        (full, BF16), (full, BF16), (full, BF16),
        (block, F32), (block, F32), (block, F32),
        (block, BF16), (block, BF16), (block, BF16), (block, BF16), (block, BF16),
        (full, F32), (full, F32), (full, F32),
        ((3 * BLOCK, WIDTH), BF16), ((8 * BLOCK, WIDTH), BF16), ((8, WIDTH), F32),
        ((8,) + tile, BF16), ((8,) + tile, BF16), ((y_size,) + tile, BF16), ((z_size,) + tile, BF16),
        (tile, BF16),
    ]
    count = 16 + y_size + z_size
    return pl.pallas_call(
        functools.partial(main_kernel, z_size, y_size),
        out_shape=[out, out, out, out, jax.ShapeDtypeStruct((8,) + tile, BF16)],
        in_specs=[anywhere] * 8,
        out_specs=[anywhere] * 5,
        scratch_shapes=[pltpu.VMEM(shape, dtype) for shape, dtype in scratch]
        + [
            pltpu.SemaphoreType.DMA((number,))
            for number in (LOADS, STORES, MESSAGES, MESSAGES, count, count)
        ]
        + [pltpu.SemaphoreType.REGULAR((5,))],
        compiler_params=pltpu.CompilerParams(
            collective_id=0, has_side_effects=True, vmem_limit_bytes=56 * 2**20
        ),
        name="window_backward",
    )(queries, keys, values, inputs, gate, coef, rate, cotangent)


def hand_out_kernel(*refs):
    sources, targets, held = refs[:5], refs[5:12], refs[12:20]
    load_sem, store_sem = refs[20:]
    loads = [
        pltpu.make_async_copy(sources[index], held[index], load_sem.at[index]) for index in range(5)
    ]
    stores = [
        pltpu.make_async_copy(held[index if index < 4 else index + 1], targets[index], store_sem.at[index])
        for index in range(7)
    ]
    for load in loads[::-1]:
        load.start()
    done, gate, coef, rate = held[4:]
    loads[4].wait()
    for chunk in range(8):
        at = slice(chunk * LANES, (chunk + 1) * LANES)
        total = done[chunk].astype(F32)
        gate[:, at] = total[:32]
        rest = total[32:40] + total[40:]
        coef[:, at] = rest[0:1]
        if chunk == 0:
            rate[...] = rest[1:2, :HEADS]
    for store in stores[4:]:
        store.start()
    for index in range(3, -1, -1):
        loads[index].wait()
        stores[index].start()
    for store in stores:
        store.wait()


def hand_out(results):
    anywhere = pl.BlockSpec(memory_space=pltpu.HBM)
    params = [jax.ShapeDtypeStruct(shape, F32) for shape in ((32, WIDTH), (1, WIDTH), (1, HEADS))]
    shapes = [jax.ShapeDtypeStruct(a.shape, a.dtype) for a in results]
    return pl.pallas_call(
        hand_out_kernel,
        out_shape=shapes[:4] + params,
        in_specs=[anywhere] * 5,
        out_specs=[anywhere] * 7,
        scratch_shapes=[pltpu.VMEM(a.shape, a.dtype) for a in shapes + params]
        + [pltpu.SemaphoreType.DMA((5,)), pltpu.SemaphoreType.DMA((7,))],
        compiler_params=pltpu.CompilerParams(vmem_limit_bytes=56 * 2**20),
        name="hand_out",
    )(*results)


def on_device(sizes, queries, keys, values, inputs, gate, coef, rate, cotangent):
    results = main_call(
        sizes,
        queries[0], keys[0], values[0], inputs[0], gate.T, coef[None], rate[None], cotangent[0],
    )
    dq, dk, dv, dx, d_gate, d_coef, d_rate = hand_out(results)
    return (dq[None], dk[None], dv[None], dx[None], d_gate.T, d_coef[0], d_rate[0])


def solution(mesh):
    rows = P("dp", "seq", None)
    y_size = min(4, max(1, mesh.shape["dp"] // 2))
    sizes = (mesh.shape["dp"] // (2 * y_size), y_size)
    return jax.shard_map(
        functools.partial(on_device, sizes),
        mesh=mesh,
        in_specs=(rows, rows, rows, rows, P(), P(), P(), rows),
        out_specs=(rows, rows, rows, rows, P(), P(), P()),
        check_vma=False,
    )
```

```python
import functools

import jax
import jax.numpy as jnp
from jax import lax
from jax.experimental import pallas as pl
from jax.experimental.pallas import tpu as pltpu
from jax.sharding import PartitionSpec as P

BLOCK = 64
LANES = 128
WIDTH = 1024
PAIRS = WIDTH // LANES
HEADS = 16
F32 = jnp.float32
BF16 = jnp.bfloat16
MESH = pl.DeviceIdType.MESH


def nn(a, b):
    return lax.dot_general(a, b, (((1,), (0,)), ((), ())), preferred_element_type=F32)


def nt(a, b):
    return lax.dot_general(a, b, (((1,), (1,)), ((), ())), preferred_element_type=F32)


def tn(a, b):
    return lax.dot_general(a, b, (((0,), (0,)), ((), ())), preferred_element_type=F32)


def pieces(a, count):
    parts = []
    for _ in range(count):
        part = a.astype(BF16)
        parts.append(part)
        a = a - part.astype(F32)
    return parts


def flag(condition):
    return jnp.where(condition, 1.0, 0.0).astype(BF16)


def iota(shape, dimension):
    return lax.broadcasted_iota(jnp.int32, shape, dimension)


Q_UP, G_UP, L_UP, S_UP, SS1_UP, SS2_UP, SS3_UP, TOT1, TOT2, TOT3 = range(10)
P_DN, R_DN, T2_DN, T3_DN, DQ_DN, DA_DN = range(10, 16)
MESSAGES = 16
LOADS = 8
STORES = 5
TALL = 48
NEVER = -1e30
WIDE = 8
GROUP = 4


def main_kernel(
    z_size, y_size,
    q_hbm, k_hbm, v_hbm, x_hbm, w_hbm, coef_hbm, rate_hbm, g_hbm,
    dq_hbm, dk_hbm, dv_hbm, dx_hbm, done_hbm,
    q_ref, k_ref, v_ref, x_ref, g_ref, w_ref, coef_ref, rate_ref,
    dq_ref, dk_ref, dv_ref, dx_ref,
    qn, gn, lbuf, tot, tot_in, s1_out, ss_out, s1_in, ss_held, ss_in, p_out, r_out, t_out, p_in, r_in, t_in,
    dqn_out, dqn_in, dan_out, dan_in,
    lrow, lx, gamma_x, blast_x, qf, wk, gq, s1c, u0c, c1c, m_in, m_mid, n_mid, n_end, z_end,
    dqf, dwk, dvf, gmat, xmat, coef_sum, keys_held, values_held,
    mine, first, second, third, done,
    load_sem, store_sem, send_sem, recv_sem, sum_send, sum_recv, ring_sem,
):
    place, dp = lax.axis_index("seq"), lax.axis_index("dp")
    z, y, core = dp // (y_size * 2), (dp // 2) % y_size, dp % 2
    last = 3

    loads = [
        pltpu.make_async_copy(source, target, load_sem.at[index])
        for index, (source, target) in enumerate(
            (
                (x_hbm, x_ref), (w_hbm, w_ref), (rate_hbm, rate_ref), (coef_hbm, coef_ref),
                (k_hbm, k_ref), (q_hbm, q_ref), (v_hbm, v_ref), (g_hbm, g_ref),
            )
        )
    ]
    for load in loads:
        load.start()
    stores = [
        pltpu.make_async_copy(source, target, store_sem.at[index])
        for index, (source, target) in enumerate(
            ((dq_ref, dq_hbm), (dk_ref, dk_hbm), (dv_ref, dv_hbm), (dx_ref, dx_hbm))
        )
    ]

    def copy(source, target, message, to):
        return pltpu.make_async_remote_copy(
            src_ref=source,
            dst_ref=target,
            send_sem=send_sem.at[message],
            recv_sem=recv_sem.at[message],
            device_id={"seq": to},
            device_id_type=MESH,
        )

    up1, up2, up3 = place - 1, place - 2, place - 3
    dn1, dn2, dn3 = place + 1, place + 2, place + 3
    around = [lax.rem(place + 4 - hop, 4) for hop in (1, 2, 3)]
    always = place >= 0
    later, earlier = place >= 1, place < last
    messages = {
        Q_UP: (copy(q_ref.at[pl.ds(0, BLOCK)], qn, Q_UP, up1), later, earlier),
        G_UP: (copy(g_ref.at[pl.ds(0, BLOCK)], gn, G_UP, up1), later, earlier),
        L_UP: (
            copy(lbuf.at[pl.ds(0, BLOCK)], lbuf.at[pl.ds(2 * BLOCK, BLOCK)], L_UP, up1), later, earlier
        ),
        S_UP: (copy(s1_out, s1_in, S_UP, up1), later, earlier),
        SS1_UP: (copy(ss_out, ss_held, SS1_UP, up1), place == 3, place == 2),
        SS2_UP: (copy(ss_out, ss_in.at[0], SS2_UP, up2), place == 2, place == 0),
        SS3_UP: (copy(ss_out, ss_in.at[1], SS3_UP, up3), place == 3, place == 0),
        TOT1: (copy(tot, tot_in.at[0], TOT1, around[0]), always, always),
        TOT2: (copy(tot, tot_in.at[1], TOT2, around[1]), always, always),
        TOT3: (copy(tot, tot_in.at[2], TOT3, around[2]), always, always),
        P_DN: (copy(p_out, p_in, P_DN, dn1), earlier, later),
        R_DN: (copy(r_out, r_in, R_DN, dn1), earlier, later),
        T2_DN: (copy(t_out, t_in.at[0], T2_DN, dn2), place == 1, place == 3),
        T3_DN: (copy(t_out, t_in.at[1], T3_DN, dn3), place == 0, place == 3),
        DQ_DN: (copy(dqn_out, dqn_in, DQ_DN, dn1), earlier, later),
        DA_DN: (copy(dan_out, dan_in, DA_DN, dn1), earlier, later),
    }

    def send(*which, places=always):
        for message in which:
            description, senders, _ = messages[message]
            pl.when(senders & places)(description.start)

    def sent(message):
        description, senders, _ = messages[message]
        pl.when(senders)(description.wait_send)

    def received(*which, places=always):
        for message in which:
            description, _, getters = messages[message]
            pl.when(getters & places)(description.wait_recv)

    eight = place * 2 + core

    def octet(hop):
        other = lax.rem(eight + hop, 8)
        return {"dp": (z * y_size + y) * 2 + other % 2, "seq": other // 2}

    def along_y(hop):
        return {"dp": (z * y_size + lax.rem(y + hop, y_size)) * 2 + core, "seq": place}

    def along_z(hop):
        return {"dp": (lax.rem(z + hop, z_size) * y_size + y) * 2 + core, "seq": place}

    barrier = pltpu.get_barrier_semaphore()
    partners = 0
    ring = z_size == 8
    near = (1, z_size - 1) if ring else range(1, z_size)
    for where, hops in ((octet, range(1, 8)), (along_y, range(1, y_size)), (along_z, near)):
        for hop in hops:
            pl.semaphore_signal(barrier, inc=1, device_id=where(hop), device_id_type=MESH)
            partners += 1

    def tell(index, hop):
        if ring:
            pl.semaphore_signal(ring_sem.at[index], inc=1, device_id=along_z(hop), device_id_type=MESH)

    def told(index):
        if ring:
            pl.semaphore_wait(ring_sem.at[index], 1)

    @pl.when(place == last)
    def _():
        qn[...] = jnp.zeros_like(qn)
        gn[...] = jnp.zeros_like(gn)
        lbuf[pl.ds(2 * BLOCK, BLOCK), :] = jnp.zeros((BLOCK, LANES), F32)
        s1_in[...] = jnp.zeros_like(s1_in)

    @pl.when(place != 0)
    def _():
        ss_in[...] = jnp.zeros_like(ss_in)

    @pl.when(place != last)
    def _():
        t_in[...] = jnp.zeros_like(t_in)

    @pl.when(place == 0)
    def _():
        p_in[...] = jnp.zeros_like(p_in)
        r_in[...] = jnp.zeros_like(r_in)
        dqn_in[...] = jnp.zeros_like(dqn_in)
        dan_in[...] = jnp.zeros_like(dan_in)

    row, col = iota((LANES, LANES), 0), iota((LANES, LANES), 1)
    same = (row // BLOCK) == (col // BLOCK)
    tri = flag(same & (col <= row))
    head_row = iota((LANES, WIDTH), 0)
    head_lane = iota((LANES, WIDTH), 1) // BLOCK
    spread = flag(head_row == head_lane)
    spread_gate = flag(head_row == head_lane + HEADS)
    spread_pieces = flag(head_row % 32 == head_lane)
    head_lanes = iota((BLOCK, LANES), 1) < HEADS
    left = iota((BLOCK, LANES), 1) < BLOCK
    left1 = iota((1, LANES), 1) < BLOCK
    srow, scol = iota((BLOCK, BLOCK), 0), iota((BLOCK, BLOCK), 1)
    upper_in = flag(scol >= srow)
    lower = flag(scol < srow)
    at_or_before = flag(scol <= srow)
    after = flag(scol > srow)

    loads[0].wait()
    loads[1].wait()
    loads[2].wait()
    w_hi, w_lo = pieces(w_ref[...], 2)
    no_rows = jnp.zeros((32, WIDTH), BF16)
    x = x_ref[...]
    logits = nt(x, jnp.concatenate([w_hi, no_rows, w_lo, no_rows], axis=0))
    logits = logits + jnp.concatenate([logits[:, BLOCK:], logits[:, :BLOCK]], axis=1)
    small = jnp.exp(-jnp.abs(logits))
    soft = jnp.maximum(logits, 0.0) + jnp.log1p(small)
    sig = jnp.where(logits >= 0.0, 1.0, small) / (1.0 + small)
    rate = jnp.concatenate([rate_ref[...], jnp.zeros((1, LANES - HEADS), F32)], axis=1)
    decay = -rate * soft
    gamma = sig * (1.0 / BLOCK)
    log_own = sum(nn(tri, part) for part in pieces(decay, 3))
    lbuf[pl.ds(0, LANES), :] = log_own
    tot[...] = jnp.zeros_like(tot)
    tot[0:1, :] = log_own[BLOCK - 1 : BLOCK]
    tot[1:2, :] = log_own[LANES - 1 :]

    for load in loads[3:]:
        load.wait()
    pl.semaphore_wait(barrier, partners)
    send(L_UP, TOT1, TOT2, TOT3)
    send(Q_UP, G_UP, places=place < last)
    tell(0, 1)
    tell(1, z_size - 1)

    def beside(a):
        parts = [part[:, :32] for part in pieces(a, 3)]
        return jnp.concatenate(parts + [jnp.zeros((a.shape[0], 32), BF16)], axis=1)

    def expand(a):
        return nn(beside(a), spread_pieces)

    def block_rows(logs, block, offset):
        pick = flag(row == (col % BLOCK) + offset)
        turned = sum(tn(part, pick) for part in pieces(logs, 3))
        for pair in range(PAIRS):
            lrow[block : block + 1, pl.ds(pair * LANES, LANES)] = jnp.where(
                left1, turned[2 * pair : 2 * pair + 1], turned[2 * pair + 1 : 2 * pair + 2]
            )

    tail0 = jnp.exp(log_own[BLOCK - 1 : BLOCK] - log_own[:BLOCK])
    tail1 = jnp.exp(log_own[LANES - 1 :] - log_own[BLOCK:])

    def twice(mask, a):
        return nn(
            jnp.concatenate([mask, mask], axis=1), jnp.concatenate(pieces(a, 2), axis=0)
        )

    def ending(mask, tail):
        return jnp.where(head_lanes, twice(mask, tail), 0.0)

    gamma_first = jnp.concatenate([gamma[:, HEADS:32], jnp.zeros((LANES, LANES - HEADS), F32)], axis=1)
    expanded = expand(
        jnp.concatenate(
            [log_own, gamma_first, ending(upper_in, tail0), ending(lower, tail1), ending(upper_in, tail1)],
            axis=0,
        )
    )
    lx[pl.ds(0, LANES), :] = expanded[:LANES]
    gamma_x[...] = expanded[LANES : 2 * LANES]
    blast_x[pl.ds(0, 3 * BLOCK), :] = expanded[2 * LANES :]

    def each_pair(step, begin=0, end=PAIRS):
        lax.fori_loop(begin, end, step, 0, unroll=end - begin)

    def together(step, group=GROUP):
        def several(index, carry):
            step([index * group + offset for offset in range(group)])
            return carry

        return several

    def all_pairs(step, group=WIDE):
        each_pair(together(step, group), 0, PAIRS // group)

    def lanes_of(pair):
        return pl.ds(pl.multiple_of(pair * LANES, LANES), LANES)

    def phi(raw, coef):
        value = raw.astype(F32)
        return 0.125 * (value + coef * value * value)

    def compact(full):
        return jnp.where(left, full[:BLOCK], full[BLOCK:])

    def diagonal(value):
        none = jnp.zeros_like(value)
        return jnp.concatenate([jnp.where(left, value, none), jnp.where(left, none, value)], axis=0)

    def weighted(a, weights):
        return (a.astype(F32) * weights).astype(BF16)

    def own_step(pairs):
        ats = [lanes_of(pair) for pair in pairs]
        coefs = [coef_ref[:, at] for at in ats]
        q_feat = [phi(q_ref[:, at], coef).astype(BF16) for at, coef in zip(ats, coefs)]
        keys = [
            (phi(k_ref[:, at], coef) * gamma_x[:, at]).astype(BF16) for at, coef in zip(ats, coefs)
        ]
        logs = [lx[pl.ds(0, LANES), at] for at in ats]
        scaled = [weighted(g_ref[:, at], jnp.exp(a)) for at, a in zip(ats, logs)]
        values = [v_ref[:, at] for at in ats]
        carried0 = [
            weighted(a[:BLOCK], blast_x[pl.ds(0, BLOCK), at]) for at, a in zip(ats, keys)
        ]
        carried1 = [weighted(a, blast_x[pl.ds(BLOCK, LANES), at]) for at, a in zip(ats, keys)]
        s0 = [compact(tn(a[:BLOCK], b[:BLOCK])) for a, b in zip(q_feat, scaled)]
        s1 = [compact(tn(a[BLOCK:], b[BLOCK:])) for a, b in zip(q_feat, scaled)]
        u0 = [compact(tn(a, b[:BLOCK])) for a, b in zip(carried0, values)]
        c1 = [compact(tn(a, b)) for a, b in zip(carried1, values)]
        for index, at in enumerate(ats):
            qf[pl.ds(0, LANES), at] = q_feat[index]
            wk[:, at] = keys[index]
            gq[:, at] = scaled[index]
            fall0 = jnp.exp(logs[index][BLOCK - 1 : BLOCK])
            fall1 = jnp.exp(logs[index][LANES - 1 :])
            s1_out[:, at] = s1[index].astype(BF16)
            ss_out[:, at] = (s0[index] + fall0 * s1[index]).astype(BF16)
            end = fall1 * u0[index] + c1[index]
            u0c[:, at] = u0[index]
            c1c[:, at] = end
            s1c[:, at] = s1[index]
            p_out[:, at] = end.astype(BF16)

    all_pairs(own_step)
    send(SS1_UP, SS2_UP, SS3_UP)
    send(Q_UP, G_UP, places=place == last)
    send(S_UP, places=place != 2)
    send(P_DN, places=place != 1)

    block_rows(log_own, 0, 0)
    block_rows(log_own, 1, BLOCK)

    step = col % BLOCK
    cur_mask = flag(same & (row % BLOCK >= step))
    prev_mask = flag(same & (row % BLOCK < step))
    both_mask = jnp.concatenate([cur_mask, prev_mask], axis=1)
    causal = (iota((LANES, LANES), 1) % BLOCK) <= (iota((LANES, LANES), 0) % BLOCK)

    def spans(rows):
        return pl.ds(rows.start, rows.stop - rows.start)

    first_rows, last_rows = slice(0, BLOCK), slice(BLOCK, LANES)

    corner = iota((LANES, LANES), 0) < BLOCK, iota((LANES, LANES), 1) < BLOCK
    first_head, second_head = corner[0] & corner[1], ~corner[0] & ~corner[1]

    def turned_diagonals(rows):
        turned = rows.T
        swapped = jnp.concatenate([turned[:, BLOCK:], turned[:, :BLOCK]], axis=1)
        none = jnp.zeros_like(turned)
        return (
            jnp.where(first_head, turned, jnp.where(second_head, swapped, none)),
            jnp.where(first_head, swapped, jnp.where(second_head, turned, none)),
        )

    def tiles(keys_bd, keys_t, values_t, queries, grads, kernels):
        scores = [nn(a, b) for a, b in zip(queries, keys_t)]
        d_weights = [nn(a, b) for a, b in zip(grads, values_t)]
        weights = [(a * b).astype(BF16) for a, b in zip(scores, kernels)]
        d_scores = [(a * b).astype(BF16) for a, b in zip(d_weights, kernels)]
        d_kernels = [(a * b).astype(BF16) for a, b in zip(d_weights, scores)]
        d_queries = [nn(a, b) for a, b in zip(d_scores, keys_bd)]
        d_values = [compact(tn(a, b)) for a, b in zip(weights, grads)]
        d_keys = [compact(tn(a, b)) for a, b in zip(d_scores, queries)]
        return d_queries, d_values, d_keys, d_kernels

    def window_step(pairs):
        ats = [lanes_of(pair) for pair in pairs]
        keys = [wk[:, at] for at in ats]
        values = [v_ref[:, at] for at in ats]
        queries = [qf[pl.ds(0, LANES), at] for at in ats]
        grads = [g_ref[:, at] for at in ats]
        rows = [
            jnp.concatenate(
                [jnp.broadcast_to(lrow[b : b + 1, at], (BLOCK, LANES)) for b in range(2)], axis=0
            )
            for at in ats
        ]
        decays = [
            jnp.exp(jnp.where(causal, lx[pl.ds(0, LANES), at] - row, NEVER))
            for at, row in zip(ats, rows)
        ]
        low = [a.astype(BF16) for a in decays]
        start = [nn(a[:BLOCK], cur_mask) for a in low]
        middle = [nn(a[BLOCK:], both_mask) for a in low]
        keys_t = [turned_diagonals(a) for a in keys]
        values_t = [turned_diagonals(a) for a in values]
        for pair, a, b in zip(pairs, keys_t, values_t):
            keys_held[pair] = a[1]
            values_held[pair] = b[1]
        dq0, dv0, dk0, db0 = tiles(
            [diagonal(a[:BLOCK]) for a in keys], [a[0] for a in keys_t], [a[0] for a in values_t],
            queries, grads,
            [jnp.concatenate([a, b[:, LANES:]], axis=0) for a, b in zip(start, middle)],
        )
        dq1, dv1, dk1, db1 = tiles(
            [diagonal(a[BLOCK:]) for a in keys], [a[1] for a in keys_t], [a[1] for a in values_t],
            [a[BLOCK:] for a in queries], [a[BLOCK:] for a in grads], [a[:, :LANES] for a in middle],
        )
        d_decays = [
            jnp.concatenate(
                [
                    nt(a[:BLOCK], cur_mask),
                    nt(jnp.concatenate([b, a[BLOCK:]], axis=1), both_mask),
                ],
                axis=0,
            )
            for a, b in zip(db0, db1)
        ]
        for index, at in enumerate(ats):
            dvf[pl.ds(0, BLOCK), at] = dv0[index]
            dvf[pl.ds(BLOCK, BLOCK), at] = dv1[index]
            dwk[pl.ds(0, BLOCK), at] = dk0[index]
            dwk[pl.ds(BLOCK, BLOCK), at] = dk1[index]
            dqf[pl.ds(0, BLOCK), at] = dq0[index][:BLOCK]
            dqf[pl.ds(BLOCK, BLOCK), at] = dq0[index][BLOCK:] + dq1[index]
            gmat[pl.ds(0, LANES), at] = (d_decays[index] * decays[index]).astype(BF16)

    each_pair(together(window_step), 0, PAIRS // GROUP // 2)

    received(L_UP)
    log_next = lbuf[pl.ds(2 * BLOCK, BLOCK), :]
    tail2 = jnp.exp(log_next[BLOCK - 1 :] - log_next)
    expanded = expand(jnp.concatenate([log_next, ending(lower, tail2)], axis=0))
    lx[pl.ds(LANES, BLOCK), :] = expanded[:BLOCK]
    blast_x[pl.ds(3 * BLOCK, BLOCK), :] = expanded[BLOCK:]

    def next_step(pairs):
        ats = [lanes_of(pair) for pair in pairs]
        carried = [
            weighted(wk[pl.ds(BLOCK, BLOCK), at], blast_x[pl.ds(3 * BLOCK, BLOCK), at]) for at in ats
        ]
        entering = [
            compact(tn(a, v_ref[pl.ds(BLOCK, BLOCK), at])) for a, at in zip(carried, ats)
        ]
        for r, at in zip(entering, ats):
            fall2 = jnp.exp(lx[3 * BLOCK - 1 : 3 * BLOCK, at])
            r_out[:, at] = r.astype(BF16)
            t_out[:, at] = (fall2 * c1c[:, at] + r).astype(BF16)

    all_pairs(next_step)
    send(T2_DN, T3_DN, R_DN)

    told(0)
    told(1)
    tell(2, 1)
    tell(3, z_size - 1)
    each_pair(together(window_step), PAIRS // GROUP // 2, PAIRS // GROUP)
    told(2)
    told(3)
    tell(4, 1)
    own0 = jnp.exp(lx[BLOCK - 1 : BLOCK, :])
    own1 = jnp.exp(lx[LANES - 1 : LANES, :])

    @pl.when(place == 2)
    def _():
        messages[SS1_UP][0].wait_recv()
        s1_out[...] = (s1c[...] + own1 * ss_held[...].astype(F32)).astype(BF16)
        messages[S_UP][0].start()

    @pl.when(place == 1)
    def _():
        messages[P_DN][0].wait_recv()
        messages[R_DN][0].wait_recv()
        entered = own0 * p_in[...].astype(F32) + r_in[...].astype(F32)
        p_out[...] = (c1c[...] + own1 * entered).astype(BF16)
        messages[P_DN][0].start()

    block_rows(lbuf[pl.ds(BLOCK, LANES), :], 2, BLOCK)

    received(Q_UP, G_UP)

    def cross_step(pairs):
        ats = [lanes_of(pair) for pair in pairs]
        queries = [phi(qn[:, at], coef_ref[:, at]).astype(BF16) for at in ats]
        grads = [gn[:, at] for at in ats]
        logs = [lx[pl.ds(LANES, BLOCK), at] for at in ats]
        decays = [
            jnp.exp(jnp.where(causal[:BLOCK], a - lrow[2:3, at], NEVER)) for at, a in zip(ats, logs)
        ]
        d_queries, d_values, d_keys, d_kernels = tiles(
            [diagonal(wk[pl.ds(BLOCK, BLOCK), at]) for at in ats],
            [keys_held[pair] for pair in pairs], [values_held[pair] for pair in pairs],
            queries, grads, [nn(a.astype(BF16), prev_mask) for a in decays],
        )
        entering = [
            compact(tn(a, weighted(b, jnp.exp(c)))) for a, b, c in zip(queries, grads, logs)
        ]
        d_decays = [nt(a, prev_mask) for a in d_kernels]
        for index, at in enumerate(ats):
            dqn_out[:, at] = d_queries[index].astype(BF16)
            raw = qn[:, at].astype(F32)
            coef_sum[1:2, at] = jnp.sum(
                d_queries[index] * (0.125 * raw * raw), axis=0, keepdims=True
            )
            dvf[pl.ds(BLOCK, BLOCK), at] = dvf[pl.ds(BLOCK, BLOCK), at] + d_values[index]
            dwk[pl.ds(BLOCK, BLOCK), at] = dwk[pl.ds(BLOCK, BLOCK), at] + d_keys[index]
            gmat[pl.ds(LANES, BLOCK), at] = (d_decays[index] * decays[index]).astype(BF16)
            c1c[:, at] = entering[index]

    each_pair(together(cross_step), 0, PAIRS // GROUP)
    send(DQ_DN)

    def decay_grad(block):
        later = nn(upper_in, gmat[pl.ds(block * BLOCK, BLOCK), :])
        lanes = iota((BLOCK, WIDTH), 1) % BLOCK
        kept = jnp.where(lanes < iota((BLOCK, WIDTH), 0), later, 0.0)
        return nt(kept.astype(BF16), spread)

    received(TOT1, S_UP, TOT2, SS2_UP, SS3_UP, TOT3)
    falls = expand(jnp.concatenate([tot_in[slot] for slot in range(3)], axis=0))
    falls = [falls[8 * slot : 8 * slot + 8] for slot in range(3)]
    next1_fall1 = jnp.exp(falls[0][1:2])
    next2_all = jnp.exp(falls[1][0:1] + falls[1][1:2])
    prev1_fall1 = jnp.exp(falls[2][1:2])
    prev1_all = jnp.exp(falls[2][0:1] + falls[2][1:2])
    prev2_fall1 = jnp.exp(falls[1][1:2])
    next0 = jnp.exp(lx[3 * BLOCK - 1 :, :])
    z_grad = s1_in[...].astype(F32) + next1_fall1 * (
        ss_in[0].astype(F32) + next2_all * ss_in[1].astype(F32)
    )
    z_end[...] = z_grad.astype(BF16)
    end_grad = next0 * z_grad + c1c[...]
    mid_grad = own1 * end_grad + s1c[...]
    n_end[...] = end_grad.astype(BF16)
    n_mid[...] = mid_grad.astype(BF16)

    def enter(index, keys, d_role, at):
        weights = blast_x[pl.ds(index * BLOCK, BLOCK), at]
        own_keys = keys.astype(F32)
        xmat[pl.ds(index * BLOCK, BLOCK), at] = (d_role * own_keys).astype(BF16)
        return (own_keys * weights).astype(BF16), d_role * weights

    def outer_step(pairs):
        ats = [lanes_of(pair) for pair in pairs]
        rows = pl.ds(BLOCK, BLOCK)
        grads = [diagonal(z_end[:, at]) for at in ats]
        d_roles = [nt(v_ref[rows, at], a) for at, a in zip(ats, grads)]
        entered = [enter(3, wk[rows, at], a, at) for at, a in zip(ats, d_roles)]
        d_values = [nn(a[0], b) for a, b in zip(entered, grads)]
        for at, a, b in zip(ats, entered, d_values):
            dwk[rows, at] = dwk[rows, at] + a[1]
            dvf[rows, at] = dvf[rows, at] + b

    all_pairs(outer_step)
    d_last = nt(xmat[pl.ds(3 * BLOCK, BLOCK), :], spread)
    dan_out[...] = decay_grad(2) + twice(lower, twice(after, d_last) * tail2)
    send(DA_DN)

    def inner_step(pairs):
        ats = [lanes_of(pair) for pair in pairs]
        keys = [wk[:, at] for at in ats]
        values = [v_ref[:, at] for at in ats]
        ends = [diagonal(n_end[:, at]) for at in ats]
        both = [
            jnp.concatenate([diagonal(n_mid[:, at]), a], axis=0) for at, a in zip(ats, ends)
        ]
        d_first = [nt(a[:BLOCK], b) for a, b in zip(values, both)]
        d_second = [nt(a[BLOCK:], b) for a, b in zip(values, ends)]
        enter0 = [enter(0, a[:BLOCK], b[:, :LANES], at) for a, b, at in zip(keys, d_first, ats)]
        enter1 = [enter(1, a[:BLOCK], b[:, LANES:], at) for a, b, at in zip(keys, d_first, ats)]
        enter2 = [enter(2, a[BLOCK:], b, at) for a, b, at in zip(keys, d_second, ats)]
        dv0 = [
            nn(jnp.concatenate([a[0], b[0]], axis=1), c) for a, b, c in zip(enter0, enter1, both)
        ]
        dv1 = [nn(a[0], b) for a, b in zip(enter2, ends)]
        for index, at in enumerate(ats):
            dv_ref[:, at] = (
                dvf[:, at] + jnp.concatenate([dv0[index], dv1[index]], axis=0)
            ).astype(BF16)
            d_keys = dwk[:, at] + jnp.concatenate(
                [enter0[index][1] + enter1[index][1], enter2[index][1]], axis=0
            )
            coef = coef_ref[:, at]
            raw = k_ref[:, at].astype(F32)
            d_feat = d_keys * gamma_x[:, at]
            square = 0.125 * raw * raw
            xmat[pl.ds(6 * BLOCK, LANES), at] = (
                d_keys * (0.125 * raw + coef * square)
            ).astype(BF16)
            dk_ref[:, at] = (d_feat * (0.125 + (0.25 * coef) * raw)).astype(BF16)
            coef_sum[0:1, at] = jnp.sum(d_feat * square, axis=0, keepdims=True)

    all_pairs(inner_step)
    stores[1].start()
    stores[2].start()
    d_enter = nt(xmat[pl.ds(0, 3 * BLOCK), :], spread)
    d_gamma = nt(xmat[pl.ds(6 * BLOCK, LANES), :], spread_gate)
    d_decay0 = decay_grad(0) + twice(lower, twice(at_or_before, d_enter[:BLOCK]) * tail0)
    entered = nn(
        jnp.concatenate([at_or_before, at_or_before, after, after], axis=1),
        jnp.concatenate(pieces(d_enter[2 * BLOCK :], 2) + pieces(d_enter[BLOCK : 2 * BLOCK], 2), axis=0),
    )
    d_decay1 = decay_grad(1) + twice(lower, entered * tail1)

    received(P_DN, R_DN, places=place != 1)
    received(T2_DN, T3_DN)
    memory = (
        p_in[...].astype(F32)
        + prev1_fall1 * t_in[0].astype(F32)
        + (prev2_fall1 * prev1_all) * t_in[1].astype(F32)
    )
    middle_memory = own0 * memory + r_in[...].astype(F32) + u0c[...]
    m_in[...] = memory.astype(BF16)
    m_mid[...] = middle_memory.astype(BF16)
    fall_grad = jnp.concatenate(
        [
            own0 * jnp.sum(memory * mid_grad, axis=0, keepdims=True),
            own1 * jnp.sum(middle_memory * end_grad, axis=0, keepdims=True),
            jnp.zeros((6, WIDTH), F32),
        ],
        axis=0,
    )
    fall_grad = sum(nt(part, spread) for part in pieces(fall_grad, 2))

    def query_step(pairs):
        ats = [lanes_of(pair) for pair in pairs]
        scaled = [gq[:, at] for at in ats]
        carried = [
            jnp.concatenate(
                [
                    nt(a[:BLOCK], diagonal(m_in[:, at])),
                    nt(a[BLOCK:], diagonal(m_mid[:, at])),
                ],
                axis=0,
            )
            for a, at in zip(scaled, ats)
        ]
        for a, at in zip(carried, ats):
            xmat[pl.ds(4 * BLOCK, LANES), at] = (
                a * qf[pl.ds(0, LANES), at].astype(F32)
            ).astype(BF16)
            raw = q_ref[:, at].astype(F32)
            d_feat = dqf[:, at] + a
            dqf[:, at] = d_feat
            coef_sum[0:1, at] = (
                coef_sum[0:1, at]
                + coef_sum[1:2, at]
                + jnp.sum(d_feat * (0.125 * raw * raw), axis=0, keepdims=True)
            )

    all_pairs(query_step)
    d_out = nt(xmat[pl.ds(4 * BLOCK, LANES), :], spread)
    received(DA_DN)
    d_decay = jnp.concatenate(
        [
            d_decay0 + dan_in[...] + twice(upper_in, d_out[:BLOCK]) + fall_grad[0:1],
            d_decay1 + twice(upper_in, d_out[BLOCK:]) + fall_grad[1:2],
        ],
        axis=0,
    )
    is_decay = iota((LANES, LANES), 1) < HEADS
    d_logits = jnp.where(is_decay, -rate * sig * d_decay, d_gamma * gamma * (1.0 - sig))
    rates = jnp.sum(jnp.where(is_decay, -soft * d_decay, 0.0), axis=0, keepdims=True)
    gate = nn(jnp.concatenate(pieces(d_logits.T[:32], 2), axis=0), x)
    gate = gate[:32] + gate[32:]

    def paired(rows):
        high = rows.astype(BF16).astype(F32)
        return jnp.concatenate([high, rows - high], axis=0).astype(BF16)

    no_rates = jnp.zeros((1, LANES), F32)
    for chunk in range(8):
        at = slice(chunk * LANES, (chunk + 1) * LANES)
        mine[chunk, 0:32, :] = gate[:32, at].astype(BF16)
        mine[chunk, 32:TALL, :] = paired(
            jnp.concatenate(
                [
                    coef_sum[0:1, at],
                    rates if chunk == 0 else no_rates,
                    jnp.zeros((6, LANES), F32),
                ],
                axis=0,
            )
        )

    def exchange(base, size, where, source, target, reach=1):
        made = [
            pltpu.make_async_remote_copy(
                src_ref=source(hop),
                dst_ref=target,
                send_sem=sum_send.at[base + hop],
                recv_sem=sum_recv.at[base + hop],
                device_id=where(hop),
                device_id_type=MESH,
            )
            for hop in sorted(range(1, size), key=lambda hop: -min(hop // reach, (size - hop) // reach))
        ]
        for one in made:
            one.start()
        return made

    def added(buffer, count):
        total = buffer[0].astype(F32)
        for index in range(1, count):
            total = total + buffer[index].astype(F32)
        return jnp.concatenate(
            [total[:32].astype(BF16), paired(total[32:40] + total[40:])], axis=0
        )

    made = exchange(0, 8, octet, lambda hop: mine.at[lax.rem(eight + hop, 8)], first.at[eight], 2)
    first[eight] = mine[eight]
    d_hi, d_lo = [part[:, :32] for part in pieces(d_logits, 2)]
    dx_ref[...] = nn(
        jnp.concatenate([d_hi, d_lo, d_hi, jnp.zeros((LANES, 32), BF16)], axis=1),
        jnp.concatenate([w_hi, w_hi, w_lo, no_rows], axis=0),
    ).astype(BF16)
    stores[3].start()
    received(DQ_DN)

    def last_step(pair, carry):
        at = lanes_of(pair)
        raw = q_ref[:, at].astype(F32)
        d_feat = dqf[:, at] + jnp.concatenate(
            [dqn_in[:, at].astype(F32), jnp.zeros((BLOCK, LANES), F32)], axis=0
        )
        dq_ref[:, at] = (d_feat * (0.125 + (0.25 * coef_ref[:, at]) * raw)).astype(BF16)
        return carry

    each_pair(last_step)
    stores[0].start()
    for one in made:
        one.wait_recv()
    second[y] = added(first, 8)
    more = exchange(8, y_size, along_y, lambda hop: second.at[y], second.at[y])
    for one in more:
        one.wait_recv()
    made += more
    third[z] = added(second, y_size)
    told(4)
    more = exchange(8 + y_size, z_size, along_z, lambda hop: third.at[z], third.at[z])
    for one in more:
        one.wait_recv()
    made += more
    done[...] = added(third, z_size)
    own = pltpu.make_async_copy(done, done_hbm.at[eight], store_sem.at[4])
    own.start()
    more = exchange(
        8 + y_size + z_size, 8, octet, lambda hop: done, done_hbm.at[eight], 2
    )
    for message in range(MESSAGES):
        sent(message)
    for store in stores:
        store.wait()
    own.wait()
    for one in made:
        one.wait_send()
    for one in more:
        one.wait()


def main_call(sizes, queries, keys, values, inputs, gate, coef, rate, cotangent):
    z_size, y_size = sizes
    rows = queries.shape[0]
    anywhere = pl.BlockSpec(memory_space=pltpu.HBM)
    block, full = (BLOCK, WIDTH), (LANES, WIDTH)
    out = jax.ShapeDtypeStruct((rows, WIDTH), BF16)
    tile = (TALL, LANES)
    scratch = [
        (full, BF16), (full, BF16), (full, BF16), (full, BF16), (full, BF16),
        (gate.shape, F32), (coef.shape, F32), (rate.shape, F32),
        (full, BF16), (full, BF16), (full, BF16), (full, BF16),
        (block, BF16), (block, BF16), ((3 * BLOCK, LANES), F32), ((8, LANES), F32), ((3, 8, LANES), F32),
        (block, BF16), (block, BF16), (block, BF16), (block, BF16), ((2,) + block, BF16),
        (block, BF16), (block, BF16), (block, BF16), (block, BF16), (block, BF16), ((2,) + block, BF16),
        (block, BF16), (block, BF16), ((BLOCK, LANES), F32), ((BLOCK, LANES), F32),
        ((8, WIDTH), F32), ((3 * BLOCK, WIDTH), F32), (full, F32), ((4 * BLOCK, WIDTH), F32),
        (full, BF16), (full, BF16), (full, BF16),
        (block, F32), (block, F32), (block, F32),
        (block, BF16), (block, BF16), (block, BF16), (block, BF16), (block, BF16),
        (full, F32), (full, F32), (full, F32),
        ((3 * BLOCK, WIDTH), BF16), ((8 * BLOCK, WIDTH), BF16), ((8, WIDTH), F32),
        ((PAIRS, LANES, LANES), BF16), ((PAIRS, LANES, LANES), BF16),
        ((8,) + tile, BF16), ((8,) + tile, BF16), ((y_size,) + tile, BF16), ((z_size,) + tile, BF16),
        (tile, BF16),
    ]
    count = 16 + y_size + z_size
    return pl.pallas_call(
        functools.partial(main_kernel, z_size, y_size),
        out_shape=[out, out, out, out, jax.ShapeDtypeStruct((8,) + tile, BF16)],
        in_specs=[anywhere] * 8,
        out_specs=[anywhere] * 5,
        scratch_shapes=[pltpu.VMEM(shape, dtype) for shape, dtype in scratch]
        + [
            pltpu.SemaphoreType.DMA((number,))
            for number in (LOADS, STORES, MESSAGES, MESSAGES, count, count)
        ]
        + [pltpu.SemaphoreType.REGULAR((5,))],
        compiler_params=pltpu.CompilerParams(
            collective_id=0, has_side_effects=True, vmem_limit_bytes=56 * 2**20
        ),
        name="window_backward",
    )(queries, keys, values, inputs, gate, coef, rate, cotangent)


def hand_out_kernel(*refs):
    sources, targets, held = refs[:5], refs[5:12], refs[12:20]
    load_sem, store_sem = refs[20:]
    loads = [
        pltpu.make_async_copy(sources[index], held[index], load_sem.at[index]) for index in range(5)
    ]
    stores = [
        pltpu.make_async_copy(held[index if index < 4 else index + 1], targets[index], store_sem.at[index])
        for index in range(7)
    ]
    for load in loads[::-1]:
        load.start()
    done, gate, coef, rate = held[4:]
    loads[4].wait()
    for chunk in range(8):
        at = slice(chunk * LANES, (chunk + 1) * LANES)
        total = done[chunk].astype(F32)
        gate[:, at] = total[:32]
        rest = total[32:40] + total[40:]
        coef[:, at] = rest[0:1]
        if chunk == 0:
            rate[...] = rest[1:2, :HEADS]
    for store in stores[4:]:
        store.start()
    for index in range(3, -1, -1):
        loads[index].wait()
        stores[index].start()
    for store in stores:
        store.wait()


def hand_out(results):
    anywhere = pl.BlockSpec(memory_space=pltpu.HBM)
    params = [jax.ShapeDtypeStruct(shape, F32) for shape in ((32, WIDTH), (1, WIDTH), (1, HEADS))]
    shapes = [jax.ShapeDtypeStruct(a.shape, a.dtype) for a in results]
    return pl.pallas_call(
        hand_out_kernel,
        out_shape=shapes[:4] + params,
        in_specs=[anywhere] * 5,
        out_specs=[anywhere] * 7,
        scratch_shapes=[pltpu.VMEM(a.shape, a.dtype) for a in shapes + params]
        + [pltpu.SemaphoreType.DMA((5,)), pltpu.SemaphoreType.DMA((7,))],
        compiler_params=pltpu.CompilerParams(vmem_limit_bytes=56 * 2**20),
        name="hand_out",
    )(*results)


def on_device(sizes, queries, keys, values, inputs, gate, coef, rate, cotangent):
    results = main_call(
        sizes,
        queries[0], keys[0], values[0], inputs[0], gate.T, coef[None], rate[None], cotangent[0],
    )
    dq, dk, dv, dx, d_gate, d_coef, d_rate = hand_out(results)
    return (dq[None], dk[None], dv[None], dx[None], d_gate.T, d_coef[0], d_rate[0])


def solution(mesh):
    rows = P("dp", "seq", None)
    y_size = min(4, max(1, mesh.shape["dp"] // 2))
    sizes = (mesh.shape["dp"] // (2 * y_size), y_size)
    return jax.shard_map(
        functools.partial(on_device, sizes),
        mesh=mesh,
        in_specs=(rows, rows, rows, rows, P(), P(), P(), rows),
        out_specs=(rows, rows, rows, rows, P(), P(), P()),
        check_vma=False,
    )
```

```python
import functools

import jax
import jax.numpy as jnp
from jax import lax
from jax.experimental import pallas as pl
from jax.experimental.pallas import tpu as pltpu
from jax.sharding import PartitionSpec as P

BLOCK = 64
LANES = 128
WIDTH = 1024
PAIRS = WIDTH // LANES
HEADS = 16
F32 = jnp.float32
BF16 = jnp.bfloat16
MESH = pl.DeviceIdType.MESH


def nn(a, b):
    return lax.dot_general(a, b, (((1,), (0,)), ((), ())), preferred_element_type=F32)


def nt(a, b):
    return lax.dot_general(a, b, (((1,), (1,)), ((), ())), preferred_element_type=F32)


def tn(a, b):
    return lax.dot_general(a, b, (((0,), (0,)), ((), ())), preferred_element_type=F32)


def pieces(a, count):
    parts = []
    for _ in range(count):
        part = a.astype(BF16)
        parts.append(part)
        a = a - part.astype(F32)
    return parts


def flag(condition):
    return jnp.where(condition, 1.0, 0.0).astype(BF16)


def iota(shape, dimension):
    return lax.broadcasted_iota(jnp.int32, shape, dimension)


Q_UP, G_UP, L_UP, S_UP, SS_ROUND, SS_ON, SS_BACK, SS_UP, TOT1, TOT2, TOT3 = range(11)
P_DN, R_DN, T2_DN, T3_DN, DQ_DN, DA_DN = range(11, 17)
MESSAGES = 17
LOADS = 8
STORES = 5
TALL = 48
NEVER = -1e30
WIDE = 8
GROUP = 4


def main_kernel(
    z_size, y_size,
    q_hbm, k_hbm, v_hbm, x_hbm, w_hbm, coef_hbm, rate_hbm, g_hbm,
    dq_hbm, dk_hbm, dv_hbm, dx_hbm, done_hbm,
    q_ref, k_ref, v_ref, x_ref, g_ref, w_ref, coef_ref, rate_ref,
    dq_ref, dk_ref, dv_ref, dx_ref,
    qn, gn, lbuf, tot, tot_in, s1_out, ss_out, s1_in, ss_held, ss_in, p_out, r_out, t_out, p_in, r_in, t_in,
    dqn_out, dqn_in, dan_out, dan_in,
    lrow, lx, gamma_x, blast_x, qf, wk, gq, s1c, u0c, c1c, m_in, m_mid, n_mid, n_end, z_end,
    dqf, dwk, dvf, gmat, xmat, coef_sum, keys_held, values_held,
    mine, first, second, third, done,
    load_sem, store_sem, send_sem, recv_sem, sum_send, sum_recv, ring_sem,
):
    place, dp = lax.axis_index("seq"), lax.axis_index("dp")
    z, y, core = dp // (y_size * 2), (dp // 2) % y_size, dp % 2
    last = 3

    loads = [
        pltpu.make_async_copy(source, target, load_sem.at[index])
        for index, (source, target) in enumerate(
            (
                (x_hbm, x_ref), (w_hbm, w_ref), (rate_hbm, rate_ref), (coef_hbm, coef_ref),
                (k_hbm, k_ref), (q_hbm, q_ref), (v_hbm, v_ref), (g_hbm, g_ref),
            )
        )
    ]
    for load in loads:
        load.start()
    stores = [
        pltpu.make_async_copy(source, target, store_sem.at[index])
        for index, (source, target) in enumerate(
            ((dq_ref, dq_hbm), (dk_ref, dk_hbm), (dv_ref, dv_hbm), (dx_ref, dx_hbm))
        )
    ]

    def copy(source, target, message, to):
        return pltpu.make_async_remote_copy(
            src_ref=source,
            dst_ref=target,
            send_sem=send_sem.at[message],
            recv_sem=recv_sem.at[message],
            device_id={"seq": to},
            device_id_type=MESH,
        )

    up1, up3 = place - 1, place - 3
    dn1, dn2, dn3 = place + 1, place + 2, place + 3
    around = [lax.rem(place + 4 - hop, 4) for hop in (1, 2, 3)]
    always = place >= 0
    later, earlier = place >= 1, place < last
    messages = {
        Q_UP: (copy(q_ref.at[pl.ds(0, BLOCK)], qn, Q_UP, up1), later, earlier),
        G_UP: (copy(g_ref.at[pl.ds(0, BLOCK)], gn, G_UP, up1), later, earlier),
        L_UP: (
            copy(lbuf.at[pl.ds(0, BLOCK)], lbuf.at[pl.ds(2 * BLOCK, BLOCK)], L_UP, up1), later, earlier
        ),
        S_UP: (copy(s1_out, s1_in, S_UP, up1), later, earlier),
        SS_UP: (copy(ss_out, ss_in.at[1], SS_UP, up3), place == 3, place == 0),
        SS_ON: (copy(ss_in.at[1], ss_in.at[0], SS_ON, dn1), place == 0, place == 1),
        SS_ROUND: (copy(ss_out, ss_held, SS_ROUND, dn1), place == 2, place == 3),
        SS_BACK: (copy(ss_held, ss_in.at[0], SS_BACK, up3), place == 3, place == 0),
        TOT1: (copy(tot, tot_in.at[0], TOT1, around[0]), always, always),
        TOT2: (copy(tot, tot_in.at[1], TOT2, around[1]), always, always),
        TOT3: (copy(tot, tot_in.at[2], TOT3, around[2]), always, always),
        P_DN: (copy(p_out, p_in, P_DN, dn1), earlier, later),
        R_DN: (copy(r_out, r_in, R_DN, dn1), earlier, later),
        T2_DN: (copy(t_out, t_in.at[0], T2_DN, dn2), place == 1, place == 3),
        T3_DN: (copy(t_out, t_in.at[1], T3_DN, dn3), place == 0, place == 3),
        DQ_DN: (copy(dqn_out, dqn_in, DQ_DN, dn1), earlier, later),
        DA_DN: (copy(dan_out, dan_in, DA_DN, dn1), earlier, later),
    }

    def send(*which, places=always):
        for message in which:
            description, senders, _ = messages[message]
            pl.when(senders & places)(description.start)

    def sent(message):
        description, senders, _ = messages[message]
        pl.when(senders)(description.wait_send)

    def received(*which, places=always):
        for message in which:
            description, _, getters = messages[message]
            pl.when(getters & places)(description.wait_recv)

    eight = place * 2 + core

    def octet(hop):
        other = lax.rem(eight + hop, 8)
        return {"dp": (z * y_size + y) * 2 + other % 2, "seq": other // 2}

    def along_y(hop):
        return {"dp": (z * y_size + lax.rem(y + hop, y_size)) * 2 + core, "seq": place}

    def along_z(hop):
        return {"dp": (lax.rem(z + hop, z_size) * y_size + y) * 2 + core, "seq": place}

    barrier = pltpu.get_barrier_semaphore()
    partners = 0
    ring = z_size == 8
    near = (1, z_size - 1) if ring else range(1, z_size)
    for where, hops in ((octet, range(1, 8)), (along_y, range(1, y_size)), (along_z, near)):
        for hop in hops:
            pl.semaphore_signal(barrier, inc=1, device_id=where(hop), device_id_type=MESH)
            partners += 1

    def tell(index, hop):
        if ring:
            pl.semaphore_signal(ring_sem.at[index], inc=1, device_id=along_z(hop), device_id_type=MESH)

    def told(index):
        if ring:
            pl.semaphore_wait(ring_sem.at[index], 1)

    @pl.when(place == last)
    def _():
        qn[...] = jnp.zeros_like(qn)
        gn[...] = jnp.zeros_like(gn)
        lbuf[pl.ds(2 * BLOCK, BLOCK), :] = jnp.zeros((BLOCK, LANES), F32)
        s1_in[...] = jnp.zeros_like(s1_in)

    @pl.when(place >= 2)
    def _():
        ss_in[0] = jnp.zeros(ss_in.shape[1:], BF16)

    @pl.when(place >= 1)
    def _():
        ss_in[1] = jnp.zeros(ss_in.shape[1:], BF16)

    @pl.when(place != last)
    def _():
        t_in[...] = jnp.zeros_like(t_in)

    @pl.when(place == 0)
    def _():
        p_in[...] = jnp.zeros_like(p_in)
        r_in[...] = jnp.zeros_like(r_in)
        dqn_in[...] = jnp.zeros_like(dqn_in)
        dan_in[...] = jnp.zeros_like(dan_in)

    row, col = iota((LANES, LANES), 0), iota((LANES, LANES), 1)
    same = (row // BLOCK) == (col // BLOCK)
    tri = flag(same & (col <= row))
    head_row = iota((LANES, WIDTH), 0)
    head_lane = iota((LANES, WIDTH), 1) // BLOCK
    spread = flag(head_row == head_lane)
    spread_gate = flag(head_row == head_lane + HEADS)
    spread_pieces = flag(head_row % 32 == head_lane)
    head_lanes = iota((BLOCK, LANES), 1) < HEADS
    left = iota((BLOCK, LANES), 1) < BLOCK
    left1 = iota((1, LANES), 1) < BLOCK
    srow, scol = iota((BLOCK, BLOCK), 0), iota((BLOCK, BLOCK), 1)
    upper_in = flag(scol >= srow)
    lower = flag(scol < srow)
    at_or_before = flag(scol <= srow)
    after = flag(scol > srow)

    loads[0].wait()
    loads[1].wait()
    loads[2].wait()
    w_hi, w_lo = pieces(w_ref[...], 2)
    no_rows = jnp.zeros((32, WIDTH), BF16)
    x = x_ref[...]
    logits = nt(x, jnp.concatenate([w_hi, no_rows, w_lo, no_rows], axis=0))
    logits = logits + jnp.concatenate([logits[:, BLOCK:], logits[:, :BLOCK]], axis=1)
    small = jnp.exp(-jnp.abs(logits))
    soft = jnp.maximum(logits, 0.0) + jnp.log1p(small)
    sig = jnp.where(logits >= 0.0, 1.0, small) / (1.0 + small)
    rate = jnp.concatenate([rate_ref[...], jnp.zeros((1, LANES - HEADS), F32)], axis=1)
    decay = -rate * soft
    gamma = sig * (1.0 / BLOCK)
    log_own = sum(nn(tri, part) for part in pieces(decay, 3))
    lbuf[pl.ds(0, LANES), :] = log_own
    tot[...] = jnp.zeros_like(tot)
    tot[0:1, :] = log_own[BLOCK - 1 : BLOCK]
    tot[1:2, :] = log_own[LANES - 1 :]

    for load in loads[3:]:
        load.wait()
    pl.semaphore_wait(barrier, partners)
    send(L_UP, TOT1, TOT2, TOT3)
    send(Q_UP, G_UP)
    tell(0, 1)
    tell(1, z_size - 1)

    def beside(a):
        parts = [part[:, :32] for part in pieces(a, 3)]
        return jnp.concatenate(parts + [jnp.zeros((a.shape[0], 32), BF16)], axis=1)

    def expand(a):
        return nn(beside(a), spread_pieces)

    def block_rows(logs, block, offset):
        pick = flag(row == (col % BLOCK) + offset)
        turned = sum(tn(part, pick) for part in pieces(logs, 3))
        for pair in range(PAIRS):
            lrow[block : block + 1, pl.ds(pair * LANES, LANES)] = jnp.where(
                left1, turned[2 * pair : 2 * pair + 1], turned[2 * pair + 1 : 2 * pair + 2]
            )

    tail0 = jnp.exp(log_own[BLOCK - 1 : BLOCK] - log_own[:BLOCK])
    tail1 = jnp.exp(log_own[LANES - 1 :] - log_own[BLOCK:])

    def twice(mask, a):
        return nn(
            jnp.concatenate([mask, mask], axis=1), jnp.concatenate(pieces(a, 2), axis=0)
        )

    def ending(mask, tail):
        return jnp.where(head_lanes, twice(mask, tail), 0.0)

    gamma_first = jnp.concatenate([gamma[:, HEADS:32], jnp.zeros((LANES, LANES - HEADS), F32)], axis=1)
    expanded = expand(
        jnp.concatenate(
            [log_own, gamma_first, ending(upper_in, tail0), ending(lower, tail1), ending(upper_in, tail1)],
            axis=0,
        )
    )
    lx[pl.ds(0, LANES), :] = expanded[:LANES]
    gamma_x[...] = expanded[LANES : 2 * LANES]
    blast_x[pl.ds(0, 3 * BLOCK), :] = expanded[2 * LANES :]

    def each_pair(step, begin=0, end=PAIRS):
        lax.fori_loop(begin, end, step, 0, unroll=end - begin)

    def together(step, group=GROUP):
        def several(index, carry):
            step([index * group + offset for offset in range(group)])
            return carry

        return several

    def all_pairs(step, group=WIDE):
        each_pair(together(step, group), 0, PAIRS // group)

    def lanes_of(pair):
        return pl.ds(pl.multiple_of(pair * LANES, LANES), LANES)

    def phi(raw, coef):
        value = raw.astype(F32)
        return 0.125 * (value + coef * value * value)

    def compact(full):
        return jnp.where(left, full[:BLOCK], full[BLOCK:])

    def diagonal(value):
        none = jnp.zeros_like(value)
        return jnp.concatenate([jnp.where(left, value, none), jnp.where(left, none, value)], axis=0)

    def weighted(a, weights):
        return (a.astype(F32) * weights).astype(BF16)

    def own_step(pairs):
        ats = [lanes_of(pair) for pair in pairs]
        coefs = [coef_ref[:, at] for at in ats]
        q_feat = [phi(q_ref[:, at], coef).astype(BF16) for at, coef in zip(ats, coefs)]
        keys = [
            (phi(k_ref[:, at], coef) * gamma_x[:, at]).astype(BF16) for at, coef in zip(ats, coefs)
        ]
        logs = [lx[pl.ds(0, LANES), at] for at in ats]
        scaled = [weighted(g_ref[:, at], jnp.exp(a)) for at, a in zip(ats, logs)]
        values = [v_ref[:, at] for at in ats]
        carried0 = [
            weighted(a[:BLOCK], blast_x[pl.ds(0, BLOCK), at]) for at, a in zip(ats, keys)
        ]
        carried1 = [weighted(a, blast_x[pl.ds(BLOCK, LANES), at]) for at, a in zip(ats, keys)]
        s0 = [compact(tn(a[:BLOCK], b[:BLOCK])) for a, b in zip(q_feat, scaled)]
        s1 = [compact(tn(a[BLOCK:], b[BLOCK:])) for a, b in zip(q_feat, scaled)]
        u0 = [compact(tn(a, b[:BLOCK])) for a, b in zip(carried0, values)]
        c1 = [compact(tn(a, b)) for a, b in zip(carried1, values)]
        for index, at in enumerate(ats):
            qf[pl.ds(0, LANES), at] = q_feat[index]
            wk[:, at] = keys[index]
            gq[:, at] = scaled[index]
            fall0 = jnp.exp(logs[index][BLOCK - 1 : BLOCK])
            fall1 = jnp.exp(logs[index][LANES - 1 :])
            s1_out[:, at] = s1[index].astype(BF16)
            ss_out[:, at] = (s0[index] + fall0 * s1[index]).astype(BF16)
            end = fall1 * u0[index] + c1[index]
            u0c[:, at] = u0[index]
            c1c[:, at] = end
            s1c[:, at] = s1[index]
            p_out[:, at] = end.astype(BF16)

    all_pairs(own_step)
    send(SS_UP, SS_ROUND, S_UP)
    send(P_DN, places=place != 1)

    block_rows(log_own, 0, 0)
    block_rows(log_own, 1, BLOCK)

    step = col % BLOCK
    cur_mask = flag(same & (row % BLOCK >= step))
    prev_mask = flag(same & (row % BLOCK < step))
    both_mask = jnp.concatenate([cur_mask, prev_mask], axis=1)
    causal = (iota((LANES, LANES), 1) % BLOCK) <= (iota((LANES, LANES), 0) % BLOCK)

    def spans(rows):
        return pl.ds(rows.start, rows.stop - rows.start)

    first_rows, last_rows = slice(0, BLOCK), slice(BLOCK, LANES)

    corner = iota((LANES, LANES), 0) < BLOCK, iota((LANES, LANES), 1) < BLOCK
    first_head, second_head = corner[0] & corner[1], ~corner[0] & ~corner[1]

    def turned_diagonals(rows):
        turned = rows.T
        swapped = jnp.concatenate([turned[:, BLOCK:], turned[:, :BLOCK]], axis=1)
        none = jnp.zeros_like(turned)
        return (
            jnp.where(first_head, turned, jnp.where(second_head, swapped, none)),
            jnp.where(first_head, swapped, jnp.where(second_head, turned, none)),
        )

    def tiles(keys_bd, keys_t, values_t, queries, grads, kernels):
        scores = [nn(a, b) for a, b in zip(queries, keys_t)]
        d_weights = [nn(a, b) for a, b in zip(grads, values_t)]
        weights = [(a * b).astype(BF16) for a, b in zip(scores, kernels)]
        d_scores = [(a * b).astype(BF16) for a, b in zip(d_weights, kernels)]
        d_kernels = [(a * b).astype(BF16) for a, b in zip(d_weights, scores)]
        d_queries = [nn(a, b) for a, b in zip(d_scores, keys_bd)]
        d_values = [compact(tn(a, b)) for a, b in zip(weights, grads)]
        d_keys = [compact(tn(a, b)) for a, b in zip(d_scores, queries)]
        return d_queries, d_values, d_keys, d_kernels

    def window_step(pairs):
        ats = [lanes_of(pair) for pair in pairs]
        keys = [wk[:, at] for at in ats]
        values = [v_ref[:, at] for at in ats]
        queries = [qf[pl.ds(0, LANES), at] for at in ats]
        grads = [g_ref[:, at] for at in ats]
        rows = [
            jnp.concatenate(
                [jnp.broadcast_to(lrow[b : b + 1, at], (BLOCK, LANES)) for b in range(2)], axis=0
            )
            for at in ats
        ]
        decays = [
            jnp.exp(jnp.where(causal, lx[pl.ds(0, LANES), at] - row, NEVER))
            for at, row in zip(ats, rows)
        ]
        low = [a.astype(BF16) for a in decays]
        start = [nn(a[:BLOCK], cur_mask) for a in low]
        middle = [nn(a[BLOCK:], both_mask) for a in low]
        keys_t = [turned_diagonals(a) for a in keys]
        values_t = [turned_diagonals(a) for a in values]
        for pair, a, b in zip(pairs, keys_t, values_t):
            keys_held[pair] = a[1]
            values_held[pair] = b[1]
        dq0, dv0, dk0, db0 = tiles(
            [diagonal(a[:BLOCK]) for a in keys], [a[0] for a in keys_t], [a[0] for a in values_t],
            queries, grads,
            [jnp.concatenate([a, b[:, LANES:]], axis=0) for a, b in zip(start, middle)],
        )
        dq1, dv1, dk1, db1 = tiles(
            [diagonal(a[BLOCK:]) for a in keys], [a[1] for a in keys_t], [a[1] for a in values_t],
            [a[BLOCK:] for a in queries], [a[BLOCK:] for a in grads], [a[:, :LANES] for a in middle],
        )
        d_decays = [
            jnp.concatenate(
                [
                    nt(a[:BLOCK], cur_mask),
                    nt(jnp.concatenate([b, a[BLOCK:]], axis=1), both_mask),
                ],
                axis=0,
            )
            for a, b in zip(db0, db1)
        ]
        for index, at in enumerate(ats):
            dvf[pl.ds(0, BLOCK), at] = dv0[index]
            dvf[pl.ds(BLOCK, BLOCK), at] = dv1[index]
            dwk[pl.ds(0, BLOCK), at] = dk0[index]
            dwk[pl.ds(BLOCK, BLOCK), at] = dk1[index]
            dqf[pl.ds(0, BLOCK), at] = dq0[index][:BLOCK]
            dqf[pl.ds(BLOCK, BLOCK), at] = dq0[index][BLOCK:] + dq1[index]
            gmat[pl.ds(0, LANES), at] = (d_decays[index] * decays[index]).astype(BF16)

    each_pair(together(window_step), 0, PAIRS // GROUP // 2)

    received(L_UP)
    log_next = lbuf[pl.ds(2 * BLOCK, BLOCK), :]
    tail2 = jnp.exp(log_next[BLOCK - 1 :] - log_next)
    expanded = expand(jnp.concatenate([log_next, ending(lower, tail2)], axis=0))
    lx[pl.ds(LANES, BLOCK), :] = expanded[:BLOCK]
    blast_x[pl.ds(3 * BLOCK, BLOCK), :] = expanded[BLOCK:]

    def next_step(pairs):
        ats = [lanes_of(pair) for pair in pairs]
        carried = [
            weighted(wk[pl.ds(BLOCK, BLOCK), at], blast_x[pl.ds(3 * BLOCK, BLOCK), at]) for at in ats
        ]
        entering = [
            compact(tn(a, v_ref[pl.ds(BLOCK, BLOCK), at])) for a, at in zip(carried, ats)
        ]
        for r, at in zip(entering, ats):
            fall2 = jnp.exp(lx[3 * BLOCK - 1 : 3 * BLOCK, at])
            r_out[:, at] = r.astype(BF16)
            t_out[:, at] = (fall2 * c1c[:, at] + r).astype(BF16)

    all_pairs(next_step)
    send(T2_DN, T3_DN, R_DN)

    told(0)
    told(1)
    tell(2, 1)
    tell(3, z_size - 1)
    each_pair(together(window_step), PAIRS // GROUP // 2, PAIRS // GROUP)
    told(2)
    told(3)
    tell(4, 1)
    own0 = jnp.exp(lx[BLOCK - 1 : BLOCK, :])
    own1 = jnp.exp(lx[LANES - 1 : LANES, :])

    @pl.when(place == 0)
    def _():
        messages[SS_UP][0].wait_recv()
        messages[SS_ON][0].start()

    @pl.when(place == last)
    def _():
        messages[SS_ROUND][0].wait_recv()
        messages[SS_BACK][0].start()

    @pl.when(place == 1)
    def _():
        messages[P_DN][0].wait_recv()
        messages[R_DN][0].wait_recv()
        entered = own0 * p_in[...].astype(F32) + r_in[...].astype(F32)
        p_out[...] = (c1c[...] + own1 * entered).astype(BF16)
        messages[P_DN][0].start()

    block_rows(lbuf[pl.ds(BLOCK, LANES), :], 2, BLOCK)

    received(Q_UP, G_UP)

    def cross_step(pairs):
        ats = [lanes_of(pair) for pair in pairs]
        queries = [phi(qn[:, at], coef_ref[:, at]).astype(BF16) for at in ats]
        grads = [gn[:, at] for at in ats]
        logs = [lx[pl.ds(LANES, BLOCK), at] for at in ats]
        decays = [
            jnp.exp(jnp.where(causal[:BLOCK], a - lrow[2:3, at], NEVER)) for at, a in zip(ats, logs)
        ]
        d_queries, d_values, d_keys, d_kernels = tiles(
            [diagonal(wk[pl.ds(BLOCK, BLOCK), at]) for at in ats],
            [keys_held[pair] for pair in pairs], [values_held[pair] for pair in pairs],
            queries, grads, [nn(a.astype(BF16), prev_mask) for a in decays],
        )
        entering = [
            compact(tn(a, weighted(b, jnp.exp(c)))) for a, b, c in zip(queries, grads, logs)
        ]
        d_decays = [nt(a, prev_mask) for a in d_kernels]
        for index, at in enumerate(ats):
            dqn_out[:, at] = d_queries[index].astype(BF16)
            raw = qn[:, at].astype(F32)
            coef_sum[1:2, at] = jnp.sum(
                d_queries[index] * (0.125 * raw * raw), axis=0, keepdims=True
            )
            dvf[pl.ds(BLOCK, BLOCK), at] = dvf[pl.ds(BLOCK, BLOCK), at] + d_values[index]
            dwk[pl.ds(BLOCK, BLOCK), at] = dwk[pl.ds(BLOCK, BLOCK), at] + d_keys[index]
            gmat[pl.ds(LANES, BLOCK), at] = (d_decays[index] * decays[index]).astype(BF16)
            c1c[:, at] = entering[index]

    each_pair(together(cross_step), 0, PAIRS // GROUP)
    send(DQ_DN)

    upper_both = flag(same & (col >= row))
    later_sums = jnp.concatenate(
        [
            nn(upper_both, gmat[pl.ds(0, LANES), :]),
            nn(upper_in, gmat[pl.ds(LANES, BLOCK), :]),
        ],
        axis=0,
    )
    before = (iota((3 * BLOCK, WIDTH), 1) % BLOCK) < (iota((3 * BLOCK, WIDTH), 0) % BLOCK)
    window_grads = nt(jnp.where(before, later_sums, 0.0).astype(BF16), spread)

    received(TOT1, S_UP, TOT2, SS_ON, SS_BACK, TOT3)
    falls = expand(jnp.concatenate([tot_in[slot] for slot in range(3)], axis=0))
    falls = [falls[8 * slot : 8 * slot + 8] for slot in range(3)]
    next1_fall1 = jnp.exp(falls[0][1:2])
    next2_all = jnp.exp(falls[1][0:1] + falls[1][1:2])
    prev1_fall1 = jnp.exp(falls[2][1:2])
    prev1_all = jnp.exp(falls[2][0:1] + falls[2][1:2])
    prev2_fall1 = jnp.exp(falls[1][1:2])
    next0 = jnp.exp(lx[3 * BLOCK - 1 :, :])
    z_grad = s1_in[...].astype(F32) + next1_fall1 * (
        ss_in[0].astype(F32) + next2_all * ss_in[1].astype(F32)
    )
    z_end[...] = z_grad.astype(BF16)
    end_grad = next0 * z_grad + c1c[...]
    mid_grad = own1 * end_grad + s1c[...]
    n_end[...] = end_grad.astype(BF16)
    n_mid[...] = mid_grad.astype(BF16)

    def enter(index, keys, d_role, at):
        weights = blast_x[pl.ds(index * BLOCK, BLOCK), at]
        own_keys = keys.astype(F32)
        xmat[pl.ds(index * BLOCK, BLOCK), at] = (d_role * own_keys).astype(BF16)
        return (own_keys * weights).astype(BF16), d_role * weights

    def outer_step(pairs):
        ats = [lanes_of(pair) for pair in pairs]
        rows = pl.ds(BLOCK, BLOCK)
        grads = [diagonal(z_end[:, at]) for at in ats]
        d_roles = [nt(v_ref[rows, at], a) for at, a in zip(ats, grads)]
        entered = [enter(3, wk[rows, at], a, at) for at, a in zip(ats, d_roles)]
        d_values = [nn(a[0], b) for a, b in zip(entered, grads)]
        for at, a, b in zip(ats, entered, d_values):
            dwk[rows, at] = dwk[rows, at] + a[1]
            dvf[rows, at] = dvf[rows, at] + b

    all_pairs(outer_step)
    d_last = nt(xmat[pl.ds(3 * BLOCK, BLOCK), :], spread)
    dan_out[...] = window_grads[LANES:] + twice(lower, twice(after, d_last) * tail2)
    send(DA_DN)

    def inner_step(pairs):
        ats = [lanes_of(pair) for pair in pairs]
        keys = [wk[:, at] for at in ats]
        values = [v_ref[:, at] for at in ats]
        ends = [diagonal(n_end[:, at]) for at in ats]
        both = [
            jnp.concatenate([diagonal(n_mid[:, at]), a], axis=0) for at, a in zip(ats, ends)
        ]
        d_first = [nt(a[:BLOCK], b) for a, b in zip(values, both)]
        d_second = [nt(a[BLOCK:], b) for a, b in zip(values, ends)]
        enter0 = [enter(0, a[:BLOCK], b[:, :LANES], at) for a, b, at in zip(keys, d_first, ats)]
        enter1 = [enter(1, a[:BLOCK], b[:, LANES:], at) for a, b, at in zip(keys, d_first, ats)]
        enter2 = [enter(2, a[BLOCK:], b, at) for a, b, at in zip(keys, d_second, ats)]
        dv0 = [
            nn(jnp.concatenate([a[0], b[0]], axis=1), c) for a, b, c in zip(enter0, enter1, both)
        ]
        dv1 = [nn(a[0], b) for a, b in zip(enter2, ends)]
        for index, at in enumerate(ats):
            dv_ref[:, at] = (
                dvf[:, at] + jnp.concatenate([dv0[index], dv1[index]], axis=0)
            ).astype(BF16)
            d_keys = dwk[:, at] + jnp.concatenate(
                [enter0[index][1] + enter1[index][1], enter2[index][1]], axis=0
            )
            coef = coef_ref[:, at]
            raw = k_ref[:, at].astype(F32)
            d_feat = d_keys * gamma_x[:, at]
            square = 0.125 * raw * raw
            xmat[pl.ds(6 * BLOCK, LANES), at] = (
                d_keys * (0.125 * raw + coef * square)
            ).astype(BF16)
            dk_ref[:, at] = (d_feat * (0.125 + (0.25 * coef) * raw)).astype(BF16)
            coef_sum[0:1, at] = jnp.sum(d_feat * square, axis=0, keepdims=True)

    all_pairs(inner_step)
    stores[1].start()
    stores[2].start()
    d_enter = nt(xmat[pl.ds(0, 3 * BLOCK), :], spread)
    d_gamma = nt(xmat[pl.ds(6 * BLOCK, LANES), :], spread_gate)
    entered0 = twice(at_or_before, d_enter[:BLOCK])
    entered1 = nn(
        jnp.concatenate([at_or_before, at_or_before, after, after], axis=1),
        jnp.concatenate(pieces(d_enter[2 * BLOCK :], 2) + pieces(d_enter[BLOCK : 2 * BLOCK], 2), axis=0),
    )
    lower_both = flag(same & (col < row))
    d_decay = window_grads[:LANES] + twice(
        lower_both, jnp.concatenate([entered0 * tail0, entered1 * tail1], axis=0)
    )

    received(P_DN, R_DN, places=place != 1)
    received(T2_DN, T3_DN)
    memory = (
        p_in[...].astype(F32)
        + prev1_fall1 * t_in[0].astype(F32)
        + (prev2_fall1 * prev1_all) * t_in[1].astype(F32)
    )
    middle_memory = own0 * memory + r_in[...].astype(F32) + u0c[...]
    m_in[...] = memory.astype(BF16)
    m_mid[...] = middle_memory.astype(BF16)
    fall_grad = jnp.concatenate(
        [
            own0 * jnp.sum(memory * mid_grad, axis=0, keepdims=True),
            own1 * jnp.sum(middle_memory * end_grad, axis=0, keepdims=True),
            jnp.zeros((6, WIDTH), F32),
        ],
        axis=0,
    )
    fall_grad = sum(nt(part, spread) for part in pieces(fall_grad, 2))

    def query_step(pairs):
        ats = [lanes_of(pair) for pair in pairs]
        scaled = [gq[:, at] for at in ats]
        carried = [
            jnp.concatenate(
                [
                    nt(a[:BLOCK], diagonal(m_in[:, at])),
                    nt(a[BLOCK:], diagonal(m_mid[:, at])),
                ],
                axis=0,
            )
            for a, at in zip(scaled, ats)
        ]
        for a, at in zip(carried, ats):
            xmat[pl.ds(4 * BLOCK, LANES), at] = (
                a * qf[pl.ds(0, LANES), at].astype(F32)
            ).astype(BF16)
            raw = q_ref[:, at].astype(F32)
            d_feat = dqf[:, at] + a
            dqf[:, at] = d_feat
            coef_sum[0:1, at] = (
                coef_sum[0:1, at]
                + coef_sum[1:2, at]
                + jnp.sum(d_feat * (0.125 * raw * raw), axis=0, keepdims=True)
            )

    all_pairs(query_step)
    d_out = nt(xmat[pl.ds(4 * BLOCK, LANES), :], spread)
    d_decay = d_decay + twice(upper_both, d_out)
    received(DA_DN)
    d_decay = d_decay + jnp.concatenate(
        [
            dan_in[...] + fall_grad[0:1],
            jnp.broadcast_to(fall_grad[1:2], (BLOCK, LANES)),
        ],
        axis=0,
    )
    is_decay = iota((LANES, LANES), 1) < HEADS
    d_logits = jnp.where(is_decay, -rate * sig * d_decay, d_gamma * gamma * (1.0 - sig))
    rates = jnp.sum(jnp.where(is_decay, -soft * d_decay, 0.0), axis=0, keepdims=True)
    gate = nn(jnp.concatenate(pieces(d_logits.T[:32], 2), axis=0), x)
    gate = gate[:32] + gate[32:]

    def paired(rows):
        high = rows.astype(BF16).astype(F32)
        return jnp.concatenate([high, rows - high], axis=0).astype(BF16)

    no_rates = jnp.zeros((1, LANES), F32)
    for chunk in range(8):
        at = slice(chunk * LANES, (chunk + 1) * LANES)
        mine[chunk, 0:32, :] = gate[:32, at].astype(BF16)
        mine[chunk, 32:TALL, :] = paired(
            jnp.concatenate(
                [
                    coef_sum[0:1, at],
                    rates if chunk == 0 else no_rates,
                    jnp.zeros((6, LANES), F32),
                ],
                axis=0,
            )
        )

    def exchange(base, size, where, source, target, reach=1):
        made = [
            pltpu.make_async_remote_copy(
                src_ref=source(hop),
                dst_ref=target,
                send_sem=sum_send.at[base + hop],
                recv_sem=sum_recv.at[base + hop],
                device_id=where(hop),
                device_id_type=MESH,
            )
            for hop in sorted(range(1, size), key=lambda hop: -min(hop // reach, (size - hop) // reach))
        ]
        for one in made:
            one.start()
        return made

    def added(buffer, count):
        total = buffer[0].astype(F32)
        for index in range(1, count):
            total = total + buffer[index].astype(F32)
        return jnp.concatenate(
            [total[:32].astype(BF16), paired(total[32:40] + total[40:])], axis=0
        )

    made = exchange(0, 8, octet, lambda hop: mine.at[lax.rem(eight + hop, 8)], first.at[eight], 2)
    first[eight] = mine[eight]
    d_hi, d_lo = [part[:, :32] for part in pieces(d_logits, 2)]
    dx_ref[...] = nn(
        jnp.concatenate([d_hi, d_lo, d_hi, jnp.zeros((LANES, 32), BF16)], axis=1),
        jnp.concatenate([w_hi, w_hi, w_lo, no_rows], axis=0),
    ).astype(BF16)
    stores[3].start()
    received(DQ_DN)

    def last_step(pair, carry):
        at = lanes_of(pair)
        raw = q_ref[:, at].astype(F32)
        d_feat = dqf[:, at] + jnp.concatenate(
            [dqn_in[:, at].astype(F32), jnp.zeros((BLOCK, LANES), F32)], axis=0
        )
        dq_ref[:, at] = (d_feat * (0.125 + (0.25 * coef_ref[:, at]) * raw)).astype(BF16)
        return carry

    each_pair(last_step)
    stores[0].start()
    for one in made:
        one.wait_recv()
    second[y] = added(first, 8)
    more = exchange(8, y_size, along_y, lambda hop: second.at[y], second.at[y])
    for one in more:
        one.wait_recv()
    made += more
    third[z] = added(second, y_size)
    told(4)
    more = exchange(8 + y_size, z_size, along_z, lambda hop: third.at[z], third.at[z])
    for one in more:
        one.wait_recv()
    made += more
    done[...] = added(third, z_size)
    own = pltpu.make_async_copy(done, done_hbm.at[eight], store_sem.at[4])
    own.start()
    more = exchange(
        8 + y_size + z_size, 8, octet, lambda hop: done, done_hbm.at[eight], 2
    )
    for message in range(MESSAGES):
        sent(message)
    for store in stores:
        store.wait()
    own.wait()
    for one in made:
        one.wait_send()
    for one in more:
        one.wait()


def main_call(sizes, queries, keys, values, inputs, gate, coef, rate, cotangent):
    z_size, y_size = sizes
    rows = queries.shape[0]
    anywhere = pl.BlockSpec(memory_space=pltpu.HBM)
    block, full = (BLOCK, WIDTH), (LANES, WIDTH)
    out = jax.ShapeDtypeStruct((rows, WIDTH), BF16)
    tile = (TALL, LANES)
    scratch = [
        (full, BF16), (full, BF16), (full, BF16), (full, BF16), (full, BF16),
        (gate.shape, F32), (coef.shape, F32), (rate.shape, F32),
        (full, BF16), (full, BF16), (full, BF16), (full, BF16),
        (block, BF16), (block, BF16), ((3 * BLOCK, LANES), F32), ((8, LANES), F32), ((3, 8, LANES), F32),
        (block, BF16), (block, BF16), (block, BF16), (block, BF16), ((2,) + block, BF16),
        (block, BF16), (block, BF16), (block, BF16), (block, BF16), (block, BF16), ((2,) + block, BF16),
        (block, BF16), (block, BF16), ((BLOCK, LANES), F32), ((BLOCK, LANES), F32),
        ((8, WIDTH), F32), ((3 * BLOCK, WIDTH), F32), (full, F32), ((4 * BLOCK, WIDTH), F32),
        (full, BF16), (full, BF16), (full, BF16),
        (block, F32), (block, F32), (block, F32),
        (block, BF16), (block, BF16), (block, BF16), (block, BF16), (block, BF16),
        (full, F32), (full, F32), (full, F32),
        ((3 * BLOCK, WIDTH), BF16), ((8 * BLOCK, WIDTH), BF16), ((8, WIDTH), F32),
        ((PAIRS, LANES, LANES), BF16), ((PAIRS, LANES, LANES), BF16),
        ((8,) + tile, BF16), ((8,) + tile, BF16), ((y_size,) + tile, BF16), ((z_size,) + tile, BF16),
        (tile, BF16),
    ]
    count = 16 + y_size + z_size
    return pl.pallas_call(
        functools.partial(main_kernel, z_size, y_size),
        out_shape=[out, out, out, out, jax.ShapeDtypeStruct((8,) + tile, BF16)],
        in_specs=[anywhere] * 8,
        out_specs=[anywhere] * 5,
        scratch_shapes=[pltpu.VMEM(shape, dtype) for shape, dtype in scratch]
        + [
            pltpu.SemaphoreType.DMA((number,))
            for number in (LOADS, STORES, MESSAGES, MESSAGES, count, count)
        ]
        + [pltpu.SemaphoreType.REGULAR((5,))],
        compiler_params=pltpu.CompilerParams(
            collective_id=0, has_side_effects=True, vmem_limit_bytes=56 * 2**20
        ),
        name="window_backward",
    )(queries, keys, values, inputs, gate, coef, rate, cotangent)


def hand_out_kernel(*refs):
    sources, targets, held = refs[:5], refs[5:12], refs[12:20]
    load_sem, store_sem = refs[20:]
    loads = [
        pltpu.make_async_copy(sources[index], held[index], load_sem.at[index]) for index in range(5)
    ]
    stores = [
        pltpu.make_async_copy(held[index if index < 4 else index + 1], targets[index], store_sem.at[index])
        for index in range(7)
    ]
    for load in loads[::-1]:
        load.start()
    done, gate, coef, rate = held[4:]
    loads[4].wait()
    for chunk in range(8):
        at = slice(chunk * LANES, (chunk + 1) * LANES)
        total = done[chunk].astype(F32)
        gate[:, at] = total[:32]
        rest = total[32:40] + total[40:]
        coef[:, at] = rest[0:1]
        if chunk == 0:
            rate[...] = rest[1:2, :HEADS]
    for store in stores[4:]:
        store.start()
    for index in range(3, -1, -1):
        loads[index].wait()
        stores[index].start()
    for store in stores:
        store.wait()


def hand_out(results):
    anywhere = pl.BlockSpec(memory_space=pltpu.HBM)
    params = [jax.ShapeDtypeStruct(shape, F32) for shape in ((32, WIDTH), (1, WIDTH), (1, HEADS))]
    shapes = [jax.ShapeDtypeStruct(a.shape, a.dtype) for a in results]
    return pl.pallas_call(
        hand_out_kernel,
        out_shape=shapes[:4] + params,
        in_specs=[anywhere] * 5,
        out_specs=[anywhere] * 7,
        scratch_shapes=[pltpu.VMEM(a.shape, a.dtype) for a in shapes + params]
        + [pltpu.SemaphoreType.DMA((5,)), pltpu.SemaphoreType.DMA((7,))],
        compiler_params=pltpu.CompilerParams(vmem_limit_bytes=56 * 2**20),
        name="hand_out",
    )(*results)


def on_device(sizes, queries, keys, values, inputs, gate, coef, rate, cotangent):
    results = main_call(
        sizes,
        queries[0], keys[0], values[0], inputs[0], gate.T, coef[None], rate[None], cotangent[0],
    )
    dq, dk, dv, dx, d_gate, d_coef, d_rate = hand_out(results)
    return (dq[None], dk[None], dv[None], dx[None], d_gate.T, d_coef[0], d_rate[0])


def solution(mesh):
    rows = P("dp", "seq", None)
    y_size = min(4, max(1, mesh.shape["dp"] // 2))
    sizes = (mesh.shape["dp"] // (2 * y_size), y_size)
    return jax.shard_map(
        functools.partial(on_device, sizes),
        mesh=mesh,
        in_specs=(rows, rows, rows, rows, P(), P(), P(), rows),
        out_specs=(rows, rows, rows, rows, P(), P(), P()),
        check_vma=False,
    )
```

```python
import functools

import jax
import jax.numpy as jnp
from jax import lax
from jax.experimental import pallas as pl
from jax.experimental.pallas import tpu as pltpu
from jax.sharding import PartitionSpec as P

BLOCK = 64
LANES = 128
WIDTH = 1024
PAIRS = WIDTH // LANES
HEADS = 16
F32 = jnp.float32
BF16 = jnp.bfloat16
MESH = pl.DeviceIdType.MESH


def nn(a, b):
    return lax.dot_general(a, b, (((1,), (0,)), ((), ())), preferred_element_type=F32)


def nt(a, b):
    return lax.dot_general(a, b, (((1,), (1,)), ((), ())), preferred_element_type=F32)


def tn(a, b):
    return lax.dot_general(a, b, (((0,), (0,)), ((), ())), preferred_element_type=F32)


def pieces(a, count):
    parts = []
    for _ in range(count):
        part = a.astype(BF16)
        parts.append(part)
        a = a - part.astype(F32)
    return parts


def flag(condition):
    return jnp.where(condition, 1.0, 0.0).astype(BF16)


def iota(shape, dimension):
    return lax.broadcasted_iota(jnp.int32, shape, dimension)


Q_UP, G_UP, L_UP, S_UP, SS_ROUND, SS_ON, SS_BACK, SS_UP, TOT1, TOT2, TOT3 = range(11)
P_DN, R_DN, T2_DN, T3_DN, DQ_DN, DA_DN = range(11, 17)
MESSAGES = 17
LOADS = 8
STORES = 5
TALL = 48
NEVER = -1e30
WIDE = 8
GROUP = 4


def main_kernel(
    z_size, y_size,
    q_hbm, k_hbm, v_hbm, x_hbm, w_hbm, coef_hbm, rate_hbm, g_hbm,
    dq_hbm, dk_hbm, dv_hbm, dx_hbm, done_hbm,
    q_ref, k_ref, v_ref, x_ref, g_ref, w_ref, coef_ref, rate_ref,
    dq_ref, dk_ref, dv_ref, dx_ref,
    qn, gn, lbuf, tot, tot_in, s1_out, ss_out, s1_in, ss_held, ss_in, p_out, r_out, t_out, p_in, r_in, t_in,
    dqn_out, dqn_in, dan_out, dan_in,
    lrow, lx, gamma_x, blast_x, qf, wk, gq, s1c, u0c, c1c, m_in, m_mid, n_mid, n_end, z_end,
    dqf, dwk, dvf, gmat, xmat, coef_sum, keys_held, values_held,
    mine, first, second, third, done,
    load_sem, store_sem, send_sem, recv_sem, sum_send, sum_recv, ring_sem,
):
    place, dp = lax.axis_index("seq"), lax.axis_index("dp")
    z, y, core = dp // (y_size * 2), (dp // 2) % y_size, dp % 2
    last = 3

    loads = [
        pltpu.make_async_copy(source, target, load_sem.at[index])
        for index, (source, target) in enumerate(
            (
                (x_hbm, x_ref), (w_hbm, w_ref), (rate_hbm, rate_ref), (coef_hbm, coef_ref),
                (k_hbm, k_ref), (q_hbm, q_ref), (v_hbm, v_ref), (g_hbm, g_ref),
            )
        )
    ]
    for load in loads:
        load.start()
    stores = [
        pltpu.make_async_copy(source, target, store_sem.at[index])
        for index, (source, target) in enumerate(
            ((dq_ref, dq_hbm), (dk_ref, dk_hbm), (dv_ref, dv_hbm), (dx_ref, dx_hbm))
        )
    ]

    def copy(source, target, message, to):
        return pltpu.make_async_remote_copy(
            src_ref=source,
            dst_ref=target,
            send_sem=send_sem.at[message],
            recv_sem=recv_sem.at[message],
            device_id={"seq": to},
            device_id_type=MESH,
        )

    up1, up3 = place - 1, place - 3
    dn1, dn2, dn3 = place + 1, place + 2, place + 3
    around = [lax.rem(place + 4 - hop, 4) for hop in (1, 2, 3)]
    always = place >= 0
    later, earlier = place >= 1, place < last
    messages = {
        Q_UP: (copy(q_ref.at[pl.ds(0, BLOCK)], qn, Q_UP, up1), later, earlier),
        G_UP: (copy(g_ref.at[pl.ds(0, BLOCK)], gn, G_UP, up1), later, earlier),
        L_UP: (
            copy(lbuf.at[pl.ds(0, BLOCK)], lbuf.at[pl.ds(2 * BLOCK, BLOCK)], L_UP, up1), later, earlier
        ),
        S_UP: (copy(s1_out, s1_in, S_UP, up1), later, earlier),
        SS_UP: (copy(ss_out, ss_in.at[1], SS_UP, up3), place == 3, place == 0),
        SS_ON: (copy(ss_in.at[1], ss_in.at[0], SS_ON, dn1), place == 0, place == 1),
        SS_ROUND: (copy(ss_out, ss_held, SS_ROUND, dn1), place == 2, place == 3),
        SS_BACK: (copy(ss_held, ss_in.at[0], SS_BACK, up3), place == 3, place == 0),
        TOT1: (copy(tot, tot_in.at[0], TOT1, around[0]), always, always),
        TOT2: (copy(tot, tot_in.at[1], TOT2, around[1]), always, always),
        TOT3: (copy(tot, tot_in.at[2], TOT3, around[2]), always, always),
        P_DN: (copy(p_out, p_in, P_DN, dn1), earlier, later),
        R_DN: (copy(r_out, r_in, R_DN, dn1), earlier, later),
        T2_DN: (copy(t_out, t_in.at[0], T2_DN, dn2), place == 1, place == 3),
        T3_DN: (copy(t_out, t_in.at[1], T3_DN, dn3), place == 0, place == 3),
        DQ_DN: (copy(dqn_out, dqn_in, DQ_DN, dn1), earlier, later),
        DA_DN: (copy(dan_out, dan_in, DA_DN, dn1), earlier, later),
    }

    def send(*which, places=always):
        for message in which:
            description, senders, _ = messages[message]
            pl.when(senders & places)(description.start)

    def sent(message):
        description, senders, _ = messages[message]
        pl.when(senders)(description.wait_send)

    def received(*which, places=always):
        for message in which:
            description, _, getters = messages[message]
            pl.when(getters & places)(description.wait_recv)

    eight = place * 2 + core

    def octet(hop):
        other = lax.rem(eight + hop, 8)
        return {"dp": (z * y_size + y) * 2 + other % 2, "seq": other // 2}

    def along_y(hop):
        return {"dp": (z * y_size + lax.rem(y + hop, y_size)) * 2 + core, "seq": place}

    def along_z(hop):
        return {"dp": (lax.rem(z + hop, z_size) * y_size + y) * 2 + core, "seq": place}

    barrier = pltpu.get_barrier_semaphore()
    partners = 0
    ring = z_size == 8
    near = (1, z_size - 1) if ring else range(1, z_size)
    for where, hops in ((octet, range(1, 8)), (along_y, range(1, y_size)), (along_z, near)):
        for hop in hops:
            pl.semaphore_signal(barrier, inc=1, device_id=where(hop), device_id_type=MESH)
            partners += 1

    def tell(index, hop):
        if ring:
            pl.semaphore_signal(ring_sem.at[index], inc=1, device_id=along_z(hop), device_id_type=MESH)

    def told(index):
        if ring:
            pl.semaphore_wait(ring_sem.at[index], 1)

    @pl.when(place == last)
    def _():
        qn[...] = jnp.zeros_like(qn)
        gn[...] = jnp.zeros_like(gn)
        lbuf[pl.ds(2 * BLOCK, BLOCK), :] = jnp.zeros((BLOCK, LANES), F32)
        s1_in[...] = jnp.zeros_like(s1_in)

    @pl.when(place >= 2)
    def _():
        ss_in[0] = jnp.zeros(ss_in.shape[1:], BF16)

    @pl.when(place >= 1)
    def _():
        ss_in[1] = jnp.zeros(ss_in.shape[1:], BF16)

    @pl.when(place != last)
    def _():
        t_in[...] = jnp.zeros_like(t_in)

    @pl.when(place == 0)
    def _():
        p_in[...] = jnp.zeros_like(p_in)
        r_in[...] = jnp.zeros_like(r_in)
        dqn_in[...] = jnp.zeros_like(dqn_in)
        dan_in[...] = jnp.zeros_like(dan_in)

    row, col = iota((LANES, LANES), 0), iota((LANES, LANES), 1)
    same = (row // BLOCK) == (col // BLOCK)
    tri = flag(same & (col <= row))
    head_row = iota((LANES, WIDTH), 0)
    head_lane = iota((LANES, WIDTH), 1) // BLOCK
    spread = flag(head_row == head_lane)
    spread_gate = flag(head_row == head_lane + HEADS)
    spread_pieces = flag(head_row % 32 == head_lane)
    head_lanes = iota((BLOCK, LANES), 1) < HEADS
    left = iota((BLOCK, LANES), 1) < BLOCK
    left1 = iota((1, LANES), 1) < BLOCK
    srow, scol = iota((BLOCK, BLOCK), 0), iota((BLOCK, BLOCK), 1)
    upper_in = flag(scol >= srow)
    lower = flag(scol < srow)
    at_or_before = flag(scol <= srow)
    after = flag(scol > srow)

    loads[0].wait()
    loads[1].wait()
    loads[2].wait()
    w_hi, w_lo = pieces(w_ref[...], 2)
    no_rows = jnp.zeros((32, WIDTH), BF16)
    x = x_ref[...]
    logits = nt(x, jnp.concatenate([w_hi, no_rows, w_lo, no_rows], axis=0))
    logits = logits + jnp.concatenate([logits[:, BLOCK:], logits[:, :BLOCK]], axis=1)
    small = jnp.exp(-jnp.abs(logits))
    soft = jnp.maximum(logits, 0.0) + jnp.log1p(small)
    sig = jnp.where(logits >= 0.0, 1.0, small) / (1.0 + small)
    rate = jnp.concatenate([rate_ref[...], jnp.zeros((1, LANES - HEADS), F32)], axis=1)
    decay = -rate * soft
    gamma = sig * (1.0 / BLOCK)
    log_own = sum(nn(tri, part) for part in pieces(decay, 3))
    lbuf[pl.ds(0, LANES), :] = log_own
    tot[...] = jnp.zeros_like(tot)
    tot[0:1, :] = log_own[BLOCK - 1 : BLOCK]
    tot[1:2, :] = log_own[LANES - 1 :]

    for load in loads[3:]:
        load.wait()
    pl.semaphore_wait(barrier, partners)
    send(L_UP, TOT1, TOT2, TOT3)
    send(Q_UP, G_UP)
    tell(0, 1)
    tell(1, z_size - 1)

    def beside(a):
        parts = [part[:, :32] for part in pieces(a, 3)]
        return jnp.concatenate(parts + [jnp.zeros((a.shape[0], 32), BF16)], axis=1)

    def expand(a):
        return nn(beside(a), spread_pieces)

    def block_rows(logs, block, offset):
        pick = flag(row == (col % BLOCK) + offset)
        turned = sum(tn(part, pick) for part in pieces(logs, 3))
        for pair in range(PAIRS):
            lrow[block : block + 1, pl.ds(pair * LANES, LANES)] = jnp.where(
                left1, turned[2 * pair : 2 * pair + 1], turned[2 * pair + 1 : 2 * pair + 2]
            )

    tail0 = jnp.exp(log_own[BLOCK - 1 : BLOCK] - log_own[:BLOCK])
    tail1 = jnp.exp(log_own[LANES - 1 :] - log_own[BLOCK:])

    def twice(mask, a):
        return nn(
            jnp.concatenate([mask, mask], axis=1), jnp.concatenate(pieces(a, 2), axis=0)
        )

    def ending(mask, tail):
        return jnp.where(head_lanes, twice(mask, tail), 0.0)

    gamma_first = jnp.concatenate([gamma[:, HEADS:32], jnp.zeros((LANES, LANES - HEADS), F32)], axis=1)
    expanded = expand(
        jnp.concatenate(
            [log_own, gamma_first, ending(upper_in, tail0), ending(lower, tail1), ending(upper_in, tail1)],
            axis=0,
        )
    )
    lx[pl.ds(0, LANES), :] = expanded[:LANES]
    gamma_x[...] = expanded[LANES : 2 * LANES]
    blast_x[pl.ds(0, 3 * BLOCK), :] = expanded[2 * LANES :]

    def each_pair(step, begin=0, end=PAIRS):
        lax.fori_loop(begin, end, step, 0, unroll=end - begin)

    def together(step, group=GROUP):
        def several(index, carry):
            step([index * group + offset for offset in range(group)])
            return carry

        return several

    def all_pairs(step, group=WIDE):
        each_pair(together(step, group), 0, PAIRS // group)

    def lanes_of(pair):
        return pl.ds(pl.multiple_of(pair * LANES, LANES), LANES)

    def phi(raw, coef):
        value = raw.astype(F32)
        return 0.125 * (value + coef * value * value)

    def compact(full):
        return jnp.where(left, full[:BLOCK], full[BLOCK:])

    def diagonal(value):
        none = jnp.zeros_like(value)
        return jnp.concatenate([jnp.where(left, value, none), jnp.where(left, none, value)], axis=0)

    def weighted(a, weights):
        return (a.astype(F32) * weights).astype(BF16)

    def own_step(pairs):
        ats = [lanes_of(pair) for pair in pairs]
        coefs = [coef_ref[:, at] for at in ats]
        q_feat = [phi(q_ref[:, at], coef).astype(BF16) for at, coef in zip(ats, coefs)]
        keys = [
            (phi(k_ref[:, at], coef) * gamma_x[:, at]).astype(BF16) for at, coef in zip(ats, coefs)
        ]
        logs = [lx[pl.ds(0, LANES), at] for at in ats]
        scaled = [weighted(g_ref[:, at], jnp.exp(a)) for at, a in zip(ats, logs)]
        values = [v_ref[:, at] for at in ats]
        carried0 = [
            weighted(a[:BLOCK], blast_x[pl.ds(0, BLOCK), at]) for at, a in zip(ats, keys)
        ]
        carried1 = [weighted(a, blast_x[pl.ds(BLOCK, LANES), at]) for at, a in zip(ats, keys)]
        s0 = [compact(tn(a[:BLOCK], b[:BLOCK])) for a, b in zip(q_feat, scaled)]
        s1 = [compact(tn(a[BLOCK:], b[BLOCK:])) for a, b in zip(q_feat, scaled)]
        u0 = [compact(tn(a, b[:BLOCK])) for a, b in zip(carried0, values)]
        c1 = [compact(tn(a, b)) for a, b in zip(carried1, values)]
        for index, at in enumerate(ats):
            qf[pl.ds(0, LANES), at] = q_feat[index]
            wk[:, at] = keys[index]
            gq[:, at] = scaled[index]
            fall0 = jnp.exp(logs[index][BLOCK - 1 : BLOCK])
            fall1 = jnp.exp(logs[index][LANES - 1 :])
            s1_out[:, at] = s1[index].astype(BF16)
            ss_out[:, at] = (s0[index] + fall0 * s1[index]).astype(BF16)
            end = fall1 * u0[index] + c1[index]
            u0c[:, at] = u0[index]
            c1c[:, at] = end
            s1c[:, at] = s1[index]
            p_out[:, at] = end.astype(BF16)

    all_pairs(own_step)
    send(SS_UP, SS_ROUND, S_UP)
    send(P_DN, places=place != 1)

    block_rows(log_own, 0, 0)
    block_rows(log_own, 1, BLOCK)

    step = col % BLOCK
    cur_mask = flag(same & (row % BLOCK >= step))
    prev_mask = flag(same & (row % BLOCK < step))
    both_mask = jnp.concatenate([cur_mask, prev_mask], axis=1)
    causal = (iota((LANES, LANES), 1) % BLOCK) <= (iota((LANES, LANES), 0) % BLOCK)

    def spans(rows):
        return pl.ds(rows.start, rows.stop - rows.start)

    first_rows, last_rows = slice(0, BLOCK), slice(BLOCK, LANES)

    corner = iota((LANES, LANES), 0) < BLOCK, iota((LANES, LANES), 1) < BLOCK
    first_head, second_head = corner[0] & corner[1], ~corner[0] & ~corner[1]

    def turned_diagonals(rows):
        turned = rows.T
        swapped = jnp.concatenate([turned[:, BLOCK:], turned[:, :BLOCK]], axis=1)
        none = jnp.zeros_like(turned)
        return (
            jnp.where(first_head, turned, jnp.where(second_head, swapped, none)),
            jnp.where(first_head, swapped, jnp.where(second_head, turned, none)),
        )

    def tiles(keys_bd, keys_t, values_t, queries, grads, kernels):
        scores = [nn(a, b) for a, b in zip(queries, keys_t)]
        d_weights = [nn(a, b) for a, b in zip(grads, values_t)]
        weights = [(a * b).astype(BF16) for a, b in zip(scores, kernels)]
        d_scores = [(a * b).astype(BF16) for a, b in zip(d_weights, kernels)]
        d_kernels = [(a * b).astype(BF16) for a, b in zip(d_weights, scores)]
        d_queries = [nn(a, b) for a, b in zip(d_scores, keys_bd)]
        d_values = [compact(tn(a, b)) for a, b in zip(weights, grads)]
        d_keys = [compact(tn(a, b)) for a, b in zip(d_scores, queries)]
        return d_queries, d_values, d_keys, d_kernels

    def window_step(pairs):
        ats = [lanes_of(pair) for pair in pairs]
        keys = [wk[:, at] for at in ats]
        values = [v_ref[:, at] for at in ats]
        queries = [qf[pl.ds(0, LANES), at] for at in ats]
        grads = [g_ref[:, at] for at in ats]
        rows = [
            jnp.concatenate(
                [jnp.broadcast_to(lrow[b : b + 1, at], (BLOCK, LANES)) for b in range(2)], axis=0
            )
            for at in ats
        ]
        decays = [
            jnp.exp(jnp.where(causal, lx[pl.ds(0, LANES), at] - row, NEVER))
            for at, row in zip(ats, rows)
        ]
        low = [a.astype(BF16) for a in decays]
        start = [nn(a[:BLOCK], cur_mask) for a in low]
        middle = [nn(a[BLOCK:], both_mask) for a in low]
        keys_t = [turned_diagonals(a) for a in keys]
        values_t = [turned_diagonals(a) for a in values]
        for pair, a, b in zip(pairs, keys_t, values_t):
            keys_held[pair] = a[1]
            values_held[pair] = b[1]
        dq0, dv0, dk0, db0 = tiles(
            [diagonal(a[:BLOCK]) for a in keys], [a[0] for a in keys_t], [a[0] for a in values_t],
            queries, grads,
            [jnp.concatenate([a, b[:, LANES:]], axis=0) for a, b in zip(start, middle)],
        )
        dq1, dv1, dk1, db1 = tiles(
            [diagonal(a[BLOCK:]) for a in keys], [a[1] for a in keys_t], [a[1] for a in values_t],
            [a[BLOCK:] for a in queries], [a[BLOCK:] for a in grads], [a[:, :LANES] for a in middle],
        )
        d_decays = [
            jnp.concatenate(
                [
                    nt(a[:BLOCK], cur_mask),
                    nt(jnp.concatenate([b, a[BLOCK:]], axis=1), both_mask),
                ],
                axis=0,
            )
            for a, b in zip(db0, db1)
        ]
        for index, at in enumerate(ats):
            dvf[pl.ds(0, BLOCK), at] = dv0[index]
            dvf[pl.ds(BLOCK, BLOCK), at] = dv1[index]
            dwk[pl.ds(0, BLOCK), at] = dk0[index]
            dwk[pl.ds(BLOCK, BLOCK), at] = dk1[index]
            dqf[pl.ds(0, BLOCK), at] = dq0[index][:BLOCK]
            dqf[pl.ds(BLOCK, BLOCK), at] = dq0[index][BLOCK:] + dq1[index]
            gmat[pl.ds(0, LANES), at] = (d_decays[index] * decays[index]).astype(BF16)


    received(L_UP)
    log_next = lbuf[pl.ds(2 * BLOCK, BLOCK), :]
    tail2 = jnp.exp(log_next[BLOCK - 1 :] - log_next)
    expanded = expand(jnp.concatenate([log_next, ending(lower, tail2)], axis=0))
    lx[pl.ds(LANES, BLOCK), :] = expanded[:BLOCK]
    blast_x[pl.ds(3 * BLOCK, BLOCK), :] = expanded[BLOCK:]

    def next_step(pairs):
        ats = [lanes_of(pair) for pair in pairs]
        carried = [
            weighted(wk[pl.ds(BLOCK, BLOCK), at], blast_x[pl.ds(3 * BLOCK, BLOCK), at]) for at in ats
        ]
        entering = [
            compact(tn(a, v_ref[pl.ds(BLOCK, BLOCK), at])) for a, at in zip(carried, ats)
        ]
        for r, at in zip(entering, ats):
            fall2 = jnp.exp(lx[3 * BLOCK - 1 : 3 * BLOCK, at])
            r_out[:, at] = r.astype(BF16)
            t_out[:, at] = (fall2 * c1c[:, at] + r).astype(BF16)

    all_pairs(next_step)
    send(T2_DN, T3_DN, R_DN)

    told(0)
    told(1)
    tell(2, 1)
    tell(3, z_size - 1)
    each_pair(together(window_step), 0, PAIRS // GROUP)
    told(2)
    told(3)
    tell(4, 1)
    own0 = jnp.exp(lx[BLOCK - 1 : BLOCK, :])
    own1 = jnp.exp(lx[LANES - 1 : LANES, :])

    @pl.when(place == 0)
    def _():
        messages[SS_UP][0].wait_recv()
        messages[SS_ON][0].start()

    @pl.when(place == last)
    def _():
        messages[SS_ROUND][0].wait_recv()
        messages[SS_BACK][0].start()

    @pl.when(place == 1)
    def _():
        messages[P_DN][0].wait_recv()
        messages[R_DN][0].wait_recv()
        entered = own0 * p_in[...].astype(F32) + r_in[...].astype(F32)
        p_out[...] = (c1c[...] + own1 * entered).astype(BF16)
        messages[P_DN][0].start()

    block_rows(lbuf[pl.ds(BLOCK, LANES), :], 2, BLOCK)

    received(Q_UP, G_UP)

    def cross_step(pairs):
        ats = [lanes_of(pair) for pair in pairs]
        queries = [phi(qn[:, at], coef_ref[:, at]).astype(BF16) for at in ats]
        grads = [gn[:, at] for at in ats]
        logs = [lx[pl.ds(LANES, BLOCK), at] for at in ats]
        decays = [
            jnp.exp(jnp.where(causal[:BLOCK], a - lrow[2:3, at], NEVER)) for at, a in zip(ats, logs)
        ]
        d_queries, d_values, d_keys, d_kernels = tiles(
            [diagonal(wk[pl.ds(BLOCK, BLOCK), at]) for at in ats],
            [keys_held[pair] for pair in pairs], [values_held[pair] for pair in pairs],
            queries, grads, [nn(a.astype(BF16), prev_mask) for a in decays],
        )
        entering = [
            compact(tn(a, weighted(b, jnp.exp(c)))) for a, b, c in zip(queries, grads, logs)
        ]
        d_decays = [nt(a, prev_mask) for a in d_kernels]
        for index, at in enumerate(ats):
            dqn_out[:, at] = d_queries[index].astype(BF16)
            raw = qn[:, at].astype(F32)
            coef_sum[1:2, at] = jnp.sum(
                d_queries[index] * (0.125 * raw * raw), axis=0, keepdims=True
            )
            dvf[pl.ds(BLOCK, BLOCK), at] = dvf[pl.ds(BLOCK, BLOCK), at] + d_values[index]
            dwk[pl.ds(BLOCK, BLOCK), at] = dwk[pl.ds(BLOCK, BLOCK), at] + d_keys[index]
            gmat[pl.ds(LANES, BLOCK), at] = (d_decays[index] * decays[index]).astype(BF16)
            c1c[:, at] = entering[index]

    each_pair(together(cross_step), 0, PAIRS // GROUP)
    send(DQ_DN)

    upper_both = flag(same & (col >= row))
    later_sums = jnp.concatenate(
        [
            nn(upper_both, gmat[pl.ds(0, LANES), :]),
            nn(upper_in, gmat[pl.ds(LANES, BLOCK), :]),
        ],
        axis=0,
    )
    before = (iota((3 * BLOCK, WIDTH), 1) % BLOCK) < (iota((3 * BLOCK, WIDTH), 0) % BLOCK)
    window_grads = nt(jnp.where(before, later_sums, 0.0).astype(BF16), spread)

    received(TOT1, S_UP, TOT2, SS_ON, SS_BACK, TOT3)
    falls = expand(jnp.concatenate([tot_in[slot] for slot in range(3)], axis=0))
    falls = [falls[8 * slot : 8 * slot + 8] for slot in range(3)]
    next1_fall1 = jnp.exp(falls[0][1:2])
    next2_all = jnp.exp(falls[1][0:1] + falls[1][1:2])
    prev1_fall1 = jnp.exp(falls[2][1:2])
    prev1_all = jnp.exp(falls[2][0:1] + falls[2][1:2])
    prev2_fall1 = jnp.exp(falls[1][1:2])
    next0 = jnp.exp(lx[3 * BLOCK - 1 :, :])
    z_grad = s1_in[...].astype(F32) + next1_fall1 * (
        ss_in[0].astype(F32) + next2_all * ss_in[1].astype(F32)
    )
    z_end[...] = z_grad.astype(BF16)
    end_grad = next0 * z_grad + c1c[...]
    mid_grad = own1 * end_grad + s1c[...]
    n_end[...] = end_grad.astype(BF16)
    n_mid[...] = mid_grad.astype(BF16)

    def enter(index, keys, d_role, at):
        weights = blast_x[pl.ds(index * BLOCK, BLOCK), at]
        own_keys = keys.astype(F32)
        xmat[pl.ds(index * BLOCK, BLOCK), at] = (d_role * own_keys).astype(BF16)
        return (own_keys * weights).astype(BF16), d_role * weights

    def outer_step(pairs):
        ats = [lanes_of(pair) for pair in pairs]
        rows = pl.ds(BLOCK, BLOCK)
        grads = [diagonal(z_end[:, at]) for at in ats]
        d_roles = [nt(v_ref[rows, at], a) for at, a in zip(ats, grads)]
        entered = [enter(3, wk[rows, at], a, at) for at, a in zip(ats, d_roles)]
        d_values = [nn(a[0], b) for a, b in zip(entered, grads)]
        for at, a, b in zip(ats, entered, d_values):
            dwk[rows, at] = dwk[rows, at] + a[1]
            dvf[rows, at] = dvf[rows, at] + b

    all_pairs(outer_step)
    d_last = nt(xmat[pl.ds(3 * BLOCK, BLOCK), :], spread)
    dan_out[...] = window_grads[LANES:] + twice(lower, twice(after, d_last) * tail2)
    send(DA_DN)

    def inner_step(pairs):
        ats = [lanes_of(pair) for pair in pairs]
        keys = [wk[:, at] for at in ats]
        values = [v_ref[:, at] for at in ats]
        ends = [diagonal(n_end[:, at]) for at in ats]
        both = [
            jnp.concatenate([diagonal(n_mid[:, at]), a], axis=0) for at, a in zip(ats, ends)
        ]
        d_first = [nt(a[:BLOCK], b) for a, b in zip(values, both)]
        d_second = [nt(a[BLOCK:], b) for a, b in zip(values, ends)]
        enter0 = [enter(0, a[:BLOCK], b[:, :LANES], at) for a, b, at in zip(keys, d_first, ats)]
        enter1 = [enter(1, a[:BLOCK], b[:, LANES:], at) for a, b, at in zip(keys, d_first, ats)]
        enter2 = [enter(2, a[BLOCK:], b, at) for a, b, at in zip(keys, d_second, ats)]
        dv0 = [
            nn(jnp.concatenate([a[0], b[0]], axis=1), c) for a, b, c in zip(enter0, enter1, both)
        ]
        dv1 = [nn(a[0], b) for a, b in zip(enter2, ends)]
        for index, at in enumerate(ats):
            dv_ref[:, at] = (
                dvf[:, at] + jnp.concatenate([dv0[index], dv1[index]], axis=0)
            ).astype(BF16)
            d_keys = dwk[:, at] + jnp.concatenate(
                [enter0[index][1] + enter1[index][1], enter2[index][1]], axis=0
            )
            coef = coef_ref[:, at]
            raw = k_ref[:, at].astype(F32)
            d_feat = d_keys * gamma_x[:, at]
            square = 0.125 * raw * raw
            xmat[pl.ds(6 * BLOCK, LANES), at] = (
                d_keys * (0.125 * raw + coef * square)
            ).astype(BF16)
            dk_ref[:, at] = (d_feat * (0.125 + (0.25 * coef) * raw)).astype(BF16)
            coef_sum[0:1, at] = jnp.sum(d_feat * square, axis=0, keepdims=True)

    all_pairs(inner_step)
    stores[1].start()
    stores[2].start()
    d_enter = nt(xmat[pl.ds(0, 3 * BLOCK), :], spread)
    d_gamma = nt(xmat[pl.ds(6 * BLOCK, LANES), :], spread_gate)
    entered0 = twice(at_or_before, d_enter[:BLOCK])
    entered1 = nn(
        jnp.concatenate([at_or_before, at_or_before, after, after], axis=1),
        jnp.concatenate(pieces(d_enter[2 * BLOCK :], 2) + pieces(d_enter[BLOCK : 2 * BLOCK], 2), axis=0),
    )
    lower_both = flag(same & (col < row))
    d_decay = window_grads[:LANES] + twice(
        lower_both, jnp.concatenate([entered0 * tail0, entered1 * tail1], axis=0)
    )

    received(P_DN, R_DN, places=place != 1)
    received(T2_DN, T3_DN)
    memory = (
        p_in[...].astype(F32)
        + prev1_fall1 * t_in[0].astype(F32)
        + (prev2_fall1 * prev1_all) * t_in[1].astype(F32)
    )
    middle_memory = own0 * memory + r_in[...].astype(F32) + u0c[...]
    m_in[...] = memory.astype(BF16)
    m_mid[...] = middle_memory.astype(BF16)
    fall_grad = jnp.concatenate(
        [
            own0 * jnp.sum(memory * mid_grad, axis=0, keepdims=True),
            own1 * jnp.sum(middle_memory * end_grad, axis=0, keepdims=True),
            jnp.zeros((6, WIDTH), F32),
        ],
        axis=0,
    )
    fall_grad = sum(nt(part, spread) for part in pieces(fall_grad, 2))

    def query_step(pairs):
        ats = [lanes_of(pair) for pair in pairs]
        scaled = [gq[:, at] for at in ats]
        carried = [
            jnp.concatenate(
                [
                    nt(a[:BLOCK], diagonal(m_in[:, at])),
                    nt(a[BLOCK:], diagonal(m_mid[:, at])),
                ],
                axis=0,
            )
            for a, at in zip(scaled, ats)
        ]
        for a, at in zip(carried, ats):
            xmat[pl.ds(4 * BLOCK, LANES), at] = (
                a * qf[pl.ds(0, LANES), at].astype(F32)
            ).astype(BF16)
            raw = q_ref[:, at].astype(F32)
            d_feat = dqf[:, at] + a
            dqf[:, at] = d_feat
            coef_sum[0:1, at] = (
                coef_sum[0:1, at]
                + coef_sum[1:2, at]
                + jnp.sum(d_feat * (0.125 * raw * raw), axis=0, keepdims=True)
            )

    all_pairs(query_step)
    d_out = nt(xmat[pl.ds(4 * BLOCK, LANES), :], spread)
    d_decay = d_decay + twice(upper_both, d_out)
    received(DA_DN)
    d_decay = d_decay + jnp.concatenate(
        [
            dan_in[...] + fall_grad[0:1],
            jnp.broadcast_to(fall_grad[1:2], (BLOCK, LANES)),
        ],
        axis=0,
    )
    is_decay = iota((LANES, LANES), 1) < HEADS
    d_logits = jnp.where(is_decay, -rate * sig * d_decay, d_gamma * gamma * (1.0 - sig))
    rates = jnp.sum(jnp.where(is_decay, -soft * d_decay, 0.0), axis=0, keepdims=True)
    gate = nn(jnp.concatenate(pieces(d_logits.T[:32], 2), axis=0), x)
    gate = gate[:32] + gate[32:]

    def paired(rows):
        high = rows.astype(BF16).astype(F32)
        return jnp.concatenate([high, rows - high], axis=0).astype(BF16)

    no_rates = jnp.zeros((1, LANES), F32)
    for chunk in range(8):
        at = slice(chunk * LANES, (chunk + 1) * LANES)
        mine[chunk, 0:32, :] = gate[:32, at].astype(BF16)
        mine[chunk, 32:TALL, :] = paired(
            jnp.concatenate(
                [
                    coef_sum[0:1, at],
                    rates if chunk == 0 else no_rates,
                    jnp.zeros((6, LANES), F32),
                ],
                axis=0,
            )
        )

    def exchange(base, size, where, source, target, reach=1):
        made = [
            pltpu.make_async_remote_copy(
                src_ref=source(hop),
                dst_ref=target,
                send_sem=sum_send.at[base + hop],
                recv_sem=sum_recv.at[base + hop],
                device_id=where(hop),
                device_id_type=MESH,
            )
            for hop in sorted(range(1, size), key=lambda hop: -min(hop // reach, (size - hop) // reach))
        ]
        for one in made:
            one.start()
        return made

    def added(buffer, count):
        total = buffer[0].astype(F32)
        for index in range(1, count):
            total = total + buffer[index].astype(F32)
        return jnp.concatenate(
            [total[:32].astype(BF16), paired(total[32:40] + total[40:])], axis=0
        )

    made = exchange(0, 8, octet, lambda hop: mine.at[lax.rem(eight + hop, 8)], first.at[eight], 2)
    first[eight] = mine[eight]
    d_hi, d_lo = [part[:, :32] for part in pieces(d_logits, 2)]
    dx_ref[...] = nn(
        jnp.concatenate([d_hi, d_lo, d_hi, jnp.zeros((LANES, 32), BF16)], axis=1),
        jnp.concatenate([w_hi, w_hi, w_lo, no_rows], axis=0),
    ).astype(BF16)
    stores[3].start()
    received(DQ_DN)

    def last_step(pair, carry):
        at = lanes_of(pair)
        raw = q_ref[:, at].astype(F32)
        d_feat = dqf[:, at] + jnp.concatenate(
            [dqn_in[:, at].astype(F32), jnp.zeros((BLOCK, LANES), F32)], axis=0
        )
        dq_ref[:, at] = (d_feat * (0.125 + (0.25 * coef_ref[:, at]) * raw)).astype(BF16)
        return carry

    each_pair(last_step)
    stores[0].start()
    for one in made:
        one.wait_recv()
    second[y] = added(first, 8)
    more = exchange(8, y_size, along_y, lambda hop: second.at[y], second.at[y])
    for one in more:
        one.wait_recv()
    made += more
    third[z] = added(second, y_size)
    told(4)
    more = exchange(8 + y_size, z_size, along_z, lambda hop: third.at[z], third.at[z])
    for one in more:
        one.wait_recv()
    made += more
    done[...] = added(third, z_size)
    own = pltpu.make_async_copy(done, done_hbm.at[eight], store_sem.at[4])
    own.start()
    more = exchange(
        8 + y_size + z_size, 8, octet, lambda hop: done, done_hbm.at[eight], 2
    )
    for message in range(MESSAGES):
        sent(message)
    for store in stores:
        store.wait()
    own.wait()
    for one in made:
        one.wait_send()
    for one in more:
        one.wait()


def main_call(sizes, queries, keys, values, inputs, gate, coef, rate, cotangent):
    z_size, y_size = sizes
    rows = queries.shape[0]
    anywhere = pl.BlockSpec(memory_space=pltpu.HBM)
    block, full = (BLOCK, WIDTH), (LANES, WIDTH)
    out = jax.ShapeDtypeStruct((rows, WIDTH), BF16)
    tile = (TALL, LANES)
    scratch = [
        (full, BF16), (full, BF16), (full, BF16), (full, BF16), (full, BF16),
        (gate.shape, F32), (coef.shape, F32), (rate.shape, F32),
        (full, BF16), (full, BF16), (full, BF16), (full, BF16),
        (block, BF16), (block, BF16), ((3 * BLOCK, LANES), F32), ((8, LANES), F32), ((3, 8, LANES), F32),
        (block, BF16), (block, BF16), (block, BF16), (block, BF16), ((2,) + block, BF16),
        (block, BF16), (block, BF16), (block, BF16), (block, BF16), (block, BF16), ((2,) + block, BF16),
        (block, BF16), (block, BF16), ((BLOCK, LANES), F32), ((BLOCK, LANES), F32),
        ((8, WIDTH), F32), ((3 * BLOCK, WIDTH), F32), (full, F32), ((4 * BLOCK, WIDTH), F32),
        (full, BF16), (full, BF16), (full, BF16),
        (block, F32), (block, F32), (block, F32),
        (block, BF16), (block, BF16), (block, BF16), (block, BF16), (block, BF16),
        (full, F32), (full, F32), (full, F32),
        ((3 * BLOCK, WIDTH), BF16), ((8 * BLOCK, WIDTH), BF16), ((8, WIDTH), F32),
        ((PAIRS, LANES, LANES), BF16), ((PAIRS, LANES, LANES), BF16),
        ((8,) + tile, BF16), ((8,) + tile, BF16), ((y_size,) + tile, BF16), ((z_size,) + tile, BF16),
        (tile, BF16),
    ]
    count = 16 + y_size + z_size
    return pl.pallas_call(
        functools.partial(main_kernel, z_size, y_size),
        out_shape=[out, out, out, out, jax.ShapeDtypeStruct((8,) + tile, BF16)],
        in_specs=[anywhere] * 8,
        out_specs=[anywhere] * 5,
        scratch_shapes=[pltpu.VMEM(shape, dtype) for shape, dtype in scratch]
        + [
            pltpu.SemaphoreType.DMA((number,))
            for number in (LOADS, STORES, MESSAGES, MESSAGES, count, count)
        ]
        + [pltpu.SemaphoreType.REGULAR((5,))],
        compiler_params=pltpu.CompilerParams(
            collective_id=0, has_side_effects=True, vmem_limit_bytes=56 * 2**20
        ),
        name="window_backward",
    )(queries, keys, values, inputs, gate, coef, rate, cotangent)


def hand_out_kernel(*refs):
    sources, targets, held = refs[:5], refs[5:12], refs[12:20]
    load_sem, store_sem = refs[20:]
    loads = [
        pltpu.make_async_copy(sources[index], held[index], load_sem.at[index]) for index in range(5)
    ]
    stores = [
        pltpu.make_async_copy(held[index if index < 4 else index + 1], targets[index], store_sem.at[index])
        for index in range(7)
    ]
    for load in loads[::-1]:
        load.start()
    done, gate, coef, rate = held[4:]
    loads[4].wait()
    for chunk in range(8):
        at = slice(chunk * LANES, (chunk + 1) * LANES)
        total = done[chunk].astype(F32)
        gate[:, at] = total[:32]
        rest = total[32:40] + total[40:]
        coef[:, at] = rest[0:1]
        if chunk == 0:
            rate[...] = rest[1:2, :HEADS]
    for store in stores[4:]:
        store.start()
    for index in range(3, -1, -1):
        loads[index].wait()
        stores[index].start()
    for store in stores:
        store.wait()


def hand_out(results):
    anywhere = pl.BlockSpec(memory_space=pltpu.HBM)
    params = [jax.ShapeDtypeStruct(shape, F32) for shape in ((32, WIDTH), (1, WIDTH), (1, HEADS))]
    shapes = [jax.ShapeDtypeStruct(a.shape, a.dtype) for a in results]
    return pl.pallas_call(
        hand_out_kernel,
        out_shape=shapes[:4] + params,
        in_specs=[anywhere] * 5,
        out_specs=[anywhere] * 7,
        scratch_shapes=[pltpu.VMEM(a.shape, a.dtype) for a in shapes + params]
        + [pltpu.SemaphoreType.DMA((5,)), pltpu.SemaphoreType.DMA((7,))],
        compiler_params=pltpu.CompilerParams(vmem_limit_bytes=56 * 2**20),
        name="hand_out",
    )(*results)


def on_device(sizes, queries, keys, values, inputs, gate, coef, rate, cotangent):
    results = main_call(
        sizes,
        queries[0], keys[0], values[0], inputs[0], gate.T, coef[None], rate[None], cotangent[0],
    )
    dq, dk, dv, dx, d_gate, d_coef, d_rate = hand_out(results)
    return (dq[None], dk[None], dv[None], dx[None], d_gate.T, d_coef[0], d_rate[0])


def solution(mesh):
    rows = P("dp", "seq", None)
    y_size = min(4, max(1, mesh.shape["dp"] // 2))
    sizes = (mesh.shape["dp"] // (2 * y_size), y_size)
    return jax.shard_map(
        functools.partial(on_device, sizes),
        mesh=mesh,
        in_specs=(rows, rows, rows, rows, P(), P(), P(), rows),
        out_specs=(rows, rows, rows, rows, P(), P(), P()),
        check_vma=False,
    )
```
